256 devices in a mesh: lat: 4 (over z_hi), lon: 64 (over x, z_lo, y, core).
Axes of the slice: x: 4, y: 4, z: 8 (z_hi: 4, z_lo: 2; z = z_hi * 2 + z_lo), core: 2. Of those that a mesh axis runs over, the one named last changes fastest.
Arguments:
- ensemble: float32 [2, 32, 128, 16384], P(None, None, 'lat', 'lon'), may hold values from -6 to 6
- courant_x: float32 [128, 16384], P('lat', 'lon'), may hold values from -0.2 to 0.2
- courant_y: float32 [128, 16384], P('lat', 'lon'), may hold values from -0.2 to 0.2
- diffusion: float32 [2], replicated, may hold values from 0.03 to 0.12
- obs_cell: int32 [2, 1024], replicated, may hold values from 0 to 2097151, as said below
- obs_value: float32 [2, 1024], replicated, may hold values from -6 to 6
- obs_noise: float32 [2, 1024, 32], replicated, may hold values from -4 to 4
- obs_var: float32 [2, 1024], replicated, may hold values from 0.3 to 1.5
- loc_mask: int32 [4, 64, 2, 1024], P('lat', 'lon'), may hold values from 0 to 1, as said below
Outputs:
- analysis: float32 [2, 32, 128, 16384], P(None, None, 'lat', 'lon')
The draws below stay inside these ranges and needn't reach their ends.
Inputs may be any that keep to these rules, and one draw needn't show every extreme that they name: `obs_cell`: no tile of 32 x 256 cells holds more than 16 of one batch's observations; some tile holds exactly 16 in every batch. `loc_mask`: 1 exactly where the tile is at most one tile row and at most 2 tile columns (periodically) from the tile of the observation's cell, else 0.
All inputs are finite; a program needn't handle non-finite values.
Results may differ from the reference program's by a relative error of at most 0.0003.
Values sent between devices are 32-bit elements; how exact they have to be, the bound alone decides.
A program may use at most 64 MiB of HBM per device.

```python
import math
import jax
import jax.numpy as jnp
from jax import lax

F = 2
M = 32
RD = 32
CD = 256
NBATCH = 2
LOCR = 2
SLOTS = 16
TLAT = 4
TLON = 64
NOBS = 1024
NY = 128
NX = 16384


def layout(key):
    tiles = TLAT * TLON
    pattern = jnp.array([SLOTS, 2, 2, 2, 2, 3, 3, 2], dtype=jnp.int32)
    cell_parts = []
    for batch_index in range(NBATCH):
        batch_key = jax.random.fold_in(key, 7 + batch_index)
        key_count, key_order, key_row, key_col = jax.random.split(batch_key, 4)
        counts = jnp.tile(pattern, tiles // 8)[jax.random.permutation(key_count, tiles)]
        offsets = jnp.cumsum(counts) - counts
        slot_index = jnp.arange(SLOTS, dtype=jnp.int32)
        filled = slot_index[None, :] < counts[:, None]
        order_rank = jnp.minimum(offsets[:, None] + slot_index[None, :], NOBS - 1)
        shuffle = jax.random.permutation(key_order, NOBS).astype(jnp.int32)
        slot_ids = jnp.where(filled, shuffle[order_rank], -1)
        tile_ids = jnp.arange(tiles, dtype=jnp.int32)
        cell_row = jax.random.randint(key_row, (tiles, SLOTS), 0, RD, dtype=jnp.int32) + (tile_ids // TLON)[:, None] * RD
        cell_col = jax.random.randint(key_col, (tiles, SLOTS), 0, CD, dtype=jnp.int32) + (tile_ids % TLON)[:, None] * CD
        flat_cell = cell_row * NX + cell_col
        target = jnp.where(filled, slot_ids, NOBS)
        placed = jnp.zeros((NOBS,), jnp.int32).at[target.reshape(-1)].set(flat_cell.reshape(-1), mode='drop')
        cell_parts.append(placed)
    return jnp.stack(cell_parts, axis=0)


def draw_obs_cell(key, part):
    return layout(key)


def draw_loc_mask(key, part):
    placed = layout(key)
    owner_lat = placed // NX // RD
    owner_lon = placed % NX // CD
    tile_lat = jnp.arange(TLAT, dtype=jnp.int32)[:, None, None, None]
    tile_lon = jnp.arange(TLON, dtype=jnp.int32)[None, :, None, None]
    apart = jnp.abs(tile_lon - owner_lon[None, None])
    apart = jnp.minimum(apart, TLON - apart)
    within = (jnp.abs(tile_lat - owner_lat[None, None]) <= 1) & (apart <= LOCR)
    return within.astype(jnp.int32)


def steps_of(key, extent, cuts, least, top_value):
    loudness, own = 1.0, jax.random.fold_in(key, 6)
    for axis_at, shards_of in cuts:
        steps = jnp.exp(jax.random.uniform(jax.random.fold_in(own, axis_at), (shards_of,), jnp.float32, least / len(cuts), top_value / len(cuts)))
        loudness = loudness * jnp.repeat(steps, extent[axis_at] // shards_of).reshape([-1 if axis == axis_at else 1 for axis in range(len(extent))])
    return loudness


def noise(own_key, dims, scale, most, cuts=(), held_as=jnp.bfloat16):
    level = steps_of(own_key, dims, cuts, -0.22, 0.18) if cuts else 1.0
    entries = jax.random.normal(own_key, dims, jnp.float32) * scale * level
    return jnp.minimum(jnp.maximum(entries, -most), most).astype(held_as)


def setup_inputs(seed: int = 0) -> dict:
    streams_of = jax.random.split(jax.random.key(seed), 10)
    ensemble = noise(streams_of[0], (F, M, NY, NX), 1.0, 6.0, ((2, 4), (3, 64)), jnp.float32)
    courant_x = jnp.clip(jax.random.uniform(streams_of[1], (NY, NX), jnp.float32, -0.2, 0.2) * steps_of(streams_of[1], (NY, NX), ((0, 4), (1, 64)), -0.4, 0.0), -0.2, 0.2)
    courant_y = jnp.clip(jax.random.uniform(streams_of[2], (NY, NX), jnp.float32, -0.2, 0.2) * steps_of(streams_of[2], (NY, NX), ((0, 4), (1, 64)), -0.4, 0.0), -0.2, 0.2)
    diffusion = jnp.clip(jax.random.uniform(streams_of[3], (F,), jnp.float32, 0.03, 0.12), 0.03, 0.12)
    obs_cell = draw_obs_cell(jax.random.fold_in(streams_of[9], 71), 0)
    obs_value = noise(streams_of[5], (NBATCH, NOBS), 1.0, 6.0, (), jnp.float32)
    obs_noise = noise(streams_of[6], (NBATCH, NOBS, M), 0.5, 4.0, (), jnp.float32)
    obs_var = jnp.clip(jnp.exp(jax.random.uniform(streams_of[7], (NBATCH, NOBS), jnp.float32, math.log(0.3), math.log(1.5))), 0.3, 1.5)
    loc_mask = draw_loc_mask(jax.random.fold_in(streams_of[9], 71), 0)
    return {"ensemble": ensemble, "courant_x": courant_x, "courant_y": courant_y, "diffusion": diffusion, "obs_cell": obs_cell, "obs_value": obs_value, "obs_noise": obs_noise, "obs_var": obs_var, "loc_mask": loc_mask}


def combine_terms(center, west_side, east_side, south_side, north_side, courant_x, courant_y, diff_rate):
    out = center - jnp.maximum(courant_x, 0.0) * (center - west_side) - jnp.minimum(courant_x, 0.0) * (east_side - center)
    out = out - jnp.maximum(courant_y, 0.0) * (center - south_side) - jnp.minimum(courant_y, 0.0) * (north_side - center)
    return out + diff_rate * (west_side + east_side + south_side + north_side - 4.0 * center)

def advance(ensemble, courant_x, courant_y, diffusion):
    zero_row = jnp.zeros_like(ensemble[:, :, :1])
    north_side = jnp.concatenate([ensemble[:, :, 1:], zero_row], axis=2)
    south_side = jnp.concatenate([zero_row, ensemble[:, :, :-1]], axis=2)
    east_side = jnp.roll(ensemble, -1, axis=3)
    west_side = jnp.roll(ensemble, 1, axis=3)
    return combine_terms(ensemble, west_side, east_side, south_side, north_side, courant_x, courant_y, diffusion[:, None, None, None])

def transform_of(spread, innovation, weight):
    members = spread.shape[1]
    weighted = spread * weight[:, None]
    system = (members - 1.0) * jnp.eye(members, dtype=jnp.float32) + jnp.dot(spread.T, weighted, precision=lax.Precision.HIGHEST)
    right_side = jnp.dot(weighted.T, innovation, precision=lax.Precision.HIGHEST)
    factor = jnp.linalg.cholesky(system)
    return jax.scipy.linalg.cho_solve((factor, True), right_side)

def reference(ensemble, courant_x, courant_y, diffusion, obs_cell, obs_value, obs_noise, obs_var, loc_mask):
    for substep in range(2):
        ensemble = advance(ensemble, courant_x, courant_y, diffusion)
    for batch_index in range(NBATCH):
        observed_field = batch_index % F
        priors = ensemble[observed_field].reshape(M, NY * NX)[:, obs_cell[batch_index]].T
        spread = priors - jnp.mean(priors, axis=1, keepdims=True)
        innovation = obs_value[batch_index][:, None] + obs_noise[batch_index] - priors

        def solve_tile(tile_number):
            mask_row = loc_mask[tile_number // TLON, tile_number % TLON, batch_index].astype(jnp.float32)
            return transform_of(spread, innovation, mask_row / obs_var[batch_index])
        transforms = lax.map(solve_tile, jnp.arange(TLAT * TLON, dtype=jnp.int32)).reshape(TLAT, TLON, M, M)
        anomaly = ensemble - jnp.mean(ensemble, axis=1, keepdims=True)
        blocks = anomaly.reshape(F, M, TLAT, RD, TLON, CD)
        update = jnp.einsum('fmaybx,abmk->fkaybx', blocks, transforms, precision=lax.Precision.HIGHEST)
        ensemble = ensemble + update.reshape(ensemble.shape)
    return ensemble
```

```python
import jax
import jax.numpy as jnp
from jax import lax
from jax.experimental import pallas as pl
from jax.experimental.pallas import tpu as pltpu
from jax.sharding import PartitionSpec as P

MESH = pl.DeviceIdType.MESH
HI = lax.Precision.HIGHEST
F, M, R, C = 2, 32, 32, 256
H = 128
SLOTS = 16
BATCHES = 2
REACH = tuple((di, dj) for di in (-1, 0, 1) for dj in range(-2, 3) if (di, dj) != (0, 0))
ROWS, COLS, CORNER, CROWS, CCOLS = 0, 4, 8, 12, 14
CHANNELS = 16


def iota(shape, axis):
    return lax.broadcasted_iota(jnp.int32, shape, axis)


def dot(a, b):
    return lax.dot_general(a, b, (((1,), (0,)), ((), ())), precision=HI, preferred_element_type=jnp.float32)


def eliminate(system):
    parts = [system[8 * g : 8 * g + 8] for g in range(4)]
    sub = iota((8, H), 0)
    for k in range(M):
        own, at = divmod(k, 8)
        columns = [jnp.broadcast_to(part[:, k : k + 1], (8, H)) for part in parts]
        pivot = jnp.broadcast_to(columns[own][at : at + 1, :], (8, H))
        row = jnp.broadcast_to(parts[own][at : at + 1, :], (8, H)) * (1.0 / pivot)
        new = [part - column * row for part, column in zip(parts, columns)]
        new[own] = jnp.where(sub == at, row, new[own])
        parts = new
    return jnp.concatenate(parts, axis=0)


def forecast_kernel(
    ens, cx_in, cy_in, diff_in, cell_in, value_in, noise_in, var_in,
    x_out, e_out,
    halves, q, x1, x2, own_w, own_e, far_w, far_e, next_w, next_e, corner_s, corner_r, crow_s, crow_r, ccol_s, ccol_r,
    coef, cx, cy, diff, cell, cell16, value, noise, var, id_v, id_s, vn, sw, msg, got,
    in_sem, out_sem, p1_send, p1_recv, p2_send, p2_recv,
):
    la, lo = lax.axis_size("lat"), lax.axis_size("lon")
    me_i, me_j = lax.axis_index("lat"), lax.axis_index("lon")

    def at(di, dj):
        return (lax.rem(me_i + (di + la), la), lax.rem(me_j + (dj + lo), lo))

    barrier = pltpu.get_barrier_semaphore()
    for di, dj in REACH:
        pl.semaphore_signal(barrier, inc=1, device_id=at(di, dj), device_id_type=MESH)

    def load(src, dst, sem):
        copy = pltpu.make_async_copy(src, dst, in_sem.at[sem])
        copy.start()
        return copy

    ens_copies = [
        [load(ens.at[f, :, pl.ds(h * H, H)], halves.at[h, f], 2 * f + h) for h in range(2)] for f in range(F)
    ]
    c_copies = [load(cx_in, cx, 4), load(cy_in, cy, 5), load(diff_in, diff, 6)]
    o_copies = [load(cell_in, cell, 7), load(value_in, value, 8), load(var_in, var, 9)]
    n_copy = load(noise_in, noise, 10)

    lane = iota((M, H), 1)
    lane8 = iota((8, H), 1)
    started = []

    def send(channel, src, dst, target):
        copy = pltpu.make_async_remote_copy(
            src_ref=src, dst_ref=dst, send_sem=p1_send.at[channel], recv_sem=p1_recv.at[channel],
            device_id=target, device_id_type=MESH,
        )
        copy.start()
        started.append(copy)
        return copy

    for copy in c_copies:
        copy.wait()
    cxv, cyv = cx[...], cy[...]
    for side, row in ((0, R - 1), (1, 0)):
        crow_s[side, 0:1, :] = cxv[row : row + 1, :]
        crow_s[side, 1:2, :] = cyv[row : row + 1, :]
    spot = (lax.shift_right_logical(lane, 1) == iota((R, H), 0)) & (lane < 2 * R)
    for side, col in ((0, C - 1), (1, 0)):
        for n, source in enumerate((cxv, cyv)):
            spread = jnp.where(spot, jnp.broadcast_to(source[:, col : col + 1], (R, H)), 0.0)
            ccol_s[side, n : n + 1, :] = jnp.sum(spread, axis=0, keepdims=True)

    def pack(f):
        for copy in ens_copies[f]:
            copy.wait()
        def body(r, carry):
            west, east = carry
            c0 = halves[0, f, pl.ds(r, M, stride=R), :]
            c1 = halves[1, f, pl.ds(r, M, stride=R), :]
            q[f, r + 2, :, 0:H] = c0
            q[f, r + 2, :, H:C] = c1
            here = lax.shift_right_logical(lane, 1) == r
            west = jnp.where(here, pltpu.roll(c0, 2 * r, 1), west)
            east = jnp.where(here, pltpu.roll(c1, lax.rem(2 * r + 2, H), 1), east)
            return west, east

        zero = jnp.zeros((M, H), jnp.float32)
        west, east = lax.fori_loop(0, R, body, (zero, zero), unroll=8)
        own_w[f] = west
        own_e[f] = east

    def send_field(f):
        return [
            send(ROWS + 2 * f, q.at[f, pl.ds(R, 2)], q.at[f, pl.ds(0, 2)], at(1, 0)),
            send(ROWS + 2 * f + 1, q.at[f, pl.ds(2, 2)], q.at[f, pl.ds(R + 2, 2)], at(-1, 0)),
            send(COLS + 2 * f, own_e.at[f], far_w.at[f], at(0, 1)),
            send(COLS + 2 * f + 1, own_w.at[f], far_e.at[f], at(0, -1)),
        ]

    pack(0)
    pl.semaphore_wait(barrier, len(REACH))
    field_copies = [send_field(0)]
    halo_copies = [
        send(CROWS, crow_s.at[0], crow_r.at[0], at(1, 0)),
        send(CROWS + 1, crow_s.at[1], crow_r.at[1], at(-1, 0)),
        send(CCOLS, ccol_s.at[0], ccol_r.at[0], at(0, 1)),
        send(CCOLS + 1, ccol_s.at[1], ccol_r.at[1], at(0, -1)),
    ]
    pack(1)
    fill = jnp.zeros((H - F * M, H), jnp.float32)
    turned_w = jnp.concatenate([own_w[0], own_w[1], fill], axis=0).T
    turned_e = jnp.concatenate([own_e[0], own_e[1], fill], axis=0).T
    corner_s[0] = turned_e[2 * R - 8 : 2 * R]
    corner_s[1] = turned_w[2 * R - 8 : 2 * R]
    corner_s[2] = turned_e[0:8]
    corner_s[3] = turned_w[0:8]
    for n, target in enumerate(((1, 1), (1, -1), (-1, 1), (-1, -1))):
        halo_copies.append(send(CORNER + n, corner_s.at[n], corner_r.at[n], at(*target)))
    field_copies.append(send_field(1))

    for copy in o_copies:
        copy.wait()
    count = cell.shape[1]
    chunks = count // H
    wide = lo * C
    shift = wide.bit_length() - 1
    n_rows = BATCHES * chunks
    for ch in range(chunks):
        cell16[BATCHES * ch : BATCHES * (ch + 1), :] = cell[:, ch * H : (ch + 1) * H]
    cells = cell16[...]
    l_row = lax.shift_right_logical(cells, shift) - me_i * R
    l_col = (cells & (wide - 1)) - me_j * C
    mine = (l_row >= 0) & (l_row < R) & (l_col >= 0) & (l_col < C)
    mask = jnp.where(mine, 1.0, 0.0)
    before = jnp.where(iota((H, H), 0) < iota((H, H), 1), 1.0, 0.0)
    ii, jj = iota((n_rows, n_rows), 0), iota((n_rows, n_rows), 1)
    rows_before = jnp.where((lax.rem(ii, BATCHES) == lax.rem(jj, BATCHES)) & (jj < ii), 1.0, 0.0)
    totals = jnp.broadcast_to(jnp.sum(mask, axis=1, keepdims=True), (n_rows, H))
    rank = dot(mask, before) + dot(rows_before, totals)
    rank = jnp.where(mine, rank, -1.0).astype(jnp.int32)
    order = lax.shift_right_logical(iota((n_rows, H), 0), 1) * H + iota((n_rows, H), 1)
    code = jnp.where(mine, (order * R + l_row) * C + l_col, 0).astype(jnp.float32)
    slot = iota((SLOTS, H), 0)
    slot_lane = iota((SLOTS, H), 1)
    columns = []
    for b in range(BATCHES):
        acc = [jnp.zeros((SLOTS, H), jnp.float32) for _ in range(3)]
        for ch in range(chunks):
            at_row = BATCHES * ch + b
            here = jnp.broadcast_to(rank[at_row : at_row + 1, :], (SLOTS, H)) == slot
            cut = slice(ch * H, (ch + 1) * H)
            for n, source in enumerate((code[at_row : at_row + 1, :], value[b : b + 1, cut], var[b : b + 1, cut])):
                acc[n] = jnp.where(here, jnp.broadcast_to(source, (SLOTS, H)), acc[n])
        sums = [jnp.broadcast_to(jnp.sum(a, axis=1, keepdims=True), (SLOTS, H)) for a in acc]
        id_v[b * SLOTS : (b + 1) * SLOTS, :] = sums[0].astype(jnp.int32)
        there = sums[2] > 0.0
        sw[b] = jnp.where(there, jnp.sqrt(1.0 / jnp.where(there, sums[2], 1.0)), 0.0)
        columns.append(sums[1])
    id_copy = load(id_v, id_s, 11)

    def parts_of(x, y):
        return jnp.maximum(x, 0.0), -jnp.minimum(x, 0.0), jnp.maximum(y, 0.0), -jnp.minimum(y, 0.0)

    rates = [diff[f] for f in range(F)]
    low_edge, high_edge = me_i == 0, me_i == la - 1

    def centre_of(p, k):
        return 1.0 - p[0] - p[1] - p[2] - p[3] - 4.0 * k

    own_parts = parts_of(cxv, cyv)
    row_id = iota((R, C), 0)

    def set_coef(f, first, values):
        for n in range(5):
            for h in range(2):
                v = values[n][:, h * H : (h + 1) * H]
                coef[f, n, h, first : first + max(8, v.shape[0]), :] = jnp.broadcast_to(v, (max(8, v.shape[0]), H))

    for f in range(F):
        south = jnp.where((row_id == 0) & low_edge, 0.0, own_parts[2] + rates[f])
        north = jnp.where((row_id == R - 1) & high_edge, 0.0, own_parts[3] + rates[f])
        set_coef(f, 8, [centre_of(own_parts, rates[f]), own_parts[0] + rates[f], own_parts[1] + rates[f], south, north])

    id_copy.wait()
    n_copy.wait()
    ids = [[id_s[b * SLOTS + s, 0] for s in range(SLOTS)] for b in range(BATCHES)]
    slot_m = iota((SLOTS, M), 0)
    move = jnp.where(iota((M, H), 1) == iota((M, H), 0) + M, 1.0, 0.0)
    middle = (slot_lane >= M) & (slot_lane < 2 * M)
    for b in range(BATCHES):
        rows = jnp.zeros((SLOTS, M), jnp.float32)
        for s in range(SLOTS):
            one = noise[b, pl.ds(lax.shift_right_logical(ids[b][s], 13) & (count - 1), 1), :]
            rows = jnp.where(slot_m == s, jnp.broadcast_to(one, (SLOTS, M)), rows)
        vn[b] = jnp.where(middle, columns[b] + dot(rows, move), 0.0)

    for copy in halo_copies:
        copy.wait_recv()
    halo_rows = [parts_of(crow_r[side, 0:1, :], crow_r[side, 1:2, :]) for side in range(2)]
    for f in range(F):
        for side, first in ((0, 0), (1, 8 + R)):
            p = halo_rows[side]
            values = [centre_of(p, rates[f])] + [part + rates[f] for part in p]
            set_coef(f, first, values)
    corners = jnp.concatenate([corner_r[n] for n in range(4)] + [jnp.zeros((H - 32, H), jnp.float32)], axis=0).T

    def halo_columns(f):
        for copy in field_copies[f][2:]:
            copy.wait_recv()
        corner = [
            jnp.broadcast_to(corners[f * M : (f + 1) * M, n : n + 1], (M, H)) for n in (7, 14, 17, 24)
        ]
        west = far_w[f]
        west = jnp.where(lane == H - 1, corner[0], jnp.where(lane == 2 * R + 1, corner[2], west))
        east = far_e[f]
        east = jnp.where(lane == H - 2, corner[1], jnp.where(lane == 2 * R, corner[3], east))
        far_w[f] = west
        far_e[f] = east
        lane_row = iota((1, H), 1)
        for side in range(2):
            p = parts_of(ccol_r[side, 0:1, :], ccol_r[side, 1:2, :])
            south = jnp.where((lane_row < 2) & low_edge, 0.0, p[2] + rates[f])
            north = jnp.where((lane_row >= 2 * R - 2) & high_edge, 0.0, p[3] + rates[f])
            rate = (centre_of(p, rates[f]), p[0] + rates[f], p[1] + rates[f], south, north)
            if side == 0:
                c, w, e = west, pltpu.roll(west, 1, 1), pltpu.roll(own_w[f], 1, 1)
            else:
                c, w, e = east, pltpu.roll(own_e[f], H - 1, 1), pltpu.roll(east, H - 1, 1)
            out = rate[0] * c + rate[1] * w + rate[2] * e
            out = out + rate[3] * pltpu.roll(c, 2, 1) + rate[4] * pltpu.roll(c, H - 2, 1)
            out = jnp.where(lane < 2 * R, out, 0.0)
            if side == 0:
                next_w[f] = out
            else:
                next_e[f] = out

    def row_step(src, dst, f, r, src_at, dst_at, far_west, far_east):
        turn = (H - 1 - 2 * r) & (H - 1)
        hw, he = pltpu.roll(far_west, turn, 1), pltpu.roll(far_east, turn, 1)
        c0, c1 = src[f, r + src_at, :, 0:H], src[f, r + src_at, :, H:C]
        w0, w1 = pltpu.roll(c0, 1, 1), pltpu.roll(c1, 1, 1)
        e0, e1 = pltpu.roll(c0, H - 1, 1), pltpu.roll(c1, H - 1, 1)
        first, last = lane == 0, lane == H - 1
        w0, w1 = jnp.where(first, hw, w0), jnp.where(first, w0, w1)
        e0, e1 = jnp.where(last, e1, e0), jnp.where(last, he, e1)
        for h, (c, w, e) in enumerate(((c0, w0, e0), (c1, w1, e1))):
            cut = slice(h * H, (h + 1) * H)
            rate = [coef[f, n, h, pl.ds(r + 8, 1), :] for n in range(5)]
            out = rate[0] * c + rate[1] * w + rate[2] * e
            out = out + rate[3] * src[f, r + src_at - 1, :, cut] + rate[4] * src[f, r + src_at + 1, :, cut]
            dst[f, r + dst_at, :, cut] = out

    def step_one(f, r):
        row_step(q, x1, f, r, 2, 1, far_w[f], far_e[f])

    def step_two(f, r):
        row_step(x1, x2, f, r, 1, 0, next_w[f], next_e[f])

    def rows_of(step, f, begin, end):
        def body(r, carry):
            step(f, r)
            return carry

        lax.fori_loop(begin, end, body, 0, unroll=2)

    def forecast(f):
        halo_columns(f)
        rows_of(step_one, f, 1, R - 1)
        rows_of(step_two, f, 2, R - 2)
        for copy in field_copies[f][:2]:
            copy.wait_recv()
        for r in (-1, 0, R - 1, R):
            step_one(f, r)
        for r in (0, 1, R - 2, R - 1):
            step_two(f, r)
        copy = pltpu.make_async_copy(x2.at[f], x_out.at[f], out_sem.at[f])
        copy.start()
        return copy

    def observe(b):
        f = b % F
        seen = jnp.zeros((M, H), jnp.float32)
        for s in range(SLOTS):
            code_s = ids[b][s]
            row = x2[f, lax.shift_right_logical(code_s, 8) & (R - 1)]
            col = code_s & (C - 1)
            picked = jnp.where(lane == col, row[:, 0:H], 0.0) + jnp.where(lane + H == col, row[:, H:C], 0.0)
            seen = jnp.where(lane == s, jnp.broadcast_to(jnp.sum(picked, axis=1, keepdims=True), (M, H)), seen)
        mean = jnp.sum(seen, axis=0, keepdims=True) * (1.0 / M)
        stacked = jnp.concatenate([seen - mean, seen, jnp.zeros((H - 2 * M, H), jnp.float32)], axis=0)
        return stacked.T[0:SLOTS]

    def tell(b, z):
        signed = jnp.where(slot_lane < M, z, -z)
        r = sw[b] * (vn[b] + signed)
        r = jnp.where(slot_lane < 2 * M, r, 0.0)
        packed = r[0:8] + pltpu.roll(r[8:16], 2 * M, 1)
        msg[b] = packed
        got[b, 14] = packed
        got[b, 15] = jnp.zeros((8, H), jnp.float32)
        copies = []
        for n, (di, dj) in enumerate(REACH):
            copy = pltpu.make_async_remote_copy(
                src_ref=msg.at[b], dst_ref=got.at[b, n], send_sem=p2_send.at[b, n], recv_sem=p2_recv.at[b, n],
                device_id=at(-di, -dj), device_id_type=MESH,
            )
            copy.start()
            copies.append(copy)
        started.extend(copies)
        return copies

    lower = iota((8, H), 0)

    def transform(b, copies):
        for copy in copies:
            copy.wait_recv()
        stack = got[b].reshape(16 * 8, H)
        place = iota((16 * 8, H), 0)
        keep = jnp.where(low_edge & (place < 5 * 8), 0.0, 1.0)
        keep = jnp.where(high_edge & (place >= 9 * 8) & (place < 14 * 8), 0.0, keep)
        stack = stack * keep
        turned = stack.T
        gram = dot(jnp.concatenate([turned[0:M], turned[2 * M : 3 * M]], axis=0), stack)
        both = gram[0:M] + pltpu.roll(gram[M : 2 * M], 2 * M, 1)
        system = jnp.where(lane < 2 * M, both, 0.0) + jnp.where(lane == iota((M, H), 0), M - 1.0, 0.0)
        return eliminate(system)

    def centered_rows(solved):
        w = jnp.where(lane < M, pltpu.roll(solved, H - M, 1), 0.0)
        return w - jnp.sum(w, axis=0, keepdims=True) * (1.0 / M)

    outs = [forecast(0)]
    z0 = observe(0)
    copies0 = tell(0, z0)
    outs.append(forecast(1))
    z1 = observe(1)
    solved0 = transform(0, copies0)
    w0 = jnp.where(lane < M, pltpu.roll(solved0, H - M, 1), 0.0)
    w0_mean = jnp.sum(w0, axis=1, keepdims=True) * (1.0 / M)
    both0 = jnp.where(lane < M, w0 - w0_mean, jnp.where(lane < 2 * M, solved0, 0.0))
    z1 = z1 + dot(z1[:, 0:M], both0)
    copies1 = tell(1, z1)
    c0 = centered_rows(solved0)
    solved1 = transform(1, copies1)
    c1 = centered_rows(solved1)
    e_out[...] = c0 + c1 + dot(c0[:, 0:M], c1)

    for copy in started:
        copy.wait_send()
    for copy in outs:
        copy.wait()


def analysis_kernel(e_ref, x_in, out, x, y, in_sem, out_sem):
    groups = [(f, r) for f in range(F) for r in range(0, R, 8)]
    loads = []
    for n, (f, r) in enumerate(groups):
        copy = pltpu.make_async_copy(x_in.at[f, pl.ds(r, 8)], x.at[f, pl.ds(r, 8)], in_sem.at[n])
        copy.start()
        loads.append(copy)
    e = jnp.concatenate([e_ref[...], jnp.zeros((H - M, H), jnp.float32)], axis=0).T[0:M, 0:M]
    e_hi = e.astype(jnp.bfloat16)
    e_lo = (e - e_hi.astype(jnp.float32)).astype(jnp.bfloat16)
    left = jnp.concatenate([e_hi, e_hi, e_lo], axis=1)
    stores = []
    for n, (f, r) in enumerate(groups):
        loads[n].wait()
        for row in range(r, r + 8):
            v = x[f, row]
            hi = v.astype(jnp.bfloat16)
            low = (v - hi.astype(jnp.float32)).astype(jnp.bfloat16)
            right = jnp.concatenate([hi, low, hi], axis=0)
            add = lax.dot_general(left, right, (((1,), (0,)), ((), ())), preferred_element_type=jnp.float32)
            y[f, row] = v + add
        for row in range(r, r + 8):
            copy = pltpu.make_async_copy(y.at[f, row], out.at[f, :, row, :], out_sem.at[f, row])
            copy.start()
            stores.append(copy)
    for copy in stores:
        copy.wait()


def local(ensemble, courant_x, courant_y, diffusion, obs_cell, obs_value, obs_noise, obs_var, loc_mask):
    any_space = pl.BlockSpec(memory_space=pl.ANY)
    f32 = jnp.float32
    count = obs_cell.shape[1]
    vmem = pltpu.VMEM
    dma = pltpu.SemaphoreType.DMA
    forecast, combined = pl.pallas_call(
        forecast_kernel,
        out_shape=(jax.ShapeDtypeStruct((F, R, M, C), f32), jax.ShapeDtypeStruct((M, H), f32)),
        in_specs=[any_space] * 8,
        out_specs=(any_space, pl.BlockSpec(memory_space=pltpu.VMEM)),
        scratch_shapes=[
            vmem((2, F, M * R, H), f32),
            vmem((F, R + 4, M, C), f32),
            vmem((F, R + 2, M, C), f32),
            vmem((F, R, M, C), f32),
            vmem((F, M, H), f32),
            vmem((F, M, H), f32),
            vmem((F, M, H), f32),
            vmem((F, M, H), f32),
            vmem((F, M, H), f32),
            vmem((F, M, H), f32),
            vmem((4, 8, H), f32),
            vmem((4, 8, H), f32),
            vmem((2, 8, C), f32),
            vmem((2, 8, C), f32),
            vmem((2, 8, H), f32),
            vmem((2, 8, H), f32),
            vmem((F, 5, 2, R + 16, H), f32),
            vmem((R, C), f32),
            vmem((R, C), f32),
            pltpu.SMEM((F,), f32),
            vmem((BATCHES, count), jnp.int32),
            vmem((BATCHES * count // H, H), jnp.int32),
            vmem((BATCHES, count), f32),
            vmem((BATCHES, count, M), f32),
            vmem((BATCHES, count), f32),
            vmem((BATCHES * SLOTS, H), jnp.int32),
            pltpu.SMEM((BATCHES * SLOTS, H), jnp.int32),
            vmem((BATCHES, SLOTS, H), f32),
            vmem((BATCHES, SLOTS, H), f32),
            vmem((BATCHES, 8, H), f32),
            vmem((BATCHES, 16, 8, H), f32),
            dma((12,)),
            dma((F,)),
            dma((CHANNELS,)),
            dma((CHANNELS,)),
            dma((BATCHES, len(REACH))),
            dma((BATCHES, len(REACH))),
        ],
        compiler_params=pltpu.CompilerParams(
            collective_id=0, has_side_effects=True, vmem_limit_bytes=40 * 1024 * 1024
        ),
        name="forecast_and_transform",
    )(ensemble.reshape(F, M * R, C), courant_x, courant_y, diffusion, obs_cell, obs_value, obs_noise, obs_var)
    return pl.pallas_call(
        analysis_kernel,
        out_shape=jax.ShapeDtypeStruct((F, M, R, C), f32),
        in_specs=[pl.BlockSpec(memory_space=pltpu.VMEM), any_space],
        out_specs=any_space,
        scratch_shapes=[
            vmem((F, R, M, C), f32),
            vmem((F, R, M, C), f32),
            dma((F * R // 8,)),
            dma((F, R)),
        ],
        compiler_params=pltpu.CompilerParams(vmem_limit_bytes=40 * 1024 * 1024),
        name="analysis",
    )(combined, forecast)


def solution(mesh):
    in_specs = (
        P(None, None, "lat", "lon"),
        P("lat", "lon"),
        P("lat", "lon"),
        P(),
        P(),
        P(),
        P(),
        P(),
        P("lat", "lon", None, None),
    )
    out_specs = P(None, None, "lat", "lon")
    return jax.shard_map(local, mesh=mesh, in_specs=in_specs, out_specs=out_specs, check_vma=False)
```

```python
import jax
import jax.numpy as jnp
from jax import lax
from jax.experimental import pallas as pl
from jax.experimental.pallas import tpu as pltpu
from jax.sharding import PartitionSpec as P

MESH = pl.DeviceIdType.MESH
HI = lax.Precision.HIGHEST
F, M, R, C = 2, 32, 32, 256
H = 128
SLOTS = 16
BATCHES = 2
REACH = tuple((di, dj) for di in (-1, 0, 1) for dj in range(-2, 3) if (di, dj) != (0, 0))
ROWS, COLS, CORNER, CROWS, CCOLS = 0, 4, 8, 12, 14
CHANNELS = 16


def iota(shape, axis):
    return lax.broadcasted_iota(jnp.int32, shape, axis)


def dot(a, b):
    return lax.dot_general(a, b, (((1,), (0,)), ((), ())), precision=HI, preferred_element_type=jnp.float32)


def eliminate(system):
    parts = [system[8 * g : 8 * g + 8] for g in range(4)]
    sub = iota((8, H), 0)
    for own in range(4):
        lanes = range(8 * own, 8 * own + 8)
        columns = [[jnp.broadcast_to(part[:, k : k + 1], (8, H)) for part in parts] for k in lanes]
        pivots = [[jnp.broadcast_to(columns[j][own][i : i + 1], (8, H)) for j in range(8)] for i in range(8)]
        rows = [jnp.broadcast_to(parts[own][i : i + 1], (8, H)) for i in range(8)]
        for p in range(8):
            inverse = 1.0 / pivots[p][p]
            rows[p] = rows[p] * inverse
            for j in range(p + 1, 8):
                pivots[p][j] = pivots[p][j] * inverse
            for i in range(8):
                if i != p:
                    factor = pivots[i][p]
                    rows[i] = rows[i] - factor * rows[p]
                    for j in range(p + 1, 8):
                        pivots[i][j] = pivots[i][j] - factor * pivots[p][j]
        new = []
        for g in range(4):
            terms = [columns[j][g] * rows[j] for j in range(8)]
            while len(terms) > 1:
                terms = [terms[n] + terms[n + 1] for n in range(0, len(terms), 2)]
            new.append(parts[g] - terms[0])
        for i in range(8):
            new[own] = jnp.where(sub == i, rows[i], new[own])
        parts = new
    return jnp.concatenate(parts, axis=0)


def forecast_kernel(
    ens, cx_in, cy_in, diff_in, cell_in, value_in, noise_in, var_in,
    x_out, e_out,
    halves, q, x1, x2, own_w, own_e, far_w, far_e, next_w, next_e, corner_s, corner_r, crow_s, crow_r, ccol_s, ccol_r,
    fix_w, fix_e, coef, cx, cy, diff, cell, cell16, value, noise, var, picks, id_v, id_s, msg, got,
    in_sem, out_sem, p1_send, p1_recv, p2_send, p2_recv,
):
    la, lo = lax.axis_size("lat"), lax.axis_size("lon")
    me_i, me_j = lax.axis_index("lat"), lax.axis_index("lon")

    def at(di, dj):
        return (lax.rem(me_i + (di + la), la), lax.rem(me_j + (dj + lo), lo))

    barrier = pltpu.get_barrier_semaphore()
    for di, dj in REACH:
        pl.semaphore_signal(barrier, inc=1, device_id=at(di, dj), device_id_type=MESH)

    def load(src, dst, sem):
        copy = pltpu.make_async_copy(src, dst, in_sem.at[sem])
        copy.start()
        return copy

    ens_copies = [
        [load(ens.at[f, :, pl.ds(h * H, H)], halves.at[h, f], 2 * f + h) for h in range(2)] for f in range(F)
    ]
    c_copies = [load(cx_in, cx, 4), load(cy_in, cy, 5), load(diff_in, diff, 6)]
    o_copies = [load(cell_in, cell, 7), load(value_in, value, 8), load(var_in, var, 9)]
    n_copy = load(noise_in, noise, 10)

    lane = iota((M, H), 1)
    lane8 = iota((8, H), 1)
    started = []

    def send(channel, src, dst, target):
        copy = pltpu.make_async_remote_copy(
            src_ref=src, dst_ref=dst, send_sem=p1_send.at[channel], recv_sem=p1_recv.at[channel],
            device_id=target, device_id_type=MESH,
        )
        copy.start()
        started.append(copy)
        return copy

    for copy in c_copies:
        copy.wait()
    cxv, cyv = cx[...], cy[...]
    for side, row in ((0, R - 1), (1, 0)):
        crow_s[side, 0:1, :] = cxv[row : row + 1, :]
        crow_s[side, 1:2, :] = cyv[row : row + 1, :]
    spot = (lax.shift_right_logical(lane, 1) == iota((R, H), 0)) & (lane < 2 * R)
    even = (lane & 1) == 0
    for side, col in ((0, C - 2), (1, 0)):
        for n, source in enumerate((cxv, cyv)):
            pair = [jnp.broadcast_to(source[:, col + c : col + c + 1], (R, H)) for c in range(2)]
            spread = jnp.where(spot, jnp.where(even, pair[0], pair[1]), 0.0)
            ccol_s[side, n : n + 1, :] = jnp.sum(spread, axis=0, keepdims=True)

    for f in range(F):
        for copy in ens_copies[f]:
            copy.wait()

    def corner_lanes(f):
        cells = [
            halves[0, f, pl.ds(0, M, stride=R), :],
            pltpu.roll(halves[1, f, pl.ds(0, M, stride=R), :], 2, 1),
            pltpu.roll(halves[0, f, pl.ds(R - 1, M, stride=R), :], 2, 1),
            pltpu.roll(halves[1, f, pl.ds(R - 1, M, stride=R), :], 4, 1),
        ]
        out = jnp.where(lane == 3, cells[3], 0.0)
        for n in range(3):
            out = jnp.where(lane == n, cells[n], out)
        return out

    fill = jnp.zeros((H - F * M, H), jnp.float32)
    corner_s[...] = jnp.concatenate([corner_lanes(0), corner_lanes(1), fill], axis=0).T[0:8]

    def pack(f):
        def body(r, carry):
            west, east = carry
            c0 = halves[0, f, pl.ds(r, M, stride=R), :]
            c1 = halves[1, f, pl.ds(r, M, stride=R), :]
            q[f, r + 2, :, 0:H] = c0
            q[f, r + 2, :, H:C] = c1
            here = lax.shift_right_logical(lane, 1) == r
            west = jnp.where(here, pltpu.roll(c0, 2 * r, 1), west)
            east = jnp.where(here, pltpu.roll(c1, lax.rem(2 * r + 2, H), 1), east)
            return west, east

        zero = jnp.zeros((M, H), jnp.float32)
        west, east = lax.fori_loop(0, R, body, (zero, zero), unroll=8)
        own_w[f] = west
        own_e[f] = east

    def send_field(f):
        return [
            send(ROWS + 2 * f, q.at[f, pl.ds(R, 2)], q.at[f, pl.ds(0, 2)], at(1, 0)),
            send(ROWS + 2 * f + 1, q.at[f, pl.ds(2, 2)], q.at[f, pl.ds(R + 2, 2)], at(-1, 0)),
            send(COLS + 2 * f, own_e.at[f], far_w.at[f], at(0, 1)),
            send(COLS + 2 * f + 1, own_w.at[f], far_e.at[f], at(0, -1)),
        ]

    pl.semaphore_wait(barrier, len(REACH))
    halo_copies = []
    for n, target in enumerate(((1, 1), (1, -1), (-1, 1), (-1, -1))):
        halo_copies.append(send(CORNER + n, corner_s, corner_r.at[n], at(*target)))
    halo_copies += [
        send(CROWS, crow_s.at[0], crow_r.at[0], at(1, 0)),
        send(CROWS + 1, crow_s.at[1], crow_r.at[1], at(-1, 0)),
        send(CCOLS, ccol_s.at[0], ccol_r.at[0], at(0, 1)),
        send(CCOLS + 1, ccol_s.at[1], ccol_r.at[1], at(0, -1)),
    ]
    pack(0)
    field_copies = [send_field(0)]
    pack(1)
    field_copies.append(send_field(1))

    for copy in o_copies:
        copy.wait()
    count = cell.shape[1]
    chunks = count // H
    wide = lo * C
    shift = wide.bit_length() - 1
    n_rows = BATCHES * chunks
    for ch in range(chunks):
        cell16[BATCHES * ch : BATCHES * (ch + 1), :] = cell[:, ch * H : (ch + 1) * H]
    cells = cell16[...]
    l_row = lax.shift_right_logical(cells, shift) - me_i * R
    l_col = (cells & (wide - 1)) - me_j * C
    mine = (l_row >= 0) & (l_row < R) & (l_col >= 0) & (l_col < C)
    mask = jnp.where(mine, 1.0, 0.0)
    before = jnp.where(iota((H, H), 0) < iota((H, H), 1), 1.0, 0.0)
    ii, jj = iota((n_rows, n_rows), 0), iota((n_rows, n_rows), 1)
    rows_before = jnp.where((lax.rem(ii, BATCHES) == lax.rem(jj, BATCHES)) & (jj < ii), 1.0, 0.0)
    totals = jnp.broadcast_to(jnp.sum(mask, axis=1, keepdims=True), (n_rows, H))
    rank = dot(mask, before) + dot(rows_before, totals)
    rank = jnp.where(mine, rank, -1.0).astype(jnp.int32)
    code = jnp.where(mine, l_row * C + l_col, 0).astype(jnp.float32)
    slot = iota((SLOTS, H), 0)
    n_copy.wait()
    picks[...] = jnp.zeros((BATCHES, M + 8, H), jnp.float32)
    sub_wide = iota((8, count), 0)
    for b in range(BATCHES):
        rows_b = [BATCHES * ch + b for ch in range(chunks)]
        chosen = [jnp.where(jnp.broadcast_to(rank[n : n + 1, :], (SLOTS, H)) == slot, 1.0, 0.0) for n in rows_b]
        code_b = jnp.concatenate([code[n : n + 1, :] for n in rows_b], axis=1)
        more = jnp.where(sub_wide == 0, jnp.broadcast_to(value[b : b + 1, :], (8, count)), 0.0)
        more = jnp.where(sub_wide == 1, jnp.broadcast_to(var[b : b + 1, :], (8, count)), more)
        more = jnp.where(sub_wide == 2, jnp.broadcast_to(code_b, (8, count)), more)
        picks[b, :, 0:SLOTS] = lax.dot_general(
            jnp.concatenate([noise[b], more], axis=0), jnp.concatenate(chosen, axis=1),
            (((1,), (1,)), ((), ())), precision=HI, preferred_element_type=jnp.float32,
        )
        id_v[b] = (picks[b, M : M + 8, :] + 0.5).astype(jnp.int32)
    id_copy = load(id_v, id_s, 11)

    def parts_of(x, y):
        return jnp.maximum(x, 0.0), -jnp.minimum(x, 0.0), jnp.maximum(y, 0.0), -jnp.minimum(y, 0.0)

    rates = [diff[f] for f in range(F)]
    low_edge, high_edge = me_i == 0, me_i == la - 1

    def centre_of(p, k):
        return 1.0 - p[0] - p[1] - p[2] - p[3] - 4.0 * k

    own_parts = parts_of(cxv, cyv)
    row_id = iota((R, C), 0)

    def set_coef(f, first, values):
        for n in range(5):
            for h in range(2):
                v = values[n][:, h * H : (h + 1) * H]
                coef[f, n, h, first : first + max(8, v.shape[0]), :] = jnp.broadcast_to(v, (max(8, v.shape[0]), H))

    for f in range(F):
        south = jnp.where((row_id == 0) & low_edge, 0.0, own_parts[2] + rates[f])
        north = jnp.where((row_id == R - 1) & high_edge, 0.0, own_parts[3] + rates[f])
        set_coef(f, 8, [centre_of(own_parts, rates[f]), own_parts[0] + rates[f], own_parts[1] + rates[f], south, north])

    def row_step(src, dst, f, r, src_at, dst_at, far, south=True, north=True):
        first, last = lane == 0, lane == H - 1
        if far is None:
            hw = he = jnp.zeros((M, H), jnp.float32)
        else:
            turn = (H - 1 - 2 * r) & (H - 1)
            hw, he = pltpu.roll(far[0], turn, 1), pltpu.roll(far[1], turn, 1)
        c0, c1 = src[f, r + src_at, :, 0:H], src[f, r + src_at, :, H:C]
        w0, w1 = pltpu.roll(c0, 1, 1), pltpu.roll(c1, 1, 1)
        e0, e1 = pltpu.roll(c0, H - 1, 1), pltpu.roll(c1, H - 1, 1)
        w0, w1 = jnp.where(first, hw, w0), jnp.where(first, w0, w1)
        e0, e1 = jnp.where(last, e1, e0), jnp.where(last, he, e1)
        for h, (c, w, e) in enumerate(((c0, w0, e0), (c1, w1, e1))):
            cut = slice(h * H, (h + 1) * H)
            rate = [coef[f, n, h, pl.ds(r + 8, 1), :] for n in range(5)]
            out = rate[0] * c + rate[1] * w + rate[2] * e
            if south:
                out = out + rate[3] * src[f, r + src_at - 1, :, cut]
            if north:
                out = out + rate[4] * src[f, r + src_at + 1, :, cut]
            dst[f, r + dst_at, :, cut] = out

    def step_one(f, r):
        row_step(q, x1, f, r, 2, 1, (far_w[f], far_e[f]))

    def step_two(f, r):
        row_step(x1, x2, f, r, 1, 0, (next_w[f], next_e[f]))

    def rows_of(step, begin, end):
        def body(r, carry):
            step(r)
            return carry

        lax.fori_loop(begin, end, body, 0, unroll=2)

    def inner(src, dst, src_at, dst_at):
        row_step(src, dst, 0, 0, src_at, dst_at, None, south=False)
        rows_of(lambda r: row_step(src, dst, 0, r, src_at, dst_at, None), 1, R - 1)
        row_step(src, dst, 0, R - 1, src_at, dst_at, None, north=False)

    inner(q, x1, 2, 1)
    inner(x1, x2, 1, 0)
    id_copy.wait()
    ids = [[id_s[b, 2, s] for s in range(SLOTS)] for b in range(BATCHES)]

    for copy in halo_copies:
        copy.wait_recv()
    halo_rows = [parts_of(crow_r[side, 0:1, :], crow_r[side, 1:2, :]) for side in range(2)]
    for f in range(F):
        for side, first in ((0, 0), (1, 8 + R)):
            p = halo_rows[side]
            set_coef(f, first, [centre_of(p, rates[f])] + [part + rates[f] for part in p])
    corners = jnp.concatenate([corner_r[n] for n in range(4)] + [jnp.zeros((H - 32, H), jnp.float32)], axis=0).T
    lane_row = iota((1, H), 1)

    def packed_rates(f, ref, side):
        p = parts_of(ref[side, 0:1, :], ref[side, 1:2, :])
        south = jnp.where((lane_row < 2) & low_edge, 0.0, p[2] + rates[f])
        north = jnp.where((lane_row >= 2 * R - 2) & high_edge, 0.0, p[3] + rates[f])
        return centre_of(p, rates[f]), p[0] + rates[f], p[1] + rates[f], south, north

    def halo_columns(f):
        for copy in field_copies[f][2:]:
            copy.wait_recv()
        corner = [jnp.broadcast_to(corners[f * M : (f + 1) * M, n : n + 1], (M, H)) for n in (3, 10, 17, 24)]
        west = far_w[f]
        west = jnp.where(lane == H - 1, corner[0], jnp.where(lane == 2 * R + 1, corner[2], west))
        east = far_e[f]
        east = jnp.where(lane == H - 2, corner[1], jnp.where(lane == 2 * R, corner[3], east))
        far_w[f] = west
        far_e[f] = east
        sides = (
            (next_w, west, pltpu.roll(west, 1, 1), pltpu.roll(own_w[f], 1, 1)),
            (next_e, east, pltpu.roll(own_e[f], H - 1, 1), pltpu.roll(east, H - 1, 1)),
        )
        for side, (to, c, w, e) in enumerate(sides):
            rate = packed_rates(f, ccol_r, side)
            out = rate[0] * c + rate[1] * w + rate[2] * e
            out = out + rate[3] * pltpu.roll(c, 2, 1) + rate[4] * pltpu.roll(c, H - 2, 1)
            to[f] = jnp.where(lane < 2 * R, out, 0.0)

    def fix_columns():
        inside = lane < 2 * R
        for side, to, far, new, outer, turn in (
            (1, fix_w, far_w, next_w, even, H - 1),
            (0, fix_e, far_e, next_e, ~even, 1),
        ):
            rate = packed_rates(0, ccol_s, side)
            beside = rate[1] if side == 1 else rate[2]
            u = jnp.where(inside & outer, beside * pltpu.roll(far[0], turn, 1), 0.0)
            near = beside * pltpu.roll(new[0], turn, 1) + rate[0] * u
            near = near + rate[3] * pltpu.roll(u, 2, 1) + rate[4] * pltpu.roll(u, H - 2, 1)
            to[...] = jnp.where(inside, jnp.where(outer, near, beside * pltpu.roll(u, H - turn, 1)), 0.0)

    def fix_rows():
        for copy in field_copies[0][:2]:
            copy.wait_recv()
        first, last = lane == 0, lane == H - 1
        for halo, q_at, x_at, n, row, inner_row in ((-1, 1, 0, 3, 0, 1), (R, R + 2, R + 1, 4, R - 1, R - 2)):
            step_one(0, halo)
            rate = [[coef[0, k, h, row + 8 : row + 9, :] for k in range(5)] for h in range(2)]
            t = [rate[h][n] * q[0, q_at, :, h * H : (h + 1) * H] for h in range(2)]
            w = [pltpu.roll(v, 1, 1) for v in t]
            e = [pltpu.roll(v, H - 1, 1) for v in t]
            w = [jnp.where(first, 0.0, w[0]), jnp.where(first, w[0], w[1])]
            e = [jnp.where(last, e[1], e[0]), jnp.where(last, 0.0, e[1])]
            for h in range(2):
                cut = slice(h * H, (h + 1) * H)
                add = rate[h][n] * x1[0, x_at, :, cut] + rate[h][0] * t[h] + rate[h][1] * w[h] + rate[h][2] * e[h]
                x2[0, row, :, cut] = x2[0, row, :, cut] + add
                x2[0, inner_row, :, cut] = (
                    x2[0, inner_row, :, cut] + coef[0, n, h, inner_row + 8 : inner_row + 9, :] * t[h]
                )

    def unpack_columns():
        def body(r):
            west = pltpu.roll(fix_w[...], (H - 2 * r) & (H - 1), 1)
            east = pltpu.roll(fix_e[...], (H - 2 - 2 * r) & (H - 1), 1)
            x2[0, r, :, 0:H] = x2[0, r, :, 0:H] + jnp.where(lane < 2, west, 0.0)
            x2[0, r, :, H:C] = x2[0, r, :, H:C] + jnp.where(lane >= H - 2, east, 0.0)

        rows_of(body, 0, R)

    def give(f):
        copy = pltpu.make_async_copy(x2.at[f], x_out.at[f], out_sem.at[f])
        copy.start()
        return copy

    def forecast(f):
        halo_columns(f)
        for copy in field_copies[f][:2]:
            copy.wait_recv()
        rows_of(lambda r: step_one(f, r), -1, R + 1)
        rows_of(lambda r: step_two(f, r), 0, R)

    def observe(b, fixes):
        f = b % F
        seen = jnp.zeros((M, H), jnp.float32)
        for s in range(SLOTS):
            code_s = ids[b][s]
            at_row = lax.shift_right_logical(code_s, 8) & (R - 1)
            col = code_s & (C - 1)
            row = x2[f, at_row]
            picked = jnp.where(lane == col, row[:, 0:H], 0.0) + jnp.where(lane + H == col, row[:, H:C], 0.0)
            if fixes:
                spot_w = jnp.where(col < 2, 2 * at_row + col, -1)
                spot_e = jnp.where(col >= C - 2, 2 * at_row + col - (C - 2), -1)
                picked = picked + jnp.where(lane == spot_w, fix_w[...], 0.0) + jnp.where(lane == spot_e, fix_e[...], 0.0)
            seen = jnp.where(lane == s, jnp.broadcast_to(jnp.sum(picked, axis=1, keepdims=True), (M, H)), seen)
        mean = jnp.sum(seen, axis=0, keepdims=True) * (1.0 / M)
        var_b = picks[b, M + 1 : M + 2, :]
        there = var_b > 0.0
        scale = jnp.where(there, jnp.sqrt(1.0 / jnp.where(there, var_b, 1.0)), 0.0)
        innovation = picks[b, M : M + 1, :] + picks[b, 0:M, :] - seen
        stacked = jnp.concatenate([scale * (seen - mean), scale * innovation, fill], axis=0)
        return stacked.T[0:SLOTS]

    def tell(b, r):
        packed = r[0:8] + pltpu.roll(r[8:16], 2 * M, 1)
        msg[b] = packed
        got[b, 14] = packed
        got[b, 15] = jnp.zeros((8, H), jnp.float32)
        copies = []
        for n, (di, dj) in enumerate(REACH):
            copy = pltpu.make_async_remote_copy(
                src_ref=msg.at[b], dst_ref=got.at[b, n], send_sem=p2_send.at[b, n], recv_sem=p2_recv.at[b, n],
                device_id=at(-di, -dj), device_id_type=MESH,
            )
            copy.start()
            copies.append(copy)
        started.extend(copies)
        return copies

    def transform(b, copies):
        for copy in copies:
            copy.wait_recv()
        stack = got[b].reshape(16 * 8, H)
        place = iota((16 * 8, H), 0)
        keep = jnp.where(low_edge & (place < 5 * 8), 0.0, 1.0)
        keep = jnp.where(high_edge & (place >= 9 * 8) & (place < 14 * 8), 0.0, keep)
        stack = stack * keep
        turned = stack.T
        gram = dot(jnp.concatenate([turned[0:M], turned[2 * M : 3 * M]], axis=0), stack)
        both = gram[0:M] + pltpu.roll(gram[M : 2 * M], 2 * M, 1)
        system = jnp.where(lane < 2 * M, both, 0.0) + jnp.where(lane == iota((M, H), 0), M - 1.0, 0.0)
        return eliminate(system)

    def centered_rows(solved):
        w = jnp.where(lane < M, pltpu.roll(solved, H - M, 1), 0.0)
        return w - jnp.sum(w, axis=0, keepdims=True) * (1.0 / M)

    halo_columns(0)
    fix_columns()
    fix_rows()
    copies0 = tell(0, observe(0, True))
    forecast(1)
    outs = [give(1)]
    r1 = observe(1, False)
    unpack_columns()
    outs.append(give(0))
    solved0 = transform(0, copies0)
    w0 = jnp.where(lane < M, pltpu.roll(solved0, H - M, 1), 0.0)
    w0_mean = jnp.sum(w0, axis=1, keepdims=True) * (1.0 / M)
    both0 = jnp.where(lane < M, w0 - w0_mean, jnp.where(lane < 2 * M, -solved0, 0.0))
    copies1 = tell(1, r1 + dot(r1[:, 0:M], both0))
    c0 = centered_rows(solved0)
    for copy in outs:
        copy.wait()
    for copy in started[: -len(REACH)]:
        copy.wait_send()
    solved1 = transform(1, copies1)
    c1 = centered_rows(solved1)
    e_out[...] = c0 + c1 + dot(c0[:, 0:M], c1)
    for copy in copies1:
        copy.wait_send()


def analysis_kernel(e_ref, x_in, out, x, y, in_sem, out_sem):
    groups = [(f, r) for f in range(F) for r in range(0, R, 8)]
    loads = []
    for n, (f, r) in enumerate(groups):
        copy = pltpu.make_async_copy(x_in.at[f, pl.ds(r, 8)], x.at[f, pl.ds(r, 8)], in_sem.at[n])
        copy.start()
        loads.append(copy)
    e = jnp.concatenate([e_ref[...], jnp.zeros((H - M, H), jnp.float32)], axis=0).T[0:M, 0:M]
    e_hi = e.astype(jnp.bfloat16)
    e_lo = (e - e_hi.astype(jnp.float32)).astype(jnp.bfloat16)
    left = jnp.concatenate([e_hi, e_hi, e_lo], axis=1)
    stores = []
    for n, (f, r) in enumerate(groups):
        loads[n].wait()
        for row in range(r, r + 8):
            v = x[f, row]
            hi = v.astype(jnp.bfloat16)
            low = (v - hi.astype(jnp.float32)).astype(jnp.bfloat16)
            right = jnp.concatenate([hi, low, hi], axis=0)
            add = lax.dot_general(left, right, (((1,), (0,)), ((), ())), preferred_element_type=jnp.float32)
            y[f, row] = v + add
        for row in range(r, r + 8):
            copy = pltpu.make_async_copy(y.at[f, row], out.at[f, :, row, :], out_sem.at[f, row])
            copy.start()
            stores.append(copy)
    for copy in stores:
        copy.wait()


def local(ensemble, courant_x, courant_y, diffusion, obs_cell, obs_value, obs_noise, obs_var, loc_mask):
    any_space = pl.BlockSpec(memory_space=pl.ANY)
    f32 = jnp.float32
    count = obs_cell.shape[1]
    vmem = pltpu.VMEM
    dma = pltpu.SemaphoreType.DMA
    forecast, combined = pl.pallas_call(
        forecast_kernel,
        out_shape=(jax.ShapeDtypeStruct((F, R, M, C), f32), jax.ShapeDtypeStruct((M, H), f32)),
        in_specs=[pl.BlockSpec(memory_space=pltpu.HBM)] * 8,
        out_specs=(any_space, pl.BlockSpec(memory_space=pltpu.VMEM)),
        scratch_shapes=[
            vmem((2, F, M * R, H), f32),
            vmem((F, R + 4, M, C), f32),
            vmem((F, R + 2, M, C), f32),
            vmem((F, R, M, C), f32),
            vmem((F, M, H), f32),
            vmem((F, M, H), f32),
            vmem((F, M, H), f32),
            vmem((F, M, H), f32),
            vmem((F, M, H), f32),
            vmem((F, M, H), f32),
            vmem((8, H), f32),
            vmem((4, 8, H), f32),
            vmem((2, 8, C), f32),
            vmem((2, 8, C), f32),
            vmem((2, 8, H), f32),
            vmem((2, 8, H), f32),
            vmem((M, H), f32),
            vmem((M, H), f32),
            vmem((F, 5, 2, R + 16, H), f32),
            vmem((R, C), f32),
            vmem((R, C), f32),
            pltpu.SMEM((F,), f32),
            vmem((BATCHES, count), jnp.int32),
            vmem((BATCHES * count // H, H), jnp.int32),
            vmem((BATCHES, count), f32),
            vmem((BATCHES, M, count), f32),
            vmem((BATCHES, count), f32),
            vmem((BATCHES, M + 8, H), f32),
            vmem((BATCHES, 8, H), jnp.int32),
            pltpu.SMEM((BATCHES, 8, H), jnp.int32),
            vmem((BATCHES, 8, H), f32),
            vmem((BATCHES, 16, 8, H), f32),
            dma((12,)),
            dma((F,)),
            dma((CHANNELS,)),
            dma((CHANNELS,)),
            dma((BATCHES, len(REACH))),
            dma((BATCHES, len(REACH))),
        ],
        compiler_params=pltpu.CompilerParams(
            collective_id=0, has_side_effects=True, vmem_limit_bytes=40 * 1024 * 1024
        ),
        name="forecast_and_transform",
    )(ensemble.reshape(F, M * R, C), courant_x, courant_y, diffusion, obs_cell, obs_value, obs_noise.swapaxes(1, 2), obs_var)
    return pl.pallas_call(
        analysis_kernel,
        out_shape=jax.ShapeDtypeStruct((F, M, R, C), f32),
        in_specs=[pl.BlockSpec(memory_space=pltpu.VMEM), any_space],
        out_specs=any_space,
        scratch_shapes=[
            vmem((F, R, M, C), f32),
            vmem((F, R, M, C), f32),
            dma((F * R // 8,)),
            dma((F, R)),
        ],
        compiler_params=pltpu.CompilerParams(vmem_limit_bytes=40 * 1024 * 1024),
        name="analysis",
    )(combined, forecast)


def solution(mesh):
    in_specs = (
        P(None, None, "lat", "lon"),
        P("lat", "lon"),
        P("lat", "lon"),
        P(),
        P(),
        P(),
        P(),
        P(),
        P("lat", "lon", None, None),
    )
    out_specs = P(None, None, "lat", "lon")
    return jax.shard_map(local, mesh=mesh, in_specs=in_specs, out_specs=out_specs, check_vma=False)
```

```python
import jax
import jax.numpy as jnp
from jax import lax
from jax.experimental import pallas as pl
from jax.experimental.pallas import tpu as pltpu
from jax.sharding import PartitionSpec as P

MESH = pl.DeviceIdType.MESH
HI = lax.Precision.HIGHEST
F, M, R, C = 2, 32, 32, 256
H = 128
SLOTS = 16
BATCHES = 2
GROUP = 16
REACH = tuple(sorted(((di, dj) for di in (-1, 0, 1) for dj in range(-2, 3) if (di, dj) != (0, 0)), key=lambda d: -abs(d[0]) * 3 - abs(d[1])))
ADJACENT = tuple(d for d in REACH if abs(d[1]) < 2)
ROWS, COLS, CORNER, CROWS, CCOLS = 0, 4, 8, 12, 14
CHANNELS = 16


def iota(shape, axis):
    return lax.broadcasted_iota(jnp.int32, shape, axis)


def dot(a, b):
    return lax.dot_general(a, b, (((1,), (0,)), ((), ())), precision=HI, preferred_element_type=jnp.float32)


def eliminate(system):
    parts = [system[8 * g : 8 * g + 8] for g in range(4)]
    sub = iota((8, H), 0)
    for own in range(4):
        lanes = range(8 * own, 8 * own + 8)
        columns = [[jnp.broadcast_to(part[:, k : k + 1], (8, H)) for part in parts] for k in lanes]
        pivots = [[jnp.broadcast_to(columns[j][own][i : i + 1], (8, H)) for j in range(8)] for i in range(8)]
        rows = [jnp.broadcast_to(parts[own][i : i + 1], (8, H)) for i in range(8)]
        for p in range(8):
            inverse = 1.0 / pivots[p][p]
            rows[p] = rows[p] * inverse
            for j in range(p + 1, 8):
                pivots[p][j] = pivots[p][j] * inverse
            for i in range(8):
                if i != p:
                    factor = pivots[i][p]
                    rows[i] = rows[i] - factor * rows[p]
                    for j in range(p + 1, 8):
                        pivots[i][j] = pivots[i][j] - factor * pivots[p][j]
        new = []
        for g in range(4):
            terms = [columns[j][g] * rows[j] for j in range(8)]
            while len(terms) > 1:
                terms = [terms[n] + terms[n + 1] for n in range(0, len(terms), 2)]
            new.append(parts[g] - terms[0])
        for i in range(8):
            new[own] = jnp.where(sub == i, rows[i], new[own])
        parts = new
    return jnp.concatenate(parts, axis=0)


def forecast_kernel(
    ens, cx_in, cy_in, diff_in, cell_in, value_in, noise_in, var_in,
    x_out, e_out,
    halves, q, x1, x2, own_w, own_e, far_w, far_e, next_w, next_e, corner_s, corner_r, crow_s, crow_r, ccol_s, ccol_r,
    fix_w, fix_e, coef, cx, cy, diff, cell, cell16, value, noise, var, picks, id_v, id_s, msg, got,
    in_sem, out_sem, p1_send, p1_recv, p2_send, p2_recv,
):
    la, lo = lax.axis_size("lat"), lax.axis_size("lon")
    me_i, me_j = lax.axis_index("lat"), lax.axis_index("lon")

    def at(di, dj):
        return (lax.rem(me_i + (di + la), la), lax.rem(me_j + (dj + lo), lo))

    barrier = pltpu.get_barrier_semaphore()
    for di, dj in ADJACENT:
        pl.semaphore_signal(barrier, inc=1, device_id=at(di, dj), device_id_type=MESH)

    def load(src, dst, sem):
        copy = pltpu.make_async_copy(src, dst, in_sem.at[sem])
        copy.start()
        return copy

    ens_copies = [
        [load(ens.at[f, :, pl.ds(h * H, H)], halves.at[h, f], 2 * f + h) for h in range(2)] for f in range(F)
    ]
    c_copies = [load(cx_in, cx, 4), load(cy_in, cy, 5), load(diff_in, diff, 6)]
    o_copies = [load(cell_in, cell, 7), load(value_in, value, 8), load(var_in, var, 9)]
    n_copy = load(noise_in, noise, 10)

    lane = iota((M, H), 1)
    lane8 = iota((8, H), 1)
    started = []

    def send(channel, src, dst, target):
        copy = pltpu.make_async_remote_copy(
            src_ref=src, dst_ref=dst, send_sem=p1_send.at[channel], recv_sem=p1_recv.at[channel],
            device_id=target, device_id_type=MESH,
        )
        copy.start()
        started.append(copy)
        return copy

    for copy in c_copies:
        copy.wait()
    cxv, cyv = cx[...], cy[...]
    for side, row in ((0, R - 1), (1, 0)):
        crow_s[side, 0:1, :] = cxv[row : row + 1, :]
        crow_s[side, 1:2, :] = cyv[row : row + 1, :]
    spot = (lax.shift_right_logical(lane, 1) == iota((R, H), 0)) & (lane < 2 * R)
    even = (lane & 1) == 0
    for side, col in ((0, C - 2), (1, 0)):
        for n, source in enumerate((cxv, cyv)):
            pair = [jnp.broadcast_to(source[:, col + c : col + c + 1], (R, H)) for c in range(2)]
            spread = jnp.where(spot, jnp.where(even, pair[0], pair[1]), 0.0)
            ccol_s[side, n : n + 1, :] = jnp.sum(spread, axis=0, keepdims=True)

    for f in range(F):
        for copy in ens_copies[f]:
            copy.wait()

    def corner_lanes(f):
        cells = [
            halves[0, f, pl.ds(0, M, stride=R), :],
            pltpu.roll(halves[1, f, pl.ds(0, M, stride=R), :], 2, 1),
            pltpu.roll(halves[0, f, pl.ds(R - 1, M, stride=R), :], 2, 1),
            pltpu.roll(halves[1, f, pl.ds(R - 1, M, stride=R), :], 4, 1),
        ]
        out = jnp.where(lane == 3, cells[3], 0.0)
        for n in range(3):
            out = jnp.where(lane == n, cells[n], out)
        return out

    fill = jnp.zeros((H - F * M, H), jnp.float32)
    corner_s[...] = jnp.concatenate([corner_lanes(0), corner_lanes(1), fill], axis=0).T[0:8]

    def pack(f):
        def body(r, carry):
            west, east = carry
            c0 = halves[0, f, pl.ds(r, M, stride=R), :]
            c1 = halves[1, f, pl.ds(r, M, stride=R), :]
            q[f, r + 2, :, 0:H] = c0
            q[f, r + 2, :, H:C] = c1
            here = lax.shift_right_logical(lane, 1) == r
            west = jnp.where(here, pltpu.roll(c0, 2 * r, 1), west)
            east = jnp.where(here, pltpu.roll(c1, lax.rem(2 * r + 2, H), 1), east)
            return west, east

        zero = jnp.zeros((M, H), jnp.float32)
        west, east = lax.fori_loop(0, R, body, (zero, zero), unroll=8)
        own_w[f] = west
        own_e[f] = east

    def send_field(f):
        return [
            send(ROWS + 2 * f, q.at[f, pl.ds(R, 2)], q.at[f, pl.ds(0, 2)], at(1, 0)),
            send(ROWS + 2 * f + 1, q.at[f, pl.ds(2, 2)], q.at[f, pl.ds(R + 2, 2)], at(-1, 0)),
            send(COLS + 2 * f, own_e.at[f], far_w.at[f], at(0, 1)),
            send(COLS + 2 * f + 1, own_w.at[f], far_e.at[f], at(0, -1)),
        ]

    pack(0)
    pack(1)
    pl.semaphore_wait(barrier, len(ADJACENT))
    halo_copies = []
    for n, target in enumerate(((1, 1), (1, -1), (-1, 1), (-1, -1))):
        halo_copies.append(send(CORNER + n, corner_s, corner_r.at[n], at(*target)))
    halo_copies += [
        send(CROWS, crow_s.at[0], crow_r.at[0], at(1, 0)),
        send(CROWS + 1, crow_s.at[1], crow_r.at[1], at(-1, 0)),
        send(CCOLS, ccol_s.at[0], ccol_r.at[0], at(0, 1)),
        send(CCOLS + 1, ccol_s.at[1], ccol_r.at[1], at(0, -1)),
    ]
    field_copies = [send_field(0)]
    field_copies.append(send_field(1))

    for copy in o_copies:
        copy.wait()
    count = cell.shape[1]
    chunks = count // H
    wide = lo * C
    shift = wide.bit_length() - 1
    n_rows = BATCHES * chunks
    for ch in range(chunks):
        cell16[BATCHES * ch : BATCHES * (ch + 1), :] = cell[:, ch * H : (ch + 1) * H]
    cells = cell16[...]
    l_row = lax.shift_right_logical(cells, shift) - me_i * R
    l_col = (cells & (wide - 1)) - me_j * C
    mine = (l_row >= 0) & (l_row < R) & (l_col >= 0) & (l_col < C)
    mask = jnp.where(mine, 1.0, 0.0)
    before = jnp.where(iota((H, H), 0) < iota((H, H), 1), 1.0, 0.0)
    ii, jj = iota((n_rows, n_rows), 0), iota((n_rows, n_rows), 1)
    rows_before = jnp.where((lax.rem(ii, BATCHES) == lax.rem(jj, BATCHES)) & (jj < ii), 1.0, 0.0)
    totals = jnp.broadcast_to(jnp.sum(mask, axis=1, keepdims=True), (n_rows, H))
    rank = dot(mask, before) + dot(rows_before, totals)
    rank = jnp.where(mine, rank, -1.0).astype(jnp.int32)
    code = jnp.where(mine, l_row * C + l_col, 0).astype(jnp.float32)
    slot = iota((SLOTS, H), 0)
    n_copy.wait()
    picks[...] = jnp.zeros((BATCHES, M + 8, H), jnp.float32)
    sub_wide = iota((8, count), 0)
    for b in range(BATCHES):
        rows_b = [BATCHES * ch + b for ch in range(chunks)]
        chosen = [jnp.where(jnp.broadcast_to(rank[n : n + 1, :], (SLOTS, H)) == slot, 1.0, 0.0) for n in rows_b]
        code_b = jnp.concatenate([code[n : n + 1, :] for n in rows_b], axis=1)
        more = jnp.where(sub_wide == 0, jnp.broadcast_to(value[b : b + 1, :], (8, count)), 0.0)
        more = jnp.where(sub_wide == 1, jnp.broadcast_to(var[b : b + 1, :], (8, count)), more)
        more = jnp.where(sub_wide == 2, jnp.broadcast_to(code_b, (8, count)), more)
        picks[b, :, 0:SLOTS] = lax.dot_general(
            jnp.concatenate([noise[b], more], axis=0), jnp.concatenate(chosen, axis=1),
            (((1,), (1,)), ((), ())), precision=HI, preferred_element_type=jnp.float32,
        )
        id_v[b] = (picks[b, M : M + 8, :] + 0.5).astype(jnp.int32)
    id_copy = load(id_v, id_s, 11)

    def parts_of(x, y):
        return jnp.maximum(x, 0.0), -jnp.minimum(x, 0.0), jnp.maximum(y, 0.0), -jnp.minimum(y, 0.0)

    rates = [diff[f] for f in range(F)]
    low_edge, high_edge = me_i == 0, me_i == la - 1

    def centre_of(p, k):
        return 1.0 - p[0] - p[1] - p[2] - p[3] - 4.0 * k

    own_parts = parts_of(cxv, cyv)
    row_id = iota((R, C), 0)

    def set_coef(f, first, values):
        for n in range(5):
            for h in range(2):
                v = values[n][:, h * H : (h + 1) * H]
                coef[f, n, h, first : first + max(8, v.shape[0]), :] = jnp.broadcast_to(v, (max(8, v.shape[0]), H))

    for f in range(F):
        south = jnp.where((row_id == 0) & low_edge, 0.0, own_parts[2] + rates[f])
        north = jnp.where((row_id == R - 1) & high_edge, 0.0, own_parts[3] + rates[f])
        set_coef(f, 8, [centre_of(own_parts, rates[f]), own_parts[0] + rates[f], own_parts[1] + rates[f], south, north])

    def row_step(src, dst, f, r, src_at, dst_at, far, south=True, north=True):
        first, last = lane == 0, lane == H - 1
        if far is None:
            hw = he = jnp.zeros((M, H), jnp.float32)
        else:
            turn = (H - 1 - 2 * r) & (H - 1)
            hw, he = pltpu.roll(far[0], turn, 1), pltpu.roll(far[1], turn, 1)
        c0, c1 = src[f, r + src_at, :, 0:H], src[f, r + src_at, :, H:C]
        w0, w1 = pltpu.roll(c0, 1, 1), pltpu.roll(c1, 1, 1)
        e0, e1 = pltpu.roll(c0, H - 1, 1), pltpu.roll(c1, H - 1, 1)
        w0, w1 = jnp.where(first, hw, w0), jnp.where(first, w0, w1)
        e0, e1 = jnp.where(last, e1, e0), jnp.where(last, he, e1)
        for h, (c, w, e) in enumerate(((c0, w0, e0), (c1, w1, e1))):
            cut = slice(h * H, (h + 1) * H)
            rate = [coef[f, n, h, pl.ds(r + 8, 1), :] for n in range(5)]
            out = rate[0] * c + rate[1] * w + rate[2] * e
            if south:
                out = out + rate[3] * src[f, r + src_at - 1, :, cut]
            if north:
                out = out + rate[4] * src[f, r + src_at + 1, :, cut]
            dst[f, r + dst_at, :, cut] = out

    def step_one(f, r):
        row_step(q, x1, f, r, 2, 1, (far_w[f], far_e[f]))

    def step_two(f, r):
        row_step(x1, x2, f, r, 1, 0, (next_w[f], next_e[f]))

    def rows_of(step, begin, end):
        def body(r, carry):
            step(r)
            return carry

        lax.fori_loop(begin, end, body, 0, unroll=2)

    def inner(src, dst, src_at, dst_at):
        row_step(src, dst, 0, 0, src_at, dst_at, None, south=False)
        rows_of(lambda r: row_step(src, dst, 0, r, src_at, dst_at, None), 1, R - 1)
        row_step(src, dst, 0, R - 1, src_at, dst_at, None, north=False)

    inner(q, x1, 2, 1)
    inner(x1, x2, 1, 0)
    id_copy.wait()
    ids = [[id_s[b, 2, s] for s in range(SLOTS)] for b in range(BATCHES)]

    for copy in halo_copies:
        copy.wait_recv()
    halo_rows = [parts_of(crow_r[side, 0:1, :], crow_r[side, 1:2, :]) for side in range(2)]
    for f in range(F):
        for side, first in ((0, 0), (1, 8 + R)):
            p = halo_rows[side]
            set_coef(f, first, [centre_of(p, rates[f])] + [part + rates[f] for part in p])
    corners = jnp.concatenate([corner_r[n] for n in range(4)] + [jnp.zeros((H - 32, H), jnp.float32)], axis=0).T
    lane_row = iota((1, H), 1)

    def packed_rates(f, ref, side):
        p = parts_of(ref[side, 0:1, :], ref[side, 1:2, :])
        south = jnp.where((lane_row < 2) & low_edge, 0.0, p[2] + rates[f])
        north = jnp.where((lane_row >= 2 * R - 2) & high_edge, 0.0, p[3] + rates[f])
        return centre_of(p, rates[f]), p[0] + rates[f], p[1] + rates[f], south, north

    def halo_columns(f):
        for copy in field_copies[f][2:]:
            copy.wait_recv()
        corner = [jnp.broadcast_to(corners[f * M : (f + 1) * M, n : n + 1], (M, H)) for n in (3, 10, 17, 24)]
        west = far_w[f]
        west = jnp.where(lane == H - 1, corner[0], jnp.where(lane == 2 * R + 1, corner[2], west))
        east = far_e[f]
        east = jnp.where(lane == H - 2, corner[1], jnp.where(lane == 2 * R, corner[3], east))
        far_w[f] = west
        far_e[f] = east
        sides = (
            (next_w, west, pltpu.roll(west, 1, 1), pltpu.roll(own_w[f], 1, 1)),
            (next_e, east, pltpu.roll(own_e[f], H - 1, 1), pltpu.roll(east, H - 1, 1)),
        )
        for side, (to, c, w, e) in enumerate(sides):
            rate = packed_rates(f, ccol_r, side)
            out = rate[0] * c + rate[1] * w + rate[2] * e
            out = out + rate[3] * pltpu.roll(c, 2, 1) + rate[4] * pltpu.roll(c, H - 2, 1)
            to[f] = jnp.where(lane < 2 * R, out, 0.0)

    def fix_columns():
        inside = lane < 2 * R
        for side, to, far, new, outer, turn in (
            (1, fix_w, far_w, next_w, even, H - 1),
            (0, fix_e, far_e, next_e, ~even, 1),
        ):
            rate = packed_rates(0, ccol_s, side)
            beside = rate[1] if side == 1 else rate[2]
            u = jnp.where(inside & outer, beside * pltpu.roll(far[0], turn, 1), 0.0)
            near = beside * pltpu.roll(new[0], turn, 1) + rate[0] * u
            near = near + rate[3] * pltpu.roll(u, 2, 1) + rate[4] * pltpu.roll(u, H - 2, 1)
            to[...] = jnp.where(inside, jnp.where(outer, near, beside * pltpu.roll(u, H - turn, 1)), 0.0)

    def fix_rows():
        for copy in field_copies[0][:2]:
            copy.wait_recv()
        first, last = lane == 0, lane == H - 1
        for halo, q_at, x_at, n, row, inner_row in ((-1, 1, 0, 3, 0, 1), (R, R + 2, R + 1, 4, R - 1, R - 2)):
            step_one(0, halo)
            rate = [[coef[0, k, h, row + 8 : row + 9, :] for k in range(5)] for h in range(2)]
            t = [rate[h][n] * q[0, q_at, :, h * H : (h + 1) * H] for h in range(2)]
            w = [pltpu.roll(v, 1, 1) for v in t]
            e = [pltpu.roll(v, H - 1, 1) for v in t]
            w = [jnp.where(first, 0.0, w[0]), jnp.where(first, w[0], w[1])]
            e = [jnp.where(last, e[1], e[0]), jnp.where(last, 0.0, e[1])]
            for h in range(2):
                cut = slice(h * H, (h + 1) * H)
                add = rate[h][n] * x1[0, x_at, :, cut] + rate[h][0] * t[h] + rate[h][1] * w[h] + rate[h][2] * e[h]
                x2[0, row, :, cut] = x2[0, row, :, cut] + add
                x2[0, inner_row, :, cut] = (
                    x2[0, inner_row, :, cut] + coef[0, n, h, inner_row + 8 : inner_row + 9, :] * t[h]
                )

    def unpack_columns():
        def body(r):
            west = pltpu.roll(fix_w[...], (H - 2 * r) & (H - 1), 1)
            east = pltpu.roll(fix_e[...], (H - 2 - 2 * r) & (H - 1), 1)
            x2[0, r, :, 0:H] = x2[0, r, :, 0:H] + jnp.where(lane < 2, west, 0.0)
            x2[0, r, :, H:C] = x2[0, r, :, H:C] + jnp.where(lane >= H - 2, east, 0.0)

        rows_of(body, 0, R)

    def give(f):
        copy = pltpu.make_async_copy(x2.at[f], x_out.at[f], out_sem.at[f])
        copy.start()
        return copy

    def forecast(f):
        halo_columns(f)
        for copy in field_copies[f][:2]:
            copy.wait_recv()
        rows_of(lambda r: step_one(f, r), -1, R + 1)
        rows_of(lambda r: step_two(f, r), 0, R)

    def observe(b, fixes):
        f = b % F
        seen = jnp.zeros((M, H), jnp.float32)
        for s in range(SLOTS):
            code_s = ids[b][s]
            at_row = lax.shift_right_logical(code_s, 8) & (R - 1)
            col = code_s & (C - 1)
            row = x2[f, at_row]
            picked = jnp.where(lane == col, row[:, 0:H], 0.0) + jnp.where(lane + H == col, row[:, H:C], 0.0)
            if fixes:
                spot_w = jnp.where(col < 2, 2 * at_row + col, -1)
                spot_e = jnp.where(col >= C - 2, 2 * at_row + col - (C - 2), -1)
                picked = picked + jnp.where(lane == spot_w, fix_w[...], 0.0) + jnp.where(lane == spot_e, fix_e[...], 0.0)
            seen = jnp.where(lane == s, jnp.broadcast_to(jnp.sum(picked, axis=1, keepdims=True), (M, H)), seen)
        mean = jnp.sum(seen, axis=0, keepdims=True) * (1.0 / M)
        var_b = picks[b, M + 1 : M + 2, :]
        there = var_b > 0.0
        scale = jnp.where(there, jnp.sqrt(1.0 / jnp.where(there, var_b, 1.0)), 0.0)
        innovation = picks[b, M : M + 1, :] + picks[b, 0:M, :] - seen
        stacked = jnp.concatenate([scale * (seen - mean), scale * innovation, fill], axis=0)
        return stacked.T[0:SLOTS]

    def tell(b, r):
        packed = r[0:8] + pltpu.roll(r[8:16], 2 * M, 1)
        msg[b] = packed
        got[b, 14] = packed
        got[b, 15] = jnp.zeros((8, H), jnp.float32)
        copies = []
        for n, (di, dj) in enumerate(REACH):
            copy = pltpu.make_async_remote_copy(
                src_ref=msg.at[b], dst_ref=got.at[b, n], send_sem=p2_send.at[b, n], recv_sem=p2_recv.at[b, n],
                device_id=at(-di, -dj), device_id_type=MESH,
            )
            copy.start()
            copies.append(copy)
        started.extend(copies)
        return copies

    def transform(b, copies):
        for copy in copies:
            copy.wait_recv()
        stack = got[b].reshape(16 * 8, H)
        place = lax.shift_right_logical(iota((16 * 8, H), 0), 3)
        keep = jnp.ones((16 * 8, H), jnp.float32)
        for n, (di, dj) in enumerate(REACH):
            if di != 0:
                keep = jnp.where((low_edge if di < 0 else high_edge) & (place == n), 0.0, keep)
        stack = stack * keep
        turned = stack.T
        gram = dot(jnp.concatenate([turned[0:M], turned[2 * M : 3 * M]], axis=0), stack)
        both = gram[0:M] + pltpu.roll(gram[M : 2 * M], 2 * M, 1)
        system = jnp.where(lane < 2 * M, both, 0.0) + jnp.where(lane == iota((M, H), 0), M - 1.0, 0.0)
        return eliminate(system)

    def centered_rows(solved):
        w = jnp.where(lane < M, pltpu.roll(solved, H - M, 1), 0.0)
        return w - jnp.sum(w, axis=0, keepdims=True) * (1.0 / M)

    halo_columns(0)
    fix_columns()
    fix_rows()
    copies0 = tell(0, observe(0, True))
    forecast(1)
    outs = [give(1)]
    r1 = observe(1, False)
    solved0 = transform(0, copies0)
    w0 = jnp.where(lane < M, pltpu.roll(solved0, H - M, 1), 0.0)
    w0_mean = jnp.sum(w0, axis=1, keepdims=True) * (1.0 / M)
    both0 = jnp.where(lane < M, w0 - w0_mean, jnp.where(lane < 2 * M, -solved0, 0.0))
    copies1 = tell(1, r1 + dot(r1[:, 0:M], both0))
    c0 = centered_rows(solved0)
    unpack_columns()
    outs.append(give(0))
    for copy in outs:
        copy.wait()
    for copy in started[: -len(REACH)]:
        copy.wait_send()
    solved1 = transform(1, copies1)
    c1 = centered_rows(solved1)
    e_out[...] = c0 + c1 + dot(c0[:, 0:M], c1)
    for copy in copies1:
        copy.wait_send()


def analysis_kernel(e_ref, x_in, out, x, y, in_sem, out_sem):
    groups = [(f, r) for f in range(F) for r in range(0, R, GROUP)]
    loads = []
    for n, (f, r) in enumerate(groups):
        copy = pltpu.make_async_copy(x_in.at[f, pl.ds(r, GROUP)], x.at[f, pl.ds(r, GROUP)], in_sem.at[n])
        copy.start()
        loads.append(copy)
    e = jnp.concatenate([e_ref[...], jnp.zeros((H - M, H), jnp.float32)], axis=0).T[0:M, 0:M]
    e_hi = e.astype(jnp.bfloat16)
    e_lo = (e - e_hi.astype(jnp.float32)).astype(jnp.bfloat16)
    left = jnp.concatenate([e_hi, e_hi, e_lo], axis=1)
    stores = []
    for n, (f, r) in enumerate(groups):
        loads[n].wait()
        for row in range(r, r + GROUP):
            v = x[f, row]
            hi = v.astype(jnp.bfloat16)
            low = (v - hi.astype(jnp.float32)).astype(jnp.bfloat16)
            right = jnp.concatenate([hi, low, hi], axis=0)
            add = lax.dot_general(left, right, (((1,), (0,)), ((), ())), preferred_element_type=jnp.float32)
            y[f, row] = v + add
        for row in range(r, r + GROUP):
            copy = pltpu.make_async_copy(y.at[f, row], out.at[f, :, row, :], out_sem.at[f, row])
            copy.start()
            stores.append(copy)
    for copy in stores:
        copy.wait()


def local(ensemble, courant_x, courant_y, diffusion, obs_cell, obs_value, obs_noise, obs_var, loc_mask):
    any_space = pl.BlockSpec(memory_space=pl.ANY)
    f32 = jnp.float32
    count = obs_cell.shape[1]
    vmem = pltpu.VMEM
    dma = pltpu.SemaphoreType.DMA
    forecast, combined = pl.pallas_call(
        forecast_kernel,
        out_shape=(jax.ShapeDtypeStruct((F, R, M, C), f32), jax.ShapeDtypeStruct((M, H), f32)),
        in_specs=[pl.BlockSpec(memory_space=pltpu.HBM)] * 8,
        out_specs=(any_space, pl.BlockSpec(memory_space=pltpu.VMEM)),
        scratch_shapes=[
            vmem((2, F, M * R, H), f32),
            vmem((F, R + 4, M, C), f32),
            vmem((F, R + 2, M, C), f32),
            vmem((F, R, M, C), f32),
            vmem((F, M, H), f32),
            vmem((F, M, H), f32),
            vmem((F, M, H), f32),
            vmem((F, M, H), f32),
            vmem((F, M, H), f32),
            vmem((F, M, H), f32),
            vmem((8, H), f32),
            vmem((4, 8, H), f32),
            vmem((2, 8, C), f32),
            vmem((2, 8, C), f32),
            vmem((2, 8, H), f32),
            vmem((2, 8, H), f32),
            vmem((M, H), f32),
            vmem((M, H), f32),
            vmem((F, 5, 2, R + 16, H), f32),
            vmem((R, C), f32),
            vmem((R, C), f32),
            pltpu.SMEM((F,), f32),
            vmem((BATCHES, count), jnp.int32),
            vmem((BATCHES * count // H, H), jnp.int32),
            vmem((BATCHES, count), f32),
            vmem((BATCHES, M, count), f32),
            vmem((BATCHES, count), f32),
            vmem((BATCHES, M + 8, H), f32),
            vmem((BATCHES, 8, H), jnp.int32),
            pltpu.SMEM((BATCHES, 8, H), jnp.int32),
            vmem((BATCHES, 8, H), f32),
            vmem((BATCHES, 16, 8, H), f32),
            dma((12,)),
            dma((F,)),
            dma((CHANNELS,)),
            dma((CHANNELS,)),
            dma((BATCHES, len(REACH))),
            dma((BATCHES, len(REACH))),
        ],
        compiler_params=pltpu.CompilerParams(
            collective_id=0, has_side_effects=True, vmem_limit_bytes=60 * 1024 * 1024
        ),
        name="forecast_and_transform",
    )(ensemble.reshape(F, M * R, C), courant_x, courant_y, diffusion, obs_cell, obs_value, obs_noise.swapaxes(1, 2), obs_var)
    return pl.pallas_call(
        analysis_kernel,
        out_shape=jax.ShapeDtypeStruct((F, M, R, C), f32),
        in_specs=[pl.BlockSpec(memory_space=pltpu.VMEM), any_space],
        out_specs=any_space,
        scratch_shapes=[
            vmem((F, R, M, C), f32),
            vmem((F, R, M, C), f32),
            dma((F * R // GROUP,)),
            dma((F, R)),
        ],
        compiler_params=pltpu.CompilerParams(vmem_limit_bytes=60 * 1024 * 1024),
        name="analysis",
    )(combined, forecast)


def solution(mesh):
    in_specs = (
        P(None, None, "lat", "lon"),
        P("lat", "lon"),
        P("lat", "lon"),
        P(),
        P(),
        P(),
        P(),
        P(),
        P("lat", "lon", None, None),
    )
    out_specs = P(None, None, "lat", "lon")
    return jax.shard_map(local, mesh=mesh, in_specs=in_specs, out_specs=out_specs, check_vma=False)
```

```python
import jax
import jax.numpy as jnp
from jax import lax
from jax.experimental import pallas as pl
from jax.experimental.pallas import tpu as pltpu
from jax.sharding import PartitionSpec as P

MESH = pl.DeviceIdType.MESH
HI = lax.Precision.HIGHEST
F, M, R, C = 2, 32, 32, 256
H = 128
SLOTS = 16
BATCHES = 2
GROUP = 16
REACH = tuple(sorted(((di, dj) for di in (-1, 0, 1) for dj in range(-2, 3) if (di, dj) != (0, 0)), key=lambda d: -abs(d[0]) * 3 - abs(d[1])))
ADJACENT = tuple(d for d in REACH if abs(d[1]) < 2)
ROWS, COLS, CORNER, CROWS, CCOLS = 0, 4, 8, 12, 14
CHANNELS = 16


def iota(shape, axis):
    return lax.broadcasted_iota(jnp.int32, shape, axis)


def dot(a, b):
    return lax.dot_general(a, b, (((1,), (0,)), ((), ())), precision=HI, preferred_element_type=jnp.float32)


def eliminate(system):
    parts = [system[8 * g : 8 * g + 8] for g in range(4)]
    sub = iota((8, H), 0)
    for own in range(4):
        lanes = range(8 * own, 8 * own + 8)
        columns = [[jnp.broadcast_to(part[:, k : k + 1], (8, H)) for part in parts] for k in lanes]
        pivots = [[jnp.broadcast_to(columns[j][own][i : i + 1], (8, H)) for j in range(8)] for i in range(8)]
        rows = [jnp.broadcast_to(parts[own][i : i + 1], (8, H)) for i in range(8)]
        for p in range(8):
            inverse = 1.0 / pivots[p][p]
            rows[p] = rows[p] * inverse
            for j in range(p + 1, 8):
                pivots[p][j] = pivots[p][j] * inverse
            for i in range(8):
                if i != p:
                    factor = pivots[i][p]
                    rows[i] = rows[i] - factor * rows[p]
                    for j in range(p + 1, 8):
                        pivots[i][j] = pivots[i][j] - factor * pivots[p][j]
        new = []
        for g in range(4):
            terms = [columns[j][g] * rows[j] for j in range(8)]
            while len(terms) > 1:
                terms = [terms[n] + terms[n + 1] for n in range(0, len(terms), 2)]
            new.append(parts[g] - terms[0])
        for i in range(8):
            new[own] = jnp.where(sub == i, rows[i], new[own])
        parts = new
    return jnp.concatenate(parts, axis=0)


def forecast_kernel(
    ens, cx_in, cy_in, diff_in, cell_in, value_in, noise_in, var_in,
    x2, e_out,
    halves, q, x1, own_w, own_e, far_w, far_e, next_w, next_e, corner_s, corner_r, crow_s, crow_r, ccol_s, ccol_r,
    fix_w, fix_e, coef, cx, cy, diff, cell, cell16, value, noise, var, picks, id_v, id_s, msg, got,
    in_sem, p1_send, p1_recv, p2_send, p2_recv,
):
    la, lo = lax.axis_size("lat"), lax.axis_size("lon")
    me_i, me_j = lax.axis_index("lat"), lax.axis_index("lon")

    def at(di, dj):
        return (lax.rem(me_i + (di + la), la), lax.rem(me_j + (dj + lo), lo))

    barrier = pltpu.get_barrier_semaphore()
    for di, dj in ADJACENT:
        pl.semaphore_signal(barrier, inc=1, device_id=at(di, dj), device_id_type=MESH)

    def load(src, dst, sem):
        copy = pltpu.make_async_copy(src, dst, in_sem.at[sem])
        copy.start()
        return copy

    ens_copies = [
        [load(ens.at[f, :, pl.ds(h * H, H)], halves.at[h, f], 2 * f + h) for h in range(2)] for f in range(F)
    ]
    c_copies = [load(cx_in, cx, 4), load(cy_in, cy, 5), load(diff_in, diff, 6)]
    o_copies = [load(cell_in, cell, 7), load(value_in, value, 8), load(var_in, var, 9)]
    n_copy = load(noise_in, noise, 10)

    lane = iota((M, H), 1)
    lane8 = iota((8, H), 1)
    started = []

    def send(channel, src, dst, target):
        copy = pltpu.make_async_remote_copy(
            src_ref=src, dst_ref=dst, send_sem=p1_send.at[channel], recv_sem=p1_recv.at[channel],
            device_id=target, device_id_type=MESH,
        )
        copy.start()
        started.append(copy)
        return copy

    for copy in c_copies:
        copy.wait()
    cxv, cyv = cx[...], cy[...]
    for side, row in ((0, R - 1), (1, 0)):
        crow_s[side, 0:1, :] = cxv[row : row + 1, :]
        crow_s[side, 1:2, :] = cyv[row : row + 1, :]
    spot = (lax.shift_right_logical(lane, 1) == iota((R, H), 0)) & (lane < 2 * R)
    even = (lane & 1) == 0
    for side, col in ((0, C - 2), (1, 0)):
        for n, source in enumerate((cxv, cyv)):
            pair = [jnp.broadcast_to(source[:, col + c : col + c + 1], (R, H)) for c in range(2)]
            spread = jnp.where(spot, jnp.where(even, pair[0], pair[1]), 0.0)
            ccol_s[side, n : n + 1, :] = jnp.sum(spread, axis=0, keepdims=True)

    for f in range(F):
        for copy in ens_copies[f]:
            copy.wait()

    def corner_lanes(f):
        cells = [
            halves[0, f, pl.ds(0, M, stride=R), :],
            pltpu.roll(halves[1, f, pl.ds(0, M, stride=R), :], 2, 1),
            pltpu.roll(halves[0, f, pl.ds(R - 1, M, stride=R), :], 2, 1),
            pltpu.roll(halves[1, f, pl.ds(R - 1, M, stride=R), :], 4, 1),
        ]
        out = jnp.where(lane == 3, cells[3], 0.0)
        for n in range(3):
            out = jnp.where(lane == n, cells[n], out)
        return out

    fill = jnp.zeros((H - F * M, H), jnp.float32)
    corner_s[...] = jnp.concatenate([corner_lanes(0), corner_lanes(1), fill], axis=0).T[0:8]

    def pack(f):
        def body(r, carry):
            west, east = carry
            c0 = halves[0, f, pl.ds(r, M, stride=R), :]
            c1 = halves[1, f, pl.ds(r, M, stride=R), :]
            q[f, r + 2, :, 0:H] = c0
            q[f, r + 2, :, H:C] = c1
            here = lax.shift_right_logical(lane, 1) == r
            west = jnp.where(here, pltpu.roll(c0, 2 * r, 1), west)
            east = jnp.where(here, pltpu.roll(c1, lax.rem(2 * r + 2, H), 1), east)
            return west, east

        zero = jnp.zeros((M, H), jnp.float32)
        west, east = lax.fori_loop(0, R, body, (zero, zero), unroll=8)
        own_w[f] = west
        own_e[f] = east

    def send_field(f):
        return [
            send(ROWS + 2 * f, q.at[f, pl.ds(R, 2)], q.at[f, pl.ds(0, 2)], at(1, 0)),
            send(ROWS + 2 * f + 1, q.at[f, pl.ds(2, 2)], q.at[f, pl.ds(R + 2, 2)], at(-1, 0)),
            send(COLS + 2 * f, own_e.at[f], far_w.at[f], at(0, 1)),
            send(COLS + 2 * f + 1, own_w.at[f], far_e.at[f], at(0, -1)),
        ]

    pack(0)
    pack(1)
    pl.semaphore_wait(barrier, len(ADJACENT))
    halo_copies = []
    for n, target in enumerate(((1, 1), (1, -1), (-1, 1), (-1, -1))):
        halo_copies.append(send(CORNER + n, corner_s, corner_r.at[n], at(*target)))
    halo_copies += [
        send(CROWS, crow_s.at[0], crow_r.at[0], at(1, 0)),
        send(CROWS + 1, crow_s.at[1], crow_r.at[1], at(-1, 0)),
        send(CCOLS, ccol_s.at[0], ccol_r.at[0], at(0, 1)),
        send(CCOLS + 1, ccol_s.at[1], ccol_r.at[1], at(0, -1)),
    ]
    field_copies = [send_field(0)]
    field_copies.append(send_field(1))

    for copy in o_copies:
        copy.wait()
    count = cell.shape[1]
    chunks = count // H
    wide = lo * C
    shift = wide.bit_length() - 1
    n_rows = BATCHES * chunks
    for ch in range(chunks):
        cell16[BATCHES * ch : BATCHES * (ch + 1), :] = cell[:, ch * H : (ch + 1) * H]
    cells = cell16[...]
    l_row = lax.shift_right_logical(cells, shift) - me_i * R
    l_col = (cells & (wide - 1)) - me_j * C
    mine = (l_row >= 0) & (l_row < R) & (l_col >= 0) & (l_col < C)
    mask = jnp.where(mine, 1.0, 0.0)
    before = jnp.where(iota((H, H), 0) < iota((H, H), 1), 1.0, 0.0)
    ii, jj = iota((n_rows, n_rows), 0), iota((n_rows, n_rows), 1)
    rows_before = jnp.where((lax.rem(ii, BATCHES) == lax.rem(jj, BATCHES)) & (jj < ii), 1.0, 0.0)
    totals = jnp.broadcast_to(jnp.sum(mask, axis=1, keepdims=True), (n_rows, H))
    rank = dot(mask, before) + dot(rows_before, totals)
    rank = jnp.where(mine, rank, -1.0).astype(jnp.int32)
    code = jnp.where(mine, l_row * C + l_col, 0).astype(jnp.float32)
    slot = iota((SLOTS, H), 0)
    n_copy.wait()
    picks[...] = jnp.zeros((BATCHES, M + 8, H), jnp.float32)
    sub_wide = iota((8, count), 0)
    for b in range(BATCHES):
        rows_b = [BATCHES * ch + b for ch in range(chunks)]
        chosen = [jnp.where(jnp.broadcast_to(rank[n : n + 1, :], (SLOTS, H)) == slot, 1.0, 0.0) for n in rows_b]
        code_b = jnp.concatenate([code[n : n + 1, :] for n in rows_b], axis=1)
        more = jnp.where(sub_wide == 0, jnp.broadcast_to(value[b : b + 1, :], (8, count)), 0.0)
        more = jnp.where(sub_wide == 1, jnp.broadcast_to(var[b : b + 1, :], (8, count)), more)
        more = jnp.where(sub_wide == 2, jnp.broadcast_to(code_b, (8, count)), more)
        picks[b, :, 0:SLOTS] = lax.dot_general(
            jnp.concatenate([noise[b], more], axis=0), jnp.concatenate(chosen, axis=1),
            (((1,), (1,)), ((), ())), precision=HI, preferred_element_type=jnp.float32,
        )
        id_v[b] = (picks[b, M : M + 8, :] + 0.5).astype(jnp.int32)
    id_copy = load(id_v, id_s, 11)

    def parts_of(x, y):
        return jnp.maximum(x, 0.0), -jnp.minimum(x, 0.0), jnp.maximum(y, 0.0), -jnp.minimum(y, 0.0)

    rates = [diff[f] for f in range(F)]
    low_edge, high_edge = me_i == 0, me_i == la - 1

    def centre_of(p, k):
        return 1.0 - p[0] - p[1] - p[2] - p[3] - 4.0 * k

    own_parts = parts_of(cxv, cyv)
    row_id = iota((R, C), 0)

    def set_coef(f, first, values):
        for n in range(5):
            for h in range(2):
                v = values[n][:, h * H : (h + 1) * H]
                coef[f, n, h, first : first + max(8, v.shape[0]), :] = jnp.broadcast_to(v, (max(8, v.shape[0]), H))

    for f in range(F):
        south = jnp.where((row_id == 0) & low_edge, 0.0, own_parts[2] + rates[f])
        north = jnp.where((row_id == R - 1) & high_edge, 0.0, own_parts[3] + rates[f])
        set_coef(f, 8, [centre_of(own_parts, rates[f]), own_parts[0] + rates[f], own_parts[1] + rates[f], south, north])

    def row_step(src, dst, f, r, src_at, dst_at, far, south=True, north=True):
        first, last = lane == 0, lane == H - 1
        if far is None:
            hw = he = jnp.zeros((M, H), jnp.float32)
        else:
            turn = (H - 1 - 2 * r) & (H - 1)
            hw, he = pltpu.roll(far[0], turn, 1), pltpu.roll(far[1], turn, 1)
        c0, c1 = src[f, r + src_at, :, 0:H], src[f, r + src_at, :, H:C]
        w0, w1 = pltpu.roll(c0, 1, 1), pltpu.roll(c1, 1, 1)
        e0, e1 = pltpu.roll(c0, H - 1, 1), pltpu.roll(c1, H - 1, 1)
        w0, w1 = jnp.where(first, hw, w0), jnp.where(first, w0, w1)
        e0, e1 = jnp.where(last, e1, e0), jnp.where(last, he, e1)
        for h, (c, w, e) in enumerate(((c0, w0, e0), (c1, w1, e1))):
            cut = slice(h * H, (h + 1) * H)
            rate = [coef[f, n, h, pl.ds(r + 8, 1), :] for n in range(5)]
            out = rate[0] * c + rate[1] * w + rate[2] * e
            if south:
                out = out + rate[3] * src[f, r + src_at - 1, :, cut]
            if north:
                out = out + rate[4] * src[f, r + src_at + 1, :, cut]
            dst[f, r + dst_at, :, cut] = out

    def step_one(f, r):
        row_step(q, x1, f, r, 2, 1, (far_w[f], far_e[f]))

    def step_two(f, r):
        row_step(x1, x2, f, r, 1, 0, (next_w[f], next_e[f]))

    def rows_of(step, begin, end):
        def body(r, carry):
            step(r)
            return carry

        lax.fori_loop(begin, end, body, 0, unroll=2)

    def inner(src, dst, src_at, dst_at):
        row_step(src, dst, 0, 0, src_at, dst_at, None, south=False)
        rows_of(lambda r: row_step(src, dst, 0, r, src_at, dst_at, None), 1, R - 1)
        row_step(src, dst, 0, R - 1, src_at, dst_at, None, north=False)

    inner(q, x1, 2, 1)
    inner(x1, x2, 1, 0)
    id_copy.wait()
    ids = [[id_s[b, 2, s] for s in range(SLOTS)] for b in range(BATCHES)]

    for copy in halo_copies:
        copy.wait_recv()
    halo_rows = [parts_of(crow_r[side, 0:1, :], crow_r[side, 1:2, :]) for side in range(2)]
    for f in range(F):
        for side, first in ((0, 0), (1, 8 + R)):
            p = halo_rows[side]
            set_coef(f, first, [centre_of(p, rates[f])] + [part + rates[f] for part in p])
    corners = jnp.concatenate([corner_r[n] for n in range(4)] + [jnp.zeros((H - 32, H), jnp.float32)], axis=0).T
    lane_row = iota((1, H), 1)

    def packed_rates(f, ref, side):
        p = parts_of(ref[side, 0:1, :], ref[side, 1:2, :])
        south = jnp.where((lane_row < 2) & low_edge, 0.0, p[2] + rates[f])
        north = jnp.where((lane_row >= 2 * R - 2) & high_edge, 0.0, p[3] + rates[f])
        return centre_of(p, rates[f]), p[0] + rates[f], p[1] + rates[f], south, north

    def halo_columns(f):
        for copy in field_copies[f][2:]:
            copy.wait_recv()
        corner = [jnp.broadcast_to(corners[f * M : (f + 1) * M, n : n + 1], (M, H)) for n in (3, 10, 17, 24)]
        west = far_w[f]
        west = jnp.where(lane == H - 1, corner[0], jnp.where(lane == 2 * R + 1, corner[2], west))
        east = far_e[f]
        east = jnp.where(lane == H - 2, corner[1], jnp.where(lane == 2 * R, corner[3], east))
        far_w[f] = west
        far_e[f] = east
        sides = (
            (next_w, west, pltpu.roll(west, 1, 1), pltpu.roll(own_w[f], 1, 1)),
            (next_e, east, pltpu.roll(own_e[f], H - 1, 1), pltpu.roll(east, H - 1, 1)),
        )
        for side, (to, c, w, e) in enumerate(sides):
            rate = packed_rates(f, ccol_r, side)
            out = rate[0] * c + rate[1] * w + rate[2] * e
            out = out + rate[3] * pltpu.roll(c, 2, 1) + rate[4] * pltpu.roll(c, H - 2, 1)
            to[f] = jnp.where(lane < 2 * R, out, 0.0)

    def fix_columns():
        inside = lane < 2 * R
        for side, to, far, new, outer, turn in (
            (1, fix_w, far_w, next_w, even, H - 1),
            (0, fix_e, far_e, next_e, ~even, 1),
        ):
            rate = packed_rates(0, ccol_s, side)
            beside = rate[1] if side == 1 else rate[2]
            u = jnp.where(inside & outer, beside * pltpu.roll(far[0], turn, 1), 0.0)
            near = beside * pltpu.roll(new[0], turn, 1) + rate[0] * u
            near = near + rate[3] * pltpu.roll(u, 2, 1) + rate[4] * pltpu.roll(u, H - 2, 1)
            to[...] = jnp.where(inside, jnp.where(outer, near, beside * pltpu.roll(u, H - turn, 1)), 0.0)

    def fix_rows():
        for copy in field_copies[0][:2]:
            copy.wait_recv()
        first, last = lane == 0, lane == H - 1
        for halo, q_at, x_at, n, row, inner_row in ((-1, 1, 0, 3, 0, 1), (R, R + 2, R + 1, 4, R - 1, R - 2)):
            step_one(0, halo)
            rate = [[coef[0, k, h, row + 8 : row + 9, :] for k in range(5)] for h in range(2)]
            t = [rate[h][n] * q[0, q_at, :, h * H : (h + 1) * H] for h in range(2)]
            w = [pltpu.roll(v, 1, 1) for v in t]
            e = [pltpu.roll(v, H - 1, 1) for v in t]
            w = [jnp.where(first, 0.0, w[0]), jnp.where(first, w[0], w[1])]
            e = [jnp.where(last, e[1], e[0]), jnp.where(last, 0.0, e[1])]
            for h in range(2):
                cut = slice(h * H, (h + 1) * H)
                add = rate[h][n] * x1[0, x_at, :, cut] + rate[h][0] * t[h] + rate[h][1] * w[h] + rate[h][2] * e[h]
                x2[0, row, :, cut] = x2[0, row, :, cut] + add
                x2[0, inner_row, :, cut] = (
                    x2[0, inner_row, :, cut] + coef[0, n, h, inner_row + 8 : inner_row + 9, :] * t[h]
                )

    def unpack_columns():
        def body(r):
            west = pltpu.roll(fix_w[...], (H - 2 * r) & (H - 1), 1)
            east = pltpu.roll(fix_e[...], (H - 2 - 2 * r) & (H - 1), 1)
            x2[0, r, :, 0:H] = x2[0, r, :, 0:H] + jnp.where(lane < 2, west, 0.0)
            x2[0, r, :, H:C] = x2[0, r, :, H:C] + jnp.where(lane >= H - 2, east, 0.0)

        rows_of(body, 0, R)

    def forecast(f):
        halo_columns(f)
        for copy in field_copies[f][:2]:
            copy.wait_recv()
        rows_of(lambda r: step_one(f, r), -1, R + 1)
        rows_of(lambda r: step_two(f, r), 0, R)

    def observe(b, fixes):
        f = b % F
        seen = jnp.zeros((M, H), jnp.float32)
        for s in range(SLOTS):
            code_s = ids[b][s]
            at_row = lax.shift_right_logical(code_s, 8) & (R - 1)
            col = code_s & (C - 1)
            row = x2[f, at_row]
            picked = jnp.where(lane == col, row[:, 0:H], 0.0) + jnp.where(lane + H == col, row[:, H:C], 0.0)
            if fixes:
                spot_w = jnp.where(col < 2, 2 * at_row + col, -1)
                spot_e = jnp.where(col >= C - 2, 2 * at_row + col - (C - 2), -1)
                picked = picked + jnp.where(lane == spot_w, fix_w[...], 0.0) + jnp.where(lane == spot_e, fix_e[...], 0.0)
            seen = jnp.where(lane == s, jnp.broadcast_to(jnp.sum(picked, axis=1, keepdims=True), (M, H)), seen)
        mean = jnp.sum(seen, axis=0, keepdims=True) * (1.0 / M)
        var_b = picks[b, M + 1 : M + 2, :]
        there = var_b > 0.0
        scale = jnp.where(there, jnp.sqrt(1.0 / jnp.where(there, var_b, 1.0)), 0.0)
        innovation = picks[b, M : M + 1, :] + picks[b, 0:M, :] - seen
        stacked = jnp.concatenate([scale * (seen - mean), scale * innovation, fill], axis=0)
        return stacked.T[0:SLOTS]

    def tell(b, r):
        packed = r[0:8] + pltpu.roll(r[8:16], 2 * M, 1)
        msg[b] = packed
        got[b, 14] = packed
        got[b, 15] = jnp.zeros((8, H), jnp.float32)
        copies = []
        for n, (di, dj) in enumerate(REACH):
            copy = pltpu.make_async_remote_copy(
                src_ref=msg.at[b], dst_ref=got.at[b, n], send_sem=p2_send.at[b, n], recv_sem=p2_recv.at[b, n],
                device_id=at(-di, -dj), device_id_type=MESH,
            )
            copy.start()
            copies.append(copy)
        started.extend(copies)
        return copies

    def transform(b, copies):
        for copy in copies:
            copy.wait_recv()
        stack = got[b].reshape(16 * 8, H)
        place = lax.shift_right_logical(iota((16 * 8, H), 0), 3)
        keep = jnp.ones((16 * 8, H), jnp.float32)
        for n, (di, dj) in enumerate(REACH):
            if di != 0:
                keep = jnp.where((low_edge if di < 0 else high_edge) & (place == n), 0.0, keep)
        stack = stack * keep
        turned = stack.T
        gram = dot(jnp.concatenate([turned[0:M], turned[2 * M : 3 * M]], axis=0), stack)
        both = gram[0:M] + pltpu.roll(gram[M : 2 * M], 2 * M, 1)
        system = jnp.where(lane < 2 * M, both, 0.0) + jnp.where(lane == iota((M, H), 0), M - 1.0, 0.0)
        return eliminate(system)

    def centered_rows(solved):
        w = jnp.where(lane < M, pltpu.roll(solved, H - M, 1), 0.0)
        return w - jnp.sum(w, axis=0, keepdims=True) * (1.0 / M)

    halo_columns(0)
    fix_columns()
    fix_rows()
    copies0 = tell(0, observe(0, True))
    forecast(1)
    r1 = observe(1, False)
    solved0 = transform(0, copies0)
    w0 = jnp.where(lane < M, pltpu.roll(solved0, H - M, 1), 0.0)
    w0_mean = jnp.sum(w0, axis=1, keepdims=True) * (1.0 / M)
    both0 = jnp.where(lane < M, w0 - w0_mean, jnp.where(lane < 2 * M, -solved0, 0.0))
    copies1 = tell(1, r1 + dot(r1[:, 0:M], both0))
    c0 = centered_rows(solved0)
    unpack_columns()
    for copy in started[: -len(REACH)]:
        copy.wait_send()
    solved1 = transform(1, copies1)
    c1 = centered_rows(solved1)
    e_out[...] = c0 + c1 + dot(c0[:, 0:M], c1)
    for copy in copies1:
        copy.wait_send()


def analysis_kernel(e_ref, x, out, y, out_sem):
    groups = [(f, r) for f in range(F) for r in range(0, R, GROUP)]
    e = jnp.concatenate([e_ref[...], jnp.zeros((H - M, H), jnp.float32)], axis=0).T[0:M, 0:M]
    e_hi = e.astype(jnp.bfloat16)
    e_lo = (e - e_hi.astype(jnp.float32)).astype(jnp.bfloat16)
    left = jnp.concatenate([e_hi, e_hi, e_lo], axis=1)
    stores = []
    for f, r in groups:
        for row in range(r, r + GROUP):
            v = x[f, row]
            hi = v.astype(jnp.bfloat16)
            low = (v - hi.astype(jnp.float32)).astype(jnp.bfloat16)
            right = jnp.concatenate([hi, low, hi], axis=0)
            add = lax.dot_general(left, right, (((1,), (0,)), ((), ())), preferred_element_type=jnp.float32)
            y[f, row] = v + add
        for row in range(r, r + GROUP):
            copy = pltpu.make_async_copy(y.at[f, row], out.at[f, :, row, :], out_sem.at[f, row])
            copy.start()
            stores.append(copy)
    for copy in stores:
        copy.wait()


def local(ensemble, courant_x, courant_y, diffusion, obs_cell, obs_value, obs_noise, obs_var, loc_mask):
    any_space = pl.BlockSpec(memory_space=pl.ANY)
    f32 = jnp.float32
    count = obs_cell.shape[1]
    vmem = pltpu.VMEM
    dma = pltpu.SemaphoreType.DMA
    noise_turned = obs_noise.swapaxes(1, 2)
    operands = (
        ensemble.reshape(F, M * R, C), courant_x, courant_y, diffusion, obs_cell, obs_value, noise_turned, obs_var
    )
    forecast, combined = pl.pallas_call(
        forecast_kernel,
        out_shape=(vmem((F, R, M, C), f32), vmem((M, H), f32)),
        in_specs=[pl.BlockSpec(memory_space=pltpu.HBM)] * 8,
        out_specs=(pl.BlockSpec(memory_space=pltpu.VMEM), pl.BlockSpec(memory_space=pltpu.VMEM)),
        scratch_shapes=[
            vmem((2, F, M * R, H), f32),
            vmem((F, R + 4, M, C), f32),
            vmem((F, R + 2, M, C), f32),
            vmem((F, M, H), f32),
            vmem((F, M, H), f32),
            vmem((F, M, H), f32),
            vmem((F, M, H), f32),
            vmem((F, M, H), f32),
            vmem((F, M, H), f32),
            vmem((8, H), f32),
            vmem((4, 8, H), f32),
            vmem((2, 8, C), f32),
            vmem((2, 8, C), f32),
            vmem((2, 8, H), f32),
            vmem((2, 8, H), f32),
            vmem((M, H), f32),
            vmem((M, H), f32),
            vmem((F, 5, 2, R + 16, H), f32),
            vmem((R, C), f32),
            vmem((R, C), f32),
            pltpu.SMEM((F,), f32),
            vmem((BATCHES, count), jnp.int32),
            vmem((BATCHES * count // H, H), jnp.int32),
            vmem((BATCHES, count), f32),
            vmem((BATCHES, M, count), f32),
            vmem((BATCHES, count), f32),
            vmem((BATCHES, M + 8, H), f32),
            vmem((BATCHES, 8, H), jnp.int32),
            pltpu.SMEM((BATCHES, 8, H), jnp.int32),
            vmem((BATCHES, 8, H), f32),
            vmem((BATCHES, 16, 8, H), f32),
            dma((12,)),
            dma((CHANNELS,)),
            dma((CHANNELS,)),
            dma((BATCHES, len(REACH))),
            dma((BATCHES, len(REACH))),
        ],
        compiler_params=pltpu.CompilerParams(
            collective_id=0, has_side_effects=True, vmem_limit_bytes=48 * 1024 * 1024
        ),
        name="forecast_and_transform",
    )(*(pltpu.with_memory_space_constraint(a, pltpu.HBM) for a in operands))
    return pl.pallas_call(
        analysis_kernel,
        out_shape=jax.ShapeDtypeStruct((F, M, R, C), f32),
        in_specs=[pl.BlockSpec(memory_space=pltpu.VMEM)] * 2,
        out_specs=any_space,
        scratch_shapes=[
            vmem((F, R, M, C), f32),
            dma((F, R)),
        ],
        compiler_params=pltpu.CompilerParams(vmem_limit_bytes=48 * 1024 * 1024),
        name="analysis",
    )(*(pltpu.with_memory_space_constraint(a, pltpu.VMEM) for a in (combined, forecast)))


def solution(mesh):
    in_specs = (
        P(None, None, "lat", "lon"),
        P("lat", "lon"),
        P("lat", "lon"),
        P(),
        P(),
        P(),
        P(),
        P(),
        P("lat", "lon", None, None),
    )
    out_specs = P(None, None, "lat", "lon")
    return jax.shard_map(local, mesh=mesh, in_specs=in_specs, out_specs=out_specs, check_vma=False)
```

```python
import jax
import jax.numpy as jnp
from jax import lax
from jax.experimental import pallas as pl
from jax.experimental.pallas import tpu as pltpu
from jax.sharding import PartitionSpec as P

MESH = pl.DeviceIdType.MESH
HI = lax.Precision.HIGHEST
F, M, R, C = 2, 32, 32, 256
H = 128
SLOTS = 16
BATCHES = 2
GROUP = 16
REACH = tuple(sorted(((di, dj) for di in (-1, 0, 1) for dj in range(-2, 3) if (di, dj) != (0, 0)), key=lambda d: -abs(d[0]) * 3 - abs(d[1])))
ADJACENT = tuple(d for d in REACH if abs(d[1]) < 2)
ROWS, COLS, CORNER, CROWS, CCOLS = 0, 2, 4, 5, 6
CHANNELS = 7


def iota(shape, axis):
    return lax.broadcasted_iota(jnp.int32, shape, axis)


def dot(a, b):
    return lax.dot_general(a, b, (((1,), (0,)), ((), ())), precision=HI, preferred_element_type=jnp.float32)


def eliminate(system):
    parts = [system[8 * g : 8 * g + 8] for g in range(4)]
    sub = iota((8, H), 0)
    for own in range(4):
        lanes = range(8 * own, 8 * own + 8)
        columns = [[jnp.broadcast_to(part[:, k : k + 1], (8, H)) for part in parts] for k in lanes]
        pivots = [[jnp.broadcast_to(columns[j][own][i : i + 1], (8, H)) for j in range(8)] for i in range(8)]
        rows = [jnp.broadcast_to(parts[own][i : i + 1], (8, H)) for i in range(8)]
        for p in range(8):
            inverse = 1.0 / pivots[p][p]
            rows[p] = rows[p] * inverse
            for j in range(p + 1, 8):
                pivots[p][j] = pivots[p][j] * inverse
            for i in range(8):
                if i != p:
                    factor = pivots[i][p]
                    rows[i] = rows[i] - factor * rows[p]
                    for j in range(p + 1, 8):
                        pivots[i][j] = pivots[i][j] - factor * pivots[p][j]
        new = []
        for g in range(4):
            terms = [columns[j][g] * rows[j] for j in range(8)]
            while len(terms) > 1:
                terms = [terms[n] + terms[n + 1] for n in range(0, len(terms), 2)]
            new.append(parts[g] - terms[0])
        for i in range(8):
            new[own] = jnp.where(sub == i, rows[i], new[own])
        parts = new
    return jnp.concatenate(parts, axis=0)


def forecast_kernel(
    ens, cx_in, cy_in, diff_in, cell_in, value_in, noise_in, var_in,
    x2, e_out,
    halves, q, x1, own_w, own_e, far, next_w, next_e, corner_s, corner_r, crow_s, crow_r, ccol_s, ccol_r,
    fix_w, fix_e, coef, courant, diff, cell, cell16, value, noise, picks, id_v, id_s, msg, got,
    in_sem, p1_send, p1_recv, p2_send, p2_recv,
):
    la, lo = lax.axis_size("lat"), lax.axis_size("lon")
    me_i, me_j = lax.axis_index("lat"), lax.axis_index("lon")

    def at(di, dj):
        return (lax.rem(me_i + (di + la), la), lax.rem(me_j + (dj + lo), lo))

    barrier = pltpu.get_barrier_semaphore()
    for di, dj in ADJACENT:
        pl.semaphore_signal(barrier, inc=1, device_id=at(di, dj), device_id_type=MESH)

    def load(src, dst, sem):
        copy = pltpu.make_async_copy(src, dst, in_sem.at[sem])
        copy.start()
        return copy

    def loaded(dst, sem):
        pltpu.make_async_copy(dst, dst, in_sem.at[sem]).wait()

    for f in range(F):
        for h in range(2):
            load(ens.at[f, :, pl.ds(h * H, H)], halves.at[h, f], 0)
    load(cx_in, courant.at[0], 1)
    load(cy_in, courant.at[1], 1)
    diff_copy = load(diff_in, diff, 2)
    cell_copy = load(cell_in, cell, 3)
    load(value_in, value.at[0], 4)
    load(var_in, value.at[1], 4)
    noise_copy = load(noise_in, noise, 5)

    lane = iota((M, H), 1)
    lane8 = iota((8, H), 1)
    def send(channel, src, dst, target):
        copy = pltpu.make_async_remote_copy(
            src_ref=src, dst_ref=dst, send_sem=p1_send.at[channel], recv_sem=p1_recv.at[channel],
            device_id=target, device_id_type=MESH,
        )
        copy.start()

    def sent(src, channel):
        pltpu.make_async_copy(src, src, p1_send.at[channel]).wait()

    def came(dst, channel):
        pltpu.make_async_copy(dst, dst, p1_recv.at[channel]).wait()

    loaded(courant, 1)
    diff_copy.wait()
    cxv, cyv = courant[0], courant[1]
    for side, row in ((0, R - 1), (1, 0)):
        crow_s[side, 0:1, :] = cxv[row : row + 1, :]
        crow_s[side, 1:2, :] = cyv[row : row + 1, :]
    spot = (lax.shift_right_logical(lane, 1) == iota((R, H), 0)) & (lane < 2 * R)
    even = (lane & 1) == 0
    for side, col in ((0, C - 2), (1, 0)):
        for n, source in enumerate((cxv, cyv)):
            pair = [jnp.broadcast_to(source[:, col + c : col + c + 1], (R, H)) for c in range(2)]
            spread = jnp.where(spot, jnp.where(even, pair[0], pair[1]), 0.0)
            ccol_s[side, n : n + 1, :] = jnp.sum(spread, axis=0, keepdims=True)

    loaded(halves, 0)

    def corner_lanes(f):
        cells = [
            halves[0, f, pl.ds(0, M, stride=R), :],
            pltpu.roll(halves[1, f, pl.ds(0, M, stride=R), :], 2, 1),
            pltpu.roll(halves[0, f, pl.ds(R - 1, M, stride=R), :], 2, 1),
            pltpu.roll(halves[1, f, pl.ds(R - 1, M, stride=R), :], 4, 1),
        ]
        out = jnp.where(lane == 3, cells[3], 0.0)
        for n in range(3):
            out = jnp.where(lane == n, cells[n], out)
        return out

    fill = jnp.zeros((H - F * M, H), jnp.float32)
    corner_s[...] = jnp.concatenate([corner_lanes(0), corner_lanes(1), fill], axis=0).T[0:8]

    def pack(f):
        def body(r, carry):
            west, east = carry
            c0 = halves[0, f, pl.ds(r, M, stride=R), :]
            c1 = halves[1, f, pl.ds(r, M, stride=R), :]
            q[f, r + 2, :, 0:H] = c0
            q[f, r + 2, :, H:C] = c1
            here = lax.shift_right_logical(lane, 1) == r
            west = jnp.where(here, pltpu.roll(c0, 2 * r, 1), west)
            east = jnp.where(here, pltpu.roll(c1, lax.rem(2 * r + 2, H), 1), east)
            return west, east

        zero = jnp.zeros((M, H), jnp.float32)
        west, east = lax.fori_loop(0, R, body, (zero, zero), unroll=8)
        own_w[f] = west
        own_e[f] = east

    def send_field(f):
        send(COLS + f, own_e.at[f], far.at[f, 0], at(0, 1))
        send(COLS + f, own_w.at[f], far.at[f, 1], at(0, -1))
        send(ROWS + f, q.at[f, pl.ds(R, 2)], q.at[f, pl.ds(0, 2)], at(1, 0))
        send(ROWS + f, q.at[f, pl.ds(2, 2)], q.at[f, pl.ds(R + 2, 2)], at(-1, 0))

    pack(0)
    pack(1)
    pl.semaphore_wait(barrier, len(ADJACENT))
    for n, target in enumerate(((1, 1), (1, -1), (-1, 1), (-1, -1))):
        send(CORNER, corner_s, corner_r.at[n], at(*target))
    send(CROWS, crow_s.at[0], crow_r.at[0], at(1, 0))
    send(CROWS, crow_s.at[1], crow_r.at[1], at(-1, 0))
    send(CCOLS, ccol_s.at[0], ccol_r.at[0], at(0, 1))
    send(CCOLS, ccol_s.at[1], ccol_r.at[1], at(0, -1))
    send_field(0)

    cell_copy.wait()
    loaded(value, 4)
    count = cell.shape[1]
    chunks = count // H
    wide = lo * C
    shift = wide.bit_length() - 1
    n_rows = BATCHES * chunks
    for ch in range(chunks):
        cell16[BATCHES * ch : BATCHES * (ch + 1), :] = cell[:, ch * H : (ch + 1) * H]
    cells = cell16[...]
    l_row = lax.shift_right_logical(cells, shift) - me_i * R
    l_col = (cells & (wide - 1)) - me_j * C
    mine = (l_row >= 0) & (l_row < R) & (l_col >= 0) & (l_col < C)
    mask = jnp.where(mine, 1.0, 0.0)
    before = jnp.where(iota((H, H), 0) < iota((H, H), 1), 1.0, 0.0)
    ii, jj = iota((n_rows, n_rows), 0), iota((n_rows, n_rows), 1)
    rows_before = jnp.where((lax.rem(ii, BATCHES) == lax.rem(jj, BATCHES)) & (jj < ii), 1.0, 0.0)
    totals = jnp.broadcast_to(jnp.sum(mask, axis=1, keepdims=True), (n_rows, H))
    rank = dot(mask, before) + dot(rows_before, totals)
    rank = jnp.where(mine, rank, -1.0).astype(jnp.int32)
    code = jnp.where(mine, l_row * C + l_col, 0).astype(jnp.float32)
    slot = iota((SLOTS, H), 0)
    noise_copy.wait()
    picks[...] = jnp.zeros((BATCHES, M + 8, H), jnp.float32)
    sub_wide = iota((8, count), 0)
    for b in range(BATCHES):
        rows_b = [BATCHES * ch + b for ch in range(chunks)]
        chosen = [jnp.where(jnp.broadcast_to(rank[n : n + 1, :], (SLOTS, H)) == slot, 1.0, 0.0) for n in rows_b]
        code_b = jnp.concatenate([code[n : n + 1, :] for n in rows_b], axis=1)
        more = jnp.where(sub_wide == 0, jnp.broadcast_to(value[0, b : b + 1, :], (8, count)), 0.0)
        more = jnp.where(sub_wide == 1, jnp.broadcast_to(value[1, b : b + 1, :], (8, count)), more)
        more = jnp.where(sub_wide == 2, jnp.broadcast_to(code_b, (8, count)), more)
        picks[b, :, 0:SLOTS] = lax.dot_general(
            jnp.concatenate([noise[b], more], axis=0), jnp.concatenate(chosen, axis=1),
            (((1,), (1,)), ((), ())), precision=HI, preferred_element_type=jnp.float32,
        )
        id_v[b] = (picks[b, M : M + 8, :] + 0.5).astype(jnp.int32)
    id_copy = load(id_v, id_s, 6)

    def parts_of(x, y):
        return jnp.maximum(x, 0.0), -jnp.minimum(x, 0.0), jnp.maximum(y, 0.0), -jnp.minimum(y, 0.0)

    rates = [diff[f] for f in range(F)]
    low_edge, high_edge = me_i == 0, me_i == la - 1

    def centre_of(p, k):
        return 1.0 - p[0] - p[1] - p[2] - p[3] - 4.0 * k

    own_parts = parts_of(cxv, cyv)
    row_id = iota((R, C), 0)

    def set_coef(f, first, values):
        for n in range(5):
            for h in range(2):
                v = values[n][:, h * H : (h + 1) * H]
                coef[f, n, h, first : first + max(8, v.shape[0]), :] = jnp.broadcast_to(v, (max(8, v.shape[0]), H))

    for f in range(F):
        south = jnp.where((row_id == 0) & low_edge, 0.0, own_parts[2] + rates[f])
        north = jnp.where((row_id == R - 1) & high_edge, 0.0, own_parts[3] + rates[f])
        set_coef(f, 8, [centre_of(own_parts, rates[f]), own_parts[0] + rates[f], own_parts[1] + rates[f], south, north])

    def row_step(src, dst, f, r, src_at, dst_at, far, south=True, north=True):
        first, last = lane == 0, lane == H - 1
        if far is None:
            hw = he = jnp.zeros((M, H), jnp.float32)
        else:
            turn = (H - 1 - 2 * r) & (H - 1)
            hw, he = pltpu.roll(far[0], turn, 1), pltpu.roll(far[1], turn, 1)
        c0, c1 = src[f, r + src_at, :, 0:H], src[f, r + src_at, :, H:C]
        w0, w1 = pltpu.roll(c0, 1, 1), pltpu.roll(c1, 1, 1)
        e0, e1 = pltpu.roll(c0, H - 1, 1), pltpu.roll(c1, H - 1, 1)
        w0, w1 = jnp.where(first, hw, w0), jnp.where(first, w0, w1)
        e0, e1 = jnp.where(last, e1, e0), jnp.where(last, he, e1)
        for h, (c, w, e) in enumerate(((c0, w0, e0), (c1, w1, e1))):
            cut = slice(h * H, (h + 1) * H)
            rate = [coef[f, n, h, pl.ds(r + 8, 1), :] for n in range(5)]
            out = rate[0] * c + rate[1] * w + rate[2] * e
            if south:
                out = out + rate[3] * src[f, r + src_at - 1, :, cut]
            if north:
                out = out + rate[4] * src[f, r + src_at + 1, :, cut]
            dst[f, r + dst_at, :, cut] = out

    def step_one(f, r):
        row_step(q, x1, f, r, 2, 1, (far[f, 0], far[f, 1]))

    def rows_of(step, begin, end):
        def body(r, carry):
            step(r)
            return carry

        lax.fori_loop(begin, end, body, 0, unroll=2)

    def inner(f, src, dst, src_at, dst_at):
        row_step(src, dst, f, 0, src_at, dst_at, None, south=False)
        rows_of(lambda r: row_step(src, dst, f, r, src_at, dst_at, None), 1, R - 1)
        row_step(src, dst, f, R - 1, src_at, dst_at, None, north=False)

    inner(0, q, x1, 2, 1)
    send_field(1)
    inner(0, x1, x2, 1, 0)
    id_copy.wait()
    ids = [[id_s[b, 2, s] for s in range(SLOTS)] for b in range(BATCHES)]

    came(crow_r, CROWS)
    came(ccol_r, CCOLS)
    halo_rows = [parts_of(crow_r[side, 0:1, :], crow_r[side, 1:2, :]) for side in range(2)]
    for f in range(F):
        for side, first in ((0, 0), (1, 8 + R)):
            p = halo_rows[side]
            set_coef(f, first, [centre_of(p, rates[f])] + [part + rates[f] for part in p])
    came(corner_r, CORNER)
    corners = jnp.concatenate([corner_r[n] for n in range(4)] + [jnp.zeros((H - 32, H), jnp.float32)], axis=0).T
    lane_row = iota((1, H), 1)

    def packed_rates(f, ref, side):
        p = parts_of(ref[side, 0:1, :], ref[side, 1:2, :])
        south = jnp.where((lane_row < 2) & low_edge, 0.0, p[2] + rates[f])
        north = jnp.where((lane_row >= 2 * R - 2) & high_edge, 0.0, p[3] + rates[f])
        return centre_of(p, rates[f]), p[0] + rates[f], p[1] + rates[f], south, north

    def halo_columns(f):
        came(far.at[f], COLS + f)
        corner = [jnp.broadcast_to(corners[f * M : (f + 1) * M, n : n + 1], (M, H)) for n in (3, 10, 17, 24)]
        west = far[f, 0]
        west = jnp.where(lane == H - 1, corner[0], jnp.where(lane == 2 * R + 1, corner[2], west))
        east = far[f, 1]
        east = jnp.where(lane == H - 2, corner[1], jnp.where(lane == 2 * R, corner[3], east))
        far[f, 0] = west
        far[f, 1] = east
        sides = (
            (next_w, west, pltpu.roll(west, 1, 1), pltpu.roll(own_w[f], 1, 1)),
            (next_e, east, pltpu.roll(own_e[f], H - 1, 1), pltpu.roll(east, H - 1, 1)),
        )
        for side, (to, c, w, e) in enumerate(sides):
            rate = packed_rates(f, ccol_r, side)
            out = rate[0] * c + rate[1] * w + rate[2] * e
            out = out + rate[3] * pltpu.roll(c, 2, 1) + rate[4] * pltpu.roll(c, H - 2, 1)
            to[f] = jnp.where(lane < 2 * R, out, 0.0)

    def fix_columns(f):
        inside = lane < 2 * R
        for side, to, outside, new, outer, turn in (
            (1, fix_w, far[f, 0], next_w, even, H - 1),
            (0, fix_e, far[f, 1], next_e, ~even, 1),
        ):
            rate = packed_rates(f, ccol_s, side)
            beside = rate[1] if side == 1 else rate[2]
            u = jnp.where(inside & outer, beside * pltpu.roll(outside, turn, 1), 0.0)
            near = beside * pltpu.roll(new[f], turn, 1) + rate[0] * u
            near = near + rate[3] * pltpu.roll(u, 2, 1) + rate[4] * pltpu.roll(u, H - 2, 1)
            to[f] = jnp.where(inside, jnp.where(outer, near, beside * pltpu.roll(u, H - turn, 1)), 0.0)

    def fix_rows(f):
        came(q.at[f, pl.ds(0, 4)], ROWS + f)
        first, last = lane == 0, lane == H - 1
        for halo, q_at, x_at, n, row, inner_row in ((-1, 1, 0, 3, 0, 1), (R, R + 2, R + 1, 4, R - 1, R - 2)):
            step_one(f, halo)
            rate = [[coef[f, k, h, row + 8 : row + 9, :] for k in range(5)] for h in range(2)]
            t = [rate[h][n] * q[f, q_at, :, h * H : (h + 1) * H] for h in range(2)]
            w = [pltpu.roll(v, 1, 1) for v in t]
            e = [pltpu.roll(v, H - 1, 1) for v in t]
            w = [jnp.where(first, 0.0, w[0]), jnp.where(first, w[0], w[1])]
            e = [jnp.where(last, e[1], e[0]), jnp.where(last, 0.0, e[1])]
            for h in range(2):
                cut = slice(h * H, (h + 1) * H)
                add = rate[h][n] * x1[f, x_at, :, cut] + rate[h][0] * t[h] + rate[h][1] * w[h] + rate[h][2] * e[h]
                x2[f, row, :, cut] = x2[f, row, :, cut] + add
                x2[f, inner_row, :, cut] = (
                    x2[f, inner_row, :, cut] + coef[f, n, h, inner_row + 8 : inner_row + 9, :] * t[h]
                )

    def unpack_columns(f):
        def body(r):
            west = pltpu.roll(fix_w[f], (H - 2 * r) & (H - 1), 1)
            east = pltpu.roll(fix_e[f], (H - 2 - 2 * r) & (H - 1), 1)
            x2[f, r, :, 0:H] = x2[f, r, :, 0:H] + jnp.where(lane < 2, west, 0.0)
            x2[f, r, :, H:C] = x2[f, r, :, H:C] + jnp.where(lane >= H - 2, east, 0.0)

        rows_of(body, 0, R)

    def observe(b):
        f = b % F
        seen = jnp.zeros((M, H), jnp.float32)
        for s in range(SLOTS):
            code_s = ids[b][s]
            at_row = lax.shift_right_logical(code_s, 8) & (R - 1)
            col = code_s & (C - 1)
            row = x2[f, at_row]
            picked = jnp.where(lane == col, row[:, 0:H], 0.0) + jnp.where(lane + H == col, row[:, H:C], 0.0)
            spot_w = jnp.where(col < 2, 2 * at_row + col, -1)
            spot_e = jnp.where(col >= C - 2, 2 * at_row + col - (C - 2), -1)
            picked = picked + jnp.where(lane == spot_w, fix_w[f], 0.0) + jnp.where(lane == spot_e, fix_e[f], 0.0)
            seen = jnp.where(lane == s, jnp.broadcast_to(jnp.sum(picked, axis=1, keepdims=True), (M, H)), seen)
        mean = jnp.sum(seen, axis=0, keepdims=True) * (1.0 / M)
        var_b = picks[b, M + 1 : M + 2, :]
        there = var_b > 0.0
        scale = jnp.where(there, jnp.sqrt(1.0 / jnp.where(there, var_b, 1.0)), 0.0)
        innovation = picks[b, M : M + 1, :] + picks[b, 0:M, :] - seen
        stacked = jnp.concatenate([scale * (seen - mean), scale * innovation, fill], axis=0)
        return stacked.T[0:SLOTS]

    def tell(b, r):
        packed = r[0:8] + pltpu.roll(r[8:16], 2 * M, 1)
        msg[b] = packed
        got[b, 14] = packed
        got[b, 15] = jnp.zeros((8, H), jnp.float32)
        for n, (di, dj) in enumerate(REACH):
            pltpu.make_async_remote_copy(
                src_ref=msg.at[b], dst_ref=got.at[b, n], send_sem=p2_send.at[b], recv_sem=p2_recv.at[b],
                device_id=at(-di, -dj), device_id_type=MESH,
            ).start()

    def transform(b):
        others = got.at[b, pl.ds(0, len(REACH))]
        pltpu.make_async_copy(others, others, p2_recv.at[b]).wait()
        stack = got[b].reshape(16 * 8, H)
        place = lax.shift_right_logical(iota((16 * 8, H), 0), 3)
        keep = jnp.ones((16 * 8, H), jnp.float32)
        for n, (di, dj) in enumerate(REACH):
            if di != 0:
                keep = jnp.where((low_edge if di < 0 else high_edge) & (place == n), 0.0, keep)
        stack = stack * keep
        turned = stack.T
        gram = dot(jnp.concatenate([turned[0:M], turned[2 * M : 3 * M]], axis=0), stack)
        both = gram[0:M] + pltpu.roll(gram[M : 2 * M], 2 * M, 1)
        system = jnp.where(lane < 2 * M, both, 0.0) + jnp.where(lane == iota((M, H), 0), M - 1.0, 0.0)
        return eliminate(system)

    def centered_rows(solved):
        w = jnp.where(lane < M, pltpu.roll(solved, H - M, 1), 0.0)
        return w - jnp.sum(w, axis=0, keepdims=True) * (1.0 / M)

    halo_columns(0)
    fix_columns(0)
    fix_rows(0)
    tell(0, observe(0))
    inner(1, q, x1, 2, 1)
    inner(1, x1, x2, 1, 0)
    halo_columns(1)
    fix_columns(1)
    fix_rows(1)
    r1 = observe(1)
    solved0 = transform(0)
    w0 = jnp.where(lane < M, pltpu.roll(solved0, H - M, 1), 0.0)
    w0_mean = jnp.sum(w0, axis=1, keepdims=True) * (1.0 / M)
    both0 = jnp.where(lane < M, w0 - w0_mean, jnp.where(lane < 2 * M, -solved0, 0.0))
    tell(1, r1 + dot(r1[:, 0:M], both0))
    c0 = centered_rows(solved0)
    unpack_columns(0)
    unpack_columns(1)
    for f in range(F):
        sent(q.at[f, pl.ds(2, 4)], ROWS + f)
        sent(far.at[f], COLS + f)
    sent(corner_r, CORNER)
    sent(crow_s, CROWS)
    sent(ccol_s, CCOLS)
    solved1 = transform(1)
    c1 = centered_rows(solved1)
    e_out[...] = c0 + c1 + dot(c0[:, 0:M], c1)
    for b in range(BATCHES):
        others = got.at[b, pl.ds(0, len(REACH))]
        pltpu.make_async_copy(others, others, p2_send.at[b]).wait()


def analysis_kernel(e_ref, x, out, y, out_sem):
    groups = [(f, r) for f in range(F) for r in range(0, R, GROUP)]
    e = jnp.concatenate([e_ref[...], jnp.zeros((H - M, H), jnp.float32)], axis=0).T[0:M, 0:M]
    e_hi = e.astype(jnp.bfloat16)
    e_lo = (e - e_hi.astype(jnp.float32)).astype(jnp.bfloat16)
    left = jnp.concatenate([e_hi, e_hi, e_lo], axis=1)
    for f, r in groups:
        for row in range(r, r + GROUP):
            v = x[f, row]
            hi = v.astype(jnp.bfloat16)
            low = (v - hi.astype(jnp.float32)).astype(jnp.bfloat16)
            right = jnp.concatenate([hi, low, hi], axis=0)
            add = lax.dot_general(left, right, (((1,), (0,)), ((), ())), preferred_element_type=jnp.float32)
            y[f, row] = v + add
        for row in range(r, r + GROUP):
            pltpu.make_async_copy(y.at[f, row], out.at[f, :, row, :], out_sem).start()
    pltpu.make_async_copy(y, y, out_sem).wait()


def local(ensemble, courant_x, courant_y, diffusion, obs_cell, obs_value, obs_noise, obs_var, loc_mask):
    any_space = pl.BlockSpec(memory_space=pl.ANY)
    f32 = jnp.float32
    count = obs_cell.shape[1]
    vmem = pltpu.VMEM
    dma = pltpu.SemaphoreType.DMA
    noise_turned = obs_noise.swapaxes(1, 2)
    operands = (
        ensemble.reshape(F, M * R, C), courant_x, courant_y, diffusion, obs_cell, obs_value, noise_turned, obs_var
    )
    forecast, combined = pl.pallas_call(
        forecast_kernel,
        out_shape=(vmem((F, R, M, C), f32), vmem((M, H), f32)),
        in_specs=[pl.BlockSpec(memory_space=pltpu.HBM)] * 8,
        out_specs=(pl.BlockSpec(memory_space=pltpu.VMEM), pl.BlockSpec(memory_space=pltpu.VMEM)),
        scratch_shapes=[
            vmem((2, F, M * R, H), f32),
            vmem((F, R + 4, M, C), f32),
            vmem((F, R + 2, M, C), f32),
            vmem((F, M, H), f32),
            vmem((F, M, H), f32),
            vmem((F, 2, M, H), f32),
            vmem((F, M, H), f32),
            vmem((F, M, H), f32),
            vmem((8, H), f32),
            vmem((4, 8, H), f32),
            vmem((2, 8, C), f32),
            vmem((2, 8, C), f32),
            vmem((2, 8, H), f32),
            vmem((2, 8, H), f32),
            vmem((F, M, H), f32),
            vmem((F, M, H), f32),
            vmem((F, 5, 2, R + 16, H), f32),
            vmem((2, R, C), f32),
            pltpu.SMEM((F,), f32),
            vmem((BATCHES, count), jnp.int32),
            vmem((BATCHES * count // H, H), jnp.int32),
            vmem((2, BATCHES, count), f32),
            vmem((BATCHES, M, count), f32),
            vmem((BATCHES, M + 8, H), f32),
            vmem((BATCHES, 8, H), jnp.int32),
            pltpu.SMEM((BATCHES, 8, H), jnp.int32),
            vmem((BATCHES, 8, H), f32),
            vmem((BATCHES, 16, 8, H), f32),
            dma((7,)),
            dma((CHANNELS,)),
            dma((CHANNELS,)),
            dma((BATCHES,)),
            dma((BATCHES,)),
        ],
        compiler_params=pltpu.CompilerParams(
            collective_id=0, has_side_effects=True, vmem_limit_bytes=48 * 1024 * 1024
        ),
        name="forecast_and_transform",
    )(*(pltpu.with_memory_space_constraint(a, pltpu.HBM) for a in operands))
    return pl.pallas_call(
        analysis_kernel,
        out_shape=jax.ShapeDtypeStruct((F, M, R, C), f32),
        in_specs=[pl.BlockSpec(memory_space=pltpu.VMEM)] * 2,
        out_specs=any_space,
        scratch_shapes=[
            vmem((F, R, M, C), f32),
            dma,
        ],
        compiler_params=pltpu.CompilerParams(vmem_limit_bytes=48 * 1024 * 1024),
        name="analysis",
    )(*(pltpu.with_memory_space_constraint(a, pltpu.VMEM) for a in (combined, forecast)))


def solution(mesh):
    in_specs = (
        P(None, None, "lat", "lon"),
        P("lat", "lon"),
        P("lat", "lon"),
        P(),
        P(),
        P(),
        P(),
        P(),
        P("lat", "lon", None, None),
    )
    out_specs = P(None, None, "lat", "lon")
    return jax.shard_map(local, mesh=mesh, in_specs=in_specs, out_specs=out_specs, check_vma=False)
```

```python
import jax
import jax.numpy as jnp
from jax import lax
from jax.experimental import pallas as pl
from jax.experimental.pallas import tpu as pltpu
from jax.sharding import PartitionSpec as P

MESH = pl.DeviceIdType.MESH
HI = lax.Precision.HIGHEST
F, M, R, C = 2, 32, 32, 256
H = 128
SLOTS = 16
BATCHES = 2
GROUP = 16
REACH = tuple(sorted(((di, dj) for di in (-1, 0, 1) for dj in range(-2, 3) if (di, dj) != (0, 0)), key=lambda d: -abs(d[0]) * 3 - abs(d[1])))
ADJACENT = tuple(d for d in REACH if abs(d[1]) < 2)
ROWS, COLS, CORNER, CROWS, CCOLS, NEAR = 0, 2, 4, 5, 6, 7
CHANNELS = 8


def iota(shape, axis):
    return lax.broadcasted_iota(jnp.int32, shape, axis)


def dot(a, b):
    return lax.dot_general(a, b, (((1,), (0,)), ((), ())), precision=HI, preferred_element_type=jnp.float32)


def dot_t(a, b):
    return lax.dot_general(a, b, (((1,), (1,)), ((), ())), precision=HI, preferred_element_type=jnp.float32)


def eliminate(system):
    parts = [system[8 * g : 8 * g + 8] for g in range(4)]
    sub = iota((8, H), 0)
    for own in range(4):
        lanes = range(8 * own, 8 * own + 8)
        columns = [[jnp.broadcast_to(part[:, k : k + 1], (8, H)) for part in parts] for k in lanes]
        pivots = [[jnp.broadcast_to(columns[j][own][i : i + 1], (8, H)) for j in range(8)] for i in range(8)]
        rows = [jnp.broadcast_to(parts[own][i : i + 1], (8, H)) for i in range(8)]
        for p in range(8):
            inverse = 1.0 / pivots[p][p]
            rows[p] = rows[p] * inverse
            for j in range(p + 1, 8):
                pivots[p][j] = pivots[p][j] * inverse
            for i in range(8):
                if i != p:
                    factor = pivots[i][p]
                    rows[i] = rows[i] - factor * rows[p]
                    for j in range(p + 1, 8):
                        pivots[i][j] = pivots[i][j] - factor * pivots[p][j]
        new = []
        for g in range(4):
            terms = [columns[j][g] * rows[j] for j in range(8)]
            while len(terms) > 1:
                terms = [terms[n] + terms[n + 1] for n in range(0, len(terms), 2)]
            new.append(parts[g] - terms[0])
        for i in range(8):
            new[own] = jnp.where(sub == i, rows[i], new[own])
        parts = new
    return jnp.concatenate(parts, axis=0)


def forecast_kernel(
    ens, cx_in, cy_in, diff_in, cell_in, value_in, noise_in, var_in,
    x2, e_out,
    halves, q, x1, own_w, own_e, far, next_w, next_e, corner_s, corner_r, corner_t, near_s, near_r, crow_s, crow_r, ccol_s, ccol_r,
    fix_w, fix_e, coef, courant, diff, cell, cell16, value, noise, picks, id_v, id_s, msg, got,
    in_sem, p1_send, p1_recv, p2_send, p2_recv,
):
    la, lo = lax.axis_size("lat"), lax.axis_size("lon")
    me_i, me_j = lax.axis_index("lat"), lax.axis_index("lon")

    def at(di, dj):
        return (lax.rem(me_i + (di + la), la), lax.rem(me_j + (dj + lo), lo))

    barrier = pltpu.get_barrier_semaphore()
    for di, dj in ADJACENT:
        pl.semaphore_signal(barrier, inc=1, device_id=at(di, dj), device_id_type=MESH)

    def load(src, dst, sem):
        copy = pltpu.make_async_copy(src, dst, in_sem.at[sem])
        copy.start()
        return copy

    def loaded(dst, sem):
        pltpu.make_async_copy(dst, dst, in_sem.at[sem]).wait()

    cell_copy = load(cell_in, cell, 3)
    load(cx_in, courant.at[0], 1)
    load(cy_in, courant.at[1], 1)
    for f in range(F):
        for h in range(2):
            load(ens.at[f, :, pl.ds(h * H, H)], halves.at[h, f], 0)
    diff_copy = load(diff_in, diff, 2)
    load(value_in, value.at[0], 4)
    load(var_in, value.at[1], 4)
    noise_copy = load(noise_in, noise, 5)

    lane = iota((M, H), 1)
    lane8 = iota((8, H), 1)
    def send(channel, src, dst, target):
        copy = pltpu.make_async_remote_copy(
            src_ref=src, dst_ref=dst, send_sem=p1_send.at[channel], recv_sem=p1_recv.at[channel],
            device_id=target, device_id_type=MESH,
        )
        copy.start()

    def sent(src, channel):
        pltpu.make_async_copy(src, src, p1_send.at[channel]).wait()

    def came(dst, channel):
        pltpu.make_async_copy(dst, dst, p1_recv.at[channel]).wait()

    count = cell.shape[1]
    chunks = count // H
    wide = lo * C
    shift = wide.bit_length() - 1
    n_rows = BATCHES * chunks
    cell_copy.wait()
    for ch in range(chunks):
        cell16[BATCHES * ch : BATCHES * (ch + 1), :] = cell[:, ch * H : (ch + 1) * H]
    cells = cell16[...]
    l_col = (cells & (wide - 1)) - me_j * C
    tiles = (0, 1, -1)
    masks, codes = [], []
    for di in tiles:
        l_row = lax.shift_right_logical(cells, shift) - lax.rem(me_i + (di + la), la) * R
        mine = (l_row >= 0) & (l_row < R) & (l_col >= 0) & (l_col < C)
        masks.append(jnp.where(mine, 1.0, 0.0))
        codes.append(jnp.where(mine, l_row * C + l_col, 0).astype(jnp.float32))
    mask = jnp.concatenate(masks, axis=0)
    all_rows = len(tiles) * n_rows
    before = jnp.where(iota((H, H), 0) < iota((H, H), 1), 1.0, 0.0)
    ii, jj = iota((all_rows, all_rows), 0), iota((all_rows, all_rows), 1)
    related = (lax.rem(ii, BATCHES) == lax.rem(jj, BATCHES)) & (lax.div(ii, n_rows) == lax.div(jj, n_rows))
    rows_before = jnp.where(related & (jj < ii), 1.0, 0.0)
    totals = jnp.broadcast_to(jnp.sum(mask, axis=1, keepdims=True), (all_rows, H))
    rank = dot(mask, before) + dot(rows_before, totals)
    rank = jnp.where(mask > 0.5, rank, -1.0).astype(jnp.int32)
    slot = iota((SLOTS, H), 0)
    slot_lane = iota((SLOTS, H), 1)
    slot_wide = iota((SLOTS, C), 1)
    chosen, own_code, columns = [], [], []
    for n, di in enumerate(tiles):
        for b in range(BATCHES):
            rows_b = [BATCHES * ch + b for ch in range(chunks)]
            picked = [jnp.broadcast_to(rank[n * n_rows + k : n * n_rows + k + 1, :], (SLOTS, H)) == slot for k in rows_b]
            total = jnp.zeros((SLOTS, H), jnp.float32)
            for here, k in zip(picked, rows_b):
                total = jnp.where(here, jnp.broadcast_to(codes[n][k : k + 1, :], (SLOTS, H)), total)
            code_b = jnp.sum(total, axis=1, keepdims=True).astype(jnp.int32)
            columns.append(jnp.broadcast_to(code_b & (C - 1), (SLOTS, C)))
            if di == 0:
                chosen.append(jnp.concatenate([jnp.where(here, 1.0, 0.0) for here in picked], axis=1))
                own_code.append(jnp.concatenate([codes[n][k : k + 1, :] for k in rows_b], axis=1))

    def hot(n, b, by=0):
        return jnp.where(slot_wide == columns[BATCHES * n + b] + by, 1.0, 0.0)

    loaded(courant, 1)
    diff_copy.wait()
    cxv, cyv = courant[0], courant[1]
    for side, row in ((0, R - 1), (1, 0)):
        crow_s[side, 0:1, :] = cxv[row : row + 1, :]
        crow_s[side, 1:2, :] = cyv[row : row + 1, :]
    spot = (lax.shift_right_logical(lane, 1) == iota((R, H), 0)) & (lane < 2 * R)
    even = (lane & 1) == 0
    for side, col in ((0, C - 2), (1, 0)):
        for n, source in enumerate((cxv, cyv)):
            pair = [jnp.broadcast_to(source[:, col + c : col + c + 1], (R, H)) for c in range(2)]
            spread = jnp.where(spot, jnp.where(even, pair[0], pair[1]), 0.0)
            ccol_s[side, n : n + 1, :] = jnp.sum(spread, axis=0, keepdims=True)

    loaded(halves, 0)

    def corner_lanes(f):
        cells = [
            halves[0, f, pl.ds(0, M, stride=R), :],
            pltpu.roll(halves[1, f, pl.ds(0, M, stride=R), :], 2, 1),
            pltpu.roll(halves[0, f, pl.ds(R - 1, M, stride=R), :], 2, 1),
            pltpu.roll(halves[1, f, pl.ds(R - 1, M, stride=R), :], 4, 1),
        ]
        out = jnp.where(lane == 3, cells[3], 0.0)
        for n in range(3):
            out = jnp.where(lane == n, cells[n], out)
        return out

    fill = jnp.zeros((H - F * M, H), jnp.float32)
    corner_s[...] = jnp.concatenate([corner_lanes(0), corner_lanes(1), fill], axis=0).T[0:8]

    def pack(f):
        def body(r, carry):
            west, east = carry
            c0 = halves[0, f, pl.ds(r, M, stride=R), :]
            c1 = halves[1, f, pl.ds(r, M, stride=R), :]
            q[f, r + 2, :, 0:H] = c0
            q[f, r + 2, :, H:C] = c1
            here = lax.shift_right_logical(lane, 1) == r
            west = jnp.where(here, pltpu.roll(c0, 2 * r, 1), west)
            east = jnp.where(here, pltpu.roll(c1, lax.rem(2 * r + 2, H), 1), east)
            return west, east

        zero = jnp.zeros((M, H), jnp.float32)
        west, east = lax.fori_loop(0, R, body, (zero, zero), unroll=8)
        own_w[f] = west
        own_e[f] = east

    def send_field(f):
        send(COLS + f, own_e.at[f], far.at[f, 0], at(0, 1))
        send(COLS + f, own_w.at[f], far.at[f, 1], at(0, -1))

    def send_rows(f):
        send(ROWS + f, q.at[f, pl.ds(R, 2)], q.at[f, pl.ds(0, 2)], at(1, 0))
        send(ROWS + f, q.at[f, pl.ds(2, 2)], q.at[f, pl.ds(R + 2, 2)], at(-1, 0))

    pack(0)
    pack(1)
    none = jnp.zeros((2 * M, C), jnp.float32)
    for side, (outer, inner_row) in enumerate(((R + 1, R), (2, 3))):
        out = jnp.zeros((M, H), jnp.float32)
        for b in range(BATCHES):
            spots = jnp.concatenate([hot(side + 1, b, by) for by in (-1, 0, 1, 0)], axis=0)
            spots = jnp.concatenate([spots, none] if b == 0 else [none, spots], axis=0)
            both = dot_t(jnp.concatenate([q[b % F, outer], q[b % F, inner_row]], axis=0), spots)
            out = out + jnp.where((lane & 63) < 48, both[0:M], both[M : 2 * M])
        near_s[side] = out
    pl.semaphore_wait(barrier, len(ADJACENT))
    for n, target in enumerate(((1, 1), (1, -1), (-1, 1), (-1, -1))):
        send(CORNER, corner_s, corner_r.at[n], at(*target))
    send(NEAR, near_s.at[0], near_r.at[0], at(1, 0))
    send(NEAR, near_s.at[1], near_r.at[1], at(-1, 0))
    send(CROWS, crow_s.at[0], crow_r.at[0], at(1, 0))
    send(CROWS, crow_s.at[1], crow_r.at[1], at(-1, 0))
    send(CCOLS, ccol_s.at[0], ccol_r.at[0], at(0, 1))
    send(CCOLS, ccol_s.at[1], ccol_r.at[1], at(0, -1))
    send_field(0)
    send_field(1)

    loaded(value, 4)
    noise_copy.wait()
    picks[...] = jnp.zeros((BATCHES, M + 8, H), jnp.float32)
    sub_wide = iota((8, count), 0)
    for b in range(BATCHES):
        more = jnp.where(sub_wide == 0, jnp.broadcast_to(value[0, b : b + 1, :], (8, count)), 0.0)
        more = jnp.where(sub_wide == 1, jnp.broadcast_to(value[1, b : b + 1, :], (8, count)), more)
        more = jnp.where(sub_wide == 2, jnp.broadcast_to(own_code[b], (8, count)), more)
        picks[b, :, 0:SLOTS] = dot_t(jnp.concatenate([noise[b], more], axis=0), chosen[b])
        id_v[b] = (picks[b, M : M + 8, :] + 0.5).astype(jnp.int32)
    id_copy = load(id_v, id_s, 6)

    def parts_of(x, y):
        return jnp.maximum(x, 0.0), -jnp.minimum(x, 0.0), jnp.maximum(y, 0.0), -jnp.minimum(y, 0.0)

    rates = [diff[f] for f in range(F)]
    low_edge, high_edge = me_i == 0, me_i == la - 1

    def centre_of(p, k):
        return 1.0 - p[0] - p[1] - p[2] - p[3] - 4.0 * k

    own_parts = parts_of(cxv, cyv)
    row_id = iota((R, C), 0)

    def set_coef(f, first, values):
        for n in range(5):
            for h in range(2):
                v = values[n][:, h * H : (h + 1) * H]
                coef[f, n, h, first : first + max(8, v.shape[0]), :] = jnp.broadcast_to(v, (max(8, v.shape[0]), H))

    for f in range(F):
        south = jnp.where((row_id == 0) & low_edge, 0.0, own_parts[2] + rates[f])
        north = jnp.where((row_id == R - 1) & high_edge, 0.0, own_parts[3] + rates[f])
        set_coef(f, 8, [centre_of(own_parts, rates[f]), own_parts[0] + rates[f], own_parts[1] + rates[f], south, north])

    def row_step(src, dst, f, r, src_at, dst_at, far, south=True, north=True):
        first, last = lane == 0, lane == H - 1
        if far is None:
            hw = he = jnp.zeros((M, H), jnp.float32)
        else:
            turn = (H - 1 - 2 * r) & (H - 1)
            hw, he = pltpu.roll(far[0], turn, 1), pltpu.roll(far[1], turn, 1)
        c0, c1 = src[f, r + src_at, :, 0:H], src[f, r + src_at, :, H:C]
        w0, w1 = pltpu.roll(c0, 1, 1), pltpu.roll(c1, 1, 1)
        e0, e1 = pltpu.roll(c0, H - 1, 1), pltpu.roll(c1, H - 1, 1)
        w0, w1 = jnp.where(first, hw, w0), jnp.where(first, w0, w1)
        e0, e1 = jnp.where(last, e1, e0), jnp.where(last, he, e1)
        for h, (c, w, e) in enumerate(((c0, w0, e0), (c1, w1, e1))):
            cut = slice(h * H, (h + 1) * H)
            rate = [coef[f, n, h, pl.ds(r + 8, 1), :] for n in range(5)]
            out = rate[0] * c + rate[1] * w + rate[2] * e
            if south:
                out = out + rate[3] * src[f, r + src_at - 1, :, cut]
            if north:
                out = out + rate[4] * src[f, r + src_at + 1, :, cut]
            dst[f, r + dst_at, :, cut] = out

    def step_one(f, r):
        row_step(q, x1, f, r, 2, 1, (far[f, 0], far[f, 1]))

    def rows_of(step, begin, end):
        def body(r, carry):
            step(r)
            return carry

        lax.fori_loop(begin, end, body, 0, unroll=2)

    def inner(f, src, dst, src_at, dst_at):
        row_step(src, dst, f, 0, src_at, dst_at, None, south=False)
        rows_of(lambda r: row_step(src, dst, f, r, src_at, dst_at, None), 1, R - 1)
        row_step(src, dst, f, R - 1, src_at, dst_at, None, north=False)

    inner(0, q, x1, 2, 1)
    send_rows(0)
    inner(0, x1, x2, 1, 0)
    send_rows(1)
    id_copy.wait()
    ids = [[id_s[b, 2, s] for s in range(SLOTS)] for b in range(BATCHES)]

    came(crow_r, CROWS)
    came(ccol_r, CCOLS)
    halo_rows = [parts_of(crow_r[side, 0:1, :], crow_r[side, 1:2, :]) for side in range(2)]
    for f in range(F):
        for side, first in ((0, 0), (1, 8 + R)):
            p = halo_rows[side]
            set_coef(f, first, [centre_of(p, rates[f])] + [part + rates[f] for part in p])

    def near_weights(b):
        f = b % F

        def row_of(n, r):
            return jnp.concatenate([coef[f, n, h, r + 8 : r + 9, :] for h in range(2)], axis=1)

        at_first, at_last = iota((1, C), 1) == 0, iota((1, C), 1) == C - 1
        rows = []
        for n, back, row, halo, inner_row in ((3, 4, 0, -1, 1), (4, 3, R - 1, R, R - 2)):
            edge = row_of(n, row)
            from_w = jnp.where(at_first, 0.0, pltpu.roll(edge, 1, 1))
            from_e = jnp.where(at_last, 0.0, pltpu.roll(edge, C - 1, 1))
            rows += [
                edge * row_of(1, halo) + row_of(1, row) * from_w,
                edge * row_of(0, halo) + row_of(0, row) * edge,
                edge * row_of(2, halo) + row_of(2, row) * from_e,
                edge * row_of(n, halo),
                edge * row_of(back, halo),
                row_of(n, inner_row) * edge,
            ]
        pad = jnp.zeros((H - SLOTS, C), jnp.float32)
        spots = jnp.concatenate([hot(0, b), pad], axis=0)
        sub = iota((16, C), 0)
        stacked = jnp.zeros((16, C), jnp.float32)
        for k, row in enumerate(rows):
            stacked = jnp.where(sub == k, jnp.broadcast_to(row, (16, C)), stacked)
        weights = dot_t(stacked, spots)
        own = dot_t(jnp.concatenate([q[f, 2], q[f, R + 1]], axis=0), spots)
        code_row = id_v[b, 2:3, :]
        at_row = lax.shift_right_logical(code_row, 8) & (R - 1)
        out = []
        for side, (row, inner_row) in enumerate(((0, 1), (R - 1, R - 2))):
            w = [weights[6 * side + k : 6 * side + k + 1, :] for k in range(6)]
            w = [jnp.where(at_row == row, v, 0.0) for v in w[:5]] + [jnp.where(at_row == inner_row, w[5], 0.0)]
            out.append((w[0], w[1] + w[5], w[2], w[3], w[4] * own[side * M : (side + 1) * M]))
        return out

    lane_row = iota((1, H), 1)

    def packed_rates(f, ref, side):
        p = parts_of(ref[side, 0:1, :], ref[side, 1:2, :])
        south = jnp.where((lane_row < 2) & low_edge, 0.0, p[2] + rates[f])
        north = jnp.where((lane_row >= 2 * R - 2) & high_edge, 0.0, p[3] + rates[f])
        return centre_of(p, rates[f]), p[0] + rates[f], p[1] + rates[f], south, north

    def halo_columns(f):
        came(far.at[f], COLS + f)
        west, east = far[f, 0], far[f, 1]
        sides = (
            (next_w, west, pltpu.roll(west, 1, 1), pltpu.roll(own_w[f], 1, 1)),
            (next_e, east, pltpu.roll(own_e[f], H - 1, 1), pltpu.roll(east, H - 1, 1)),
        )
        for side, (to, c, w, e) in enumerate(sides):
            rate = packed_rates(f, ccol_r, side)
            out = rate[0] * c + rate[1] * w + rate[2] * e
            out = out + rate[3] * pltpu.roll(c, 2, 1) + rate[4] * pltpu.roll(c, H - 2, 1)
            to[f] = jnp.where(lane < 2 * R, out, 0.0)

    def corner_rates(f):
        halo_w, halo_e = packed_rates(f, ccol_r, 0), packed_rates(f, ccol_r, 1)
        west, east = packed_rates(f, ccol_s, 1)[1], packed_rates(f, ccol_s, 0)[2]
        w = west * pltpu.roll(jnp.where(lane_row < R, halo_w[3], halo_w[4]), H - 1, 1)
        e = east * pltpu.roll(jnp.where(lane_row < R, halo_e[3], halo_e[4]), 1, 1)
        w = jnp.where((lane_row == 0) | (lane_row == 2 * R - 2), w, 0.0)
        e = jnp.where((lane_row == 1) | (lane_row == 2 * R - 1), e, 0.0)
        return w, e

    near = [near_weights(b) for b in range(BATCHES)]
    beyond = [corner_rates(f) for f in range(F)]

    def corner_weights(b):
        code_row = id_v[b, 2:3, :]
        at_row, at_col = lax.shift_right_logical(code_row, 8) & (R - 1), code_row & (C - 1)
        west, east = beyond[b % F]
        out = []
        for side, (row, at) in enumerate(((0, 0), (R - 1, 2 * R - 2))):
            w = near[b][side]
            through_w, through_e = west[:, at : at + 1], east[:, at + 1 : at + 2]
            out.append(jnp.where(at_col == 0, w[0] + jnp.where(at_row == row, through_w, 0.0), 0.0))
            out.append(jnp.where(at_col == C - 1, w[2] + jnp.where(at_row == row, through_e, 0.0), 0.0))
        return out

    corner_part = [corner_weights(b) for b in range(BATCHES)]

    def corner_columns(f):
        turned = corner_t[...]
        return [jnp.broadcast_to(turned[f * M : (f + 1) * M, n : n + 1], (M, H)) for n in (3, 10, 17, 24)]

    def late_corners(f):
        south_w, south_e, north_w, north_e = corner_columns(f)
        far[f, 0] = jnp.where(lane == H - 1, south_w, jnp.where(lane == 2 * R + 1, north_w, far[f, 0]))
        far[f, 1] = jnp.where(lane == H - 2, south_e, jnp.where(lane == 2 * R, north_e, far[f, 1]))
        west, east = beyond[f]
        fix_w[f] = fix_w[f] + west * jnp.where(lane < R, south_w, north_w)
        fix_e[f] = fix_e[f] + east * jnp.where(lane < R, south_e, north_e)

    def fix_columns(f):
        inside = lane < 2 * R
        for side, to, outside, new, outer, turn in (
            (1, fix_w, far[f, 0], next_w, even, H - 1),
            (0, fix_e, far[f, 1], next_e, ~even, 1),
        ):
            rate = packed_rates(f, ccol_s, side)
            beside = rate[1] if side == 1 else rate[2]
            u = jnp.where(inside & outer, beside * pltpu.roll(outside, turn, 1), 0.0)
            near = beside * pltpu.roll(new[f], turn, 1) + rate[0] * u
            near = near + rate[3] * pltpu.roll(u, 2, 1) + rate[4] * pltpu.roll(u, H - 2, 1)
            to[f] = jnp.where(inside, jnp.where(outer, near, beside * pltpu.roll(u, H - turn, 1)), 0.0)

    def fix_rows(f):
        came(q.at[f, pl.ds(0, 4)], ROWS + f)
        first, last = lane == 0, lane == H - 1
        for halo, q_at, x_at, n, row, inner_row in ((-1, 1, 0, 3, 0, 1), (R, R + 2, R + 1, 4, R - 1, R - 2)):
            step_one(f, halo)
            rate = [[coef[f, k, h, row + 8 : row + 9, :] for k in range(5)] for h in range(2)]
            t = [rate[h][n] * q[f, q_at, :, h * H : (h + 1) * H] for h in range(2)]
            w = [pltpu.roll(v, 1, 1) for v in t]
            e = [pltpu.roll(v, H - 1, 1) for v in t]
            w = [jnp.where(first, 0.0, w[0]), jnp.where(first, w[0], w[1])]
            e = [jnp.where(last, e[1], e[0]), jnp.where(last, 0.0, e[1])]
            for h in range(2):
                cut = slice(h * H, (h + 1) * H)
                add = rate[h][n] * x1[f, x_at, :, cut] + rate[h][0] * t[h] + rate[h][1] * w[h] + rate[h][2] * e[h]
                x2[f, row, :, cut] = x2[f, row, :, cut] + add
                x2[f, inner_row, :, cut] = (
                    x2[f, inner_row, :, cut] + coef[f, n, h, inner_row + 8 : inner_row + 9, :] * t[h]
                )

    def near_rows(b):
        total = jnp.zeros((M, H), jnp.float32)
        for side in range(2):
            got_rows = near_r[side]
            g = [pltpu.roll(got_rows, (2 * H - 64 * b - SLOTS * k) % H, 1) for k in range(4)]
            w = near[b][side]
            total = total + w[0] * g[0] + w[1] * g[1] + w[2] * g[2] + w[3] * g[3] + w[4]
        return total

    def unpack_columns(f):
        def body(r):
            west = pltpu.roll(fix_w[f], (H - 2 * r) & (H - 1), 1)
            east = pltpu.roll(fix_e[f], (H - 2 - 2 * r) & (H - 1), 1)
            x2[f, r, :, 0:H] = x2[f, r, :, 0:H] + jnp.where(lane < 2, west, 0.0)
            x2[f, r, :, H:C] = x2[f, r, :, H:C] + jnp.where(lane >= H - 2, east, 0.0)

        rows_of(body, 0, R)

    def see(b):
        f = b % F
        seen = jnp.zeros((M, H), jnp.float32)
        for s in range(SLOTS):
            code_s = ids[b][s]
            at_row = lax.shift_right_logical(code_s, 8) & (R - 1)
            col = code_s & (C - 1)
            row = x2[f, at_row]
            picked = jnp.where(lane == col, row[:, 0:H], 0.0) + jnp.where(lane + H == col, row[:, H:C], 0.0)
            spot_w = jnp.where(col < 2, 2 * at_row + col, -1)
            spot_e = jnp.where(col >= C - 2, 2 * at_row + col - (C - 2), -1)
            picked = picked + jnp.where(lane == spot_w, fix_w[f], 0.0) + jnp.where(lane == spot_e, fix_e[f], 0.0)
            seen = jnp.where(lane == s, jnp.broadcast_to(jnp.sum(picked, axis=1, keepdims=True), (M, H)), seen)
        return seen

    def observe(b, seen):
        for weight, column in zip(corner_part[b], corner_columns(b % F)):
            seen = seen + weight * column
        mean = jnp.sum(seen, axis=0, keepdims=True) * (1.0 / M)
        var_b = picks[b, M + 1 : M + 2, :]
        there = var_b > 0.0
        scale = jnp.where(there, jnp.sqrt(1.0 / jnp.where(there, var_b, 1.0)), 0.0)
        innovation = picks[b, M : M + 1, :] + picks[b, 0:M, :] - seen
        stacked = jnp.concatenate([scale * (seen - mean), scale * innovation, fill], axis=0)
        return stacked.T[0:SLOTS]

    def tell(b, r):
        packed = r[0:8] + pltpu.roll(r[8:16], 2 * M, 1)
        msg[b] = packed
        got[b, 14] = packed
        got[b, 15] = jnp.zeros((8, H), jnp.float32)
        for n, (di, dj) in enumerate(REACH):
            pltpu.make_async_remote_copy(
                src_ref=msg.at[b], dst_ref=got.at[b, n], send_sem=p2_send.at[b], recv_sem=p2_recv.at[b],
                device_id=at(-di, -dj), device_id_type=MESH,
            ).start()

    def transform(b):
        others = got.at[b, pl.ds(0, len(REACH))]
        pltpu.make_async_copy(others, others, p2_recv.at[b]).wait()
        stack = got[b].reshape(16 * 8, H)
        place = lax.shift_right_logical(iota((16 * 8, H), 0), 3)
        keep = jnp.ones((16 * 8, H), jnp.float32)
        for n, (di, dj) in enumerate(REACH):
            if di != 0:
                keep = jnp.where((low_edge if di < 0 else high_edge) & (place == n), 0.0, keep)
        stack = stack * keep
        turned = stack.T
        gram = dot(jnp.concatenate([turned[0:M], turned[2 * M : 3 * M]], axis=0), stack)
        both = gram[0:M] + pltpu.roll(gram[M : 2 * M], 2 * M, 1)
        system = jnp.where(lane < 2 * M, both, 0.0) + jnp.where(lane == iota((M, H), 0), M - 1.0, 0.0)
        return eliminate(system)

    def centered_rows(solved):
        w = jnp.where(lane < M, pltpu.roll(solved, H - M, 1), 0.0)
        return w - jnp.sum(w, axis=0, keepdims=True) * (1.0 / M)

    halo_columns(0)
    fix_columns(0)
    seen0 = see(0)
    came(near_r, NEAR)
    seen0 = seen0 + near_rows(0)
    came(corner_r, CORNER)
    corner_t[...] = jnp.concatenate([corner_r[n] for n in range(4)] + [jnp.zeros((H - 32, H), jnp.float32)], axis=0).T
    tell(0, observe(0, seen0))
    inner(1, q, x1, 2, 1)
    inner(1, x1, x2, 1, 0)
    halo_columns(1)
    fix_columns(1)
    r1 = observe(1, see(1) + near_rows(1))
    solved0 = transform(0)
    w0 = jnp.where(lane < M, pltpu.roll(solved0, H - M, 1), 0.0)
    w0_mean = jnp.sum(w0, axis=1, keepdims=True) * (1.0 / M)
    both0 = jnp.where(lane < M, w0 - w0_mean, jnp.where(lane < 2 * M, -solved0, 0.0))
    tell(1, r1 + dot(r1[:, 0:M], both0))
    c0 = centered_rows(solved0)
    late_corners(0)
    late_corners(1)
    unpack_columns(0)
    unpack_columns(1)
    fix_rows(0)
    fix_rows(1)
    sent(near_s, NEAR)
    for f in range(F):
        sent(q.at[f, pl.ds(2, 4)], ROWS + f)
        sent(far.at[f], COLS + f)
    sent(corner_r, CORNER)
    sent(crow_s, CROWS)
    sent(ccol_s, CCOLS)
    solved1 = transform(1)
    c1 = centered_rows(solved1)
    e_out[...] = c0 + c1 + dot(c0[:, 0:M], c1)
    for b in range(BATCHES):
        others = got.at[b, pl.ds(0, len(REACH))]
        pltpu.make_async_copy(others, others, p2_send.at[b]).wait()


def analysis_kernel(e_ref, x, out, y, out_sem):
    groups = [(f, r) for f in range(F) for r in range(0, R, GROUP)]
    e = jnp.concatenate([e_ref[...], jnp.zeros((H - M, H), jnp.float32)], axis=0).T[0:M, 0:M]
    e_hi = e.astype(jnp.bfloat16)
    e_lo = (e - e_hi.astype(jnp.float32)).astype(jnp.bfloat16)
    left = jnp.concatenate([e_hi, e_hi, e_lo], axis=1)
    for f, r in groups:
        for row in range(r, r + GROUP):
            v = x[f, row]
            hi = v.astype(jnp.bfloat16)
            low = (v - hi.astype(jnp.float32)).astype(jnp.bfloat16)
            right = jnp.concatenate([hi, low, hi], axis=0)
            add = lax.dot_general(left, right, (((1,), (0,)), ((), ())), preferred_element_type=jnp.float32)
            y[f, row] = v + add
        for row in range(r, r + GROUP):
            pltpu.make_async_copy(y.at[f, row], out.at[f, :, row, :], out_sem).start()
    pltpu.make_async_copy(y, y, out_sem).wait()


def local(ensemble, courant_x, courant_y, diffusion, obs_cell, obs_value, obs_noise, obs_var, loc_mask):
    any_space = pl.BlockSpec(memory_space=pl.ANY)
    f32 = jnp.float32
    count = obs_cell.shape[1]
    vmem = pltpu.VMEM
    dma = pltpu.SemaphoreType.DMA
    noise_turned = obs_noise.swapaxes(1, 2)
    operands = (
        ensemble.reshape(F, M * R, C), courant_x, courant_y, diffusion, obs_cell, obs_value, noise_turned, obs_var
    )
    forecast, combined = pl.pallas_call(
        forecast_kernel,
        out_shape=(vmem((F, R, M, C), f32), vmem((M, H), f32)),
        in_specs=[pl.BlockSpec(memory_space=pltpu.HBM)] * 8,
        out_specs=(pl.BlockSpec(memory_space=pltpu.VMEM), pl.BlockSpec(memory_space=pltpu.VMEM)),
        scratch_shapes=[
            vmem((2, F, M * R, H), f32),
            vmem((F, R + 4, M, C), f32),
            vmem((F, R + 2, M, C), f32),
            vmem((F, M, H), f32),
            vmem((F, M, H), f32),
            vmem((F, 2, M, H), f32),
            vmem((F, M, H), f32),
            vmem((F, M, H), f32),
            vmem((8, H), f32),
            vmem((4, 8, H), f32),
            vmem((H, H), f32),
            vmem((2, M, H), f32),
            vmem((2, M, H), f32),
            vmem((2, 8, C), f32),
            vmem((2, 8, C), f32),
            vmem((2, 8, H), f32),
            vmem((2, 8, H), f32),
            vmem((F, M, H), f32),
            vmem((F, M, H), f32),
            vmem((F, 5, 2, R + 16, H), f32),
            vmem((2, R, C), f32),
            pltpu.SMEM((F,), f32),
            vmem((BATCHES, count), jnp.int32),
            vmem((BATCHES * count // H, H), jnp.int32),
            vmem((2, BATCHES, count), f32),
            vmem((BATCHES, M, count), f32),
            vmem((BATCHES, M + 8, H), f32),
            vmem((BATCHES, 8, H), jnp.int32),
            pltpu.SMEM((BATCHES, 8, H), jnp.int32),
            vmem((BATCHES, 8, H), f32),
            vmem((BATCHES, 16, 8, H), f32),
            dma((7,)),
            dma((CHANNELS,)),
            dma((CHANNELS,)),
            dma((BATCHES,)),
            dma((BATCHES,)),
        ],
        compiler_params=pltpu.CompilerParams(
            collective_id=0, has_side_effects=True, vmem_limit_bytes=48 * 1024 * 1024
        ),
        name="forecast_and_transform",
    )(*(pltpu.with_memory_space_constraint(a, pltpu.HBM) for a in operands))
    return pl.pallas_call(
        analysis_kernel,
        out_shape=jax.ShapeDtypeStruct((F, M, R, C), f32),
        in_specs=[pl.BlockSpec(memory_space=pltpu.VMEM)] * 2,
        out_specs=any_space,
        scratch_shapes=[
            vmem((F, R, M, C), f32),
            dma,
        ],
        compiler_params=pltpu.CompilerParams(vmem_limit_bytes=48 * 1024 * 1024),
        name="analysis",
    )(*(pltpu.with_memory_space_constraint(a, pltpu.VMEM) for a in (combined, forecast)))


def solution(mesh):
    in_specs = (
        P(None, None, "lat", "lon"),
        P("lat", "lon"),
        P("lat", "lon"),
        P(),
        P(),
        P(),
        P(),
        P(),
        P("lat", "lon", None, None),
    )
    out_specs = P(None, None, "lat", "lon")
    return jax.shard_map(local, mesh=mesh, in_specs=in_specs, out_specs=out_specs, check_vma=False)
```

```python
import jax
import jax.numpy as jnp
from jax import lax
from jax.experimental import pallas as pl
from jax.experimental.pallas import tpu as pltpu
from jax.sharding import PartitionSpec as P

MESH = pl.DeviceIdType.MESH
HI = lax.Precision.HIGHEST
F, M, R, C = 2, 32, 32, 256
H = 128
SLOTS = 16
BATCHES = 2
GROUP = 32
REACH = tuple(sorted(((di, dj) for di in (-1, 0, 1) for dj in range(-2, 3) if (di, dj) != (0, 0)), key=lambda d: -abs(d[0]) * 3 - abs(d[1])))
ADJACENT = tuple(d for d in REACH if abs(d[1]) < 2)
ROWS, COLS, CORNER, CROWS, CCOLS, NEAR = 0, 2, 4, 5, 6, 7
CHANNELS = 8


def iota(shape, axis):
    return lax.broadcasted_iota(jnp.int32, shape, axis)


def dot(a, b):
    return lax.dot_general(a, b, (((1,), (0,)), ((), ())), precision=HI, preferred_element_type=jnp.float32)


def dot_t(a, b):
    return lax.dot_general(a, b, (((1,), (1,)), ((), ())), precision=HI, preferred_element_type=jnp.float32)


def eliminate(system):
    parts = [system[8 * g : 8 * g + 8] for g in range(4)]
    sub = iota((8, H), 0)
    for own in range(4):
        lanes = range(8 * own, 8 * own + 8)
        columns = [[jnp.broadcast_to(part[:, k : k + 1], (8, H)) for part in parts] for k in lanes]
        pivots = [[jnp.broadcast_to(columns[j][own][i : i + 1], (8, H)) for j in range(8)] for i in range(8)]
        rows = [jnp.broadcast_to(parts[own][i : i + 1], (8, H)) for i in range(8)]
        for p in range(8):
            inverse = 1.0 / pivots[p][p]
            rows[p] = rows[p] * inverse
            for j in range(p + 1, 8):
                pivots[p][j] = pivots[p][j] * inverse
            for i in range(8):
                if i != p:
                    factor = pivots[i][p]
                    rows[i] = rows[i] - factor * rows[p]
                    for j in range(p + 1, 8):
                        pivots[i][j] = pivots[i][j] - factor * pivots[p][j]
        new = []
        for g in range(4):
            terms = [columns[j][g] * rows[j] for j in range(8)]
            while len(terms) > 1:
                terms = [terms[n] + terms[n + 1] for n in range(0, len(terms), 2)]
            new.append(parts[g] - terms[0])
        for i in range(8):
            new[own] = jnp.where(sub == i, rows[i], new[own])
        parts = new
    return jnp.concatenate(parts, axis=0)


def forecast_kernel(
    ens, cx_in, cy_in, diff_in, cell_in, value_in, noise_in, var_in,
    x2, e_out,
    halves, q, x1, own_w, own_e, far, next_w, next_e, corner_s, corner_r, corner_t, near_s, near_r, crow_s, crow_r, ccol_s, ccol_r,
    fix_w, fix_e, coef, courant, diff, cell, cell16, value, noise, picks, id_v, id_s, msg, got,
    in_sem, p1_send, p1_recv, p2_send, p2_recv,
):
    la, lo = lax.axis_size("lat"), lax.axis_size("lon")
    me_i, me_j = lax.axis_index("lat"), lax.axis_index("lon")

    def at(di, dj):
        return (lax.rem(me_i + (di + la), la), lax.rem(me_j + (dj + lo), lo))

    barrier = pltpu.get_barrier_semaphore()
    for di, dj in ADJACENT:
        pl.semaphore_signal(barrier, inc=1, device_id=at(di, dj), device_id_type=MESH)

    def load(src, dst, sem):
        copy = pltpu.make_async_copy(src, dst, in_sem.at[sem])
        copy.start()
        return copy

    def loaded(dst, sem):
        pltpu.make_async_copy(dst, dst, in_sem.at[sem]).wait()

    cell_copy = load(cell_in, cell, 3)
    load(cx_in, courant.at[0], 1)
    load(cy_in, courant.at[1], 1)
    for f in range(F):
        for h in range(2):
            load(ens.at[f, :, pl.ds(h * H, H)], halves.at[h, f], 0)
    diff_copy = load(diff_in, diff, 2)
    load(value_in, value.at[0], 4)
    load(var_in, value.at[1], 4)
    noise_copy = load(noise_in, noise, 5)

    lane = iota((M, H), 1)
    lane8 = iota((8, H), 1)
    def send(channel, src, dst, target):
        copy = pltpu.make_async_remote_copy(
            src_ref=src, dst_ref=dst, send_sem=p1_send.at[channel], recv_sem=p1_recv.at[channel],
            device_id=target, device_id_type=MESH,
        )
        copy.start()

    def sent(src, channel):
        pltpu.make_async_copy(src, src, p1_send.at[channel]).wait()

    def came(dst, channel):
        pltpu.make_async_copy(dst, dst, p1_recv.at[channel]).wait()

    count = cell.shape[1]
    chunks = count // H
    wide = lo * C
    shift = wide.bit_length() - 1
    n_rows = BATCHES * chunks
    cell_copy.wait()
    for ch in range(chunks):
        cell16[BATCHES * ch : BATCHES * (ch + 1), :] = cell[:, ch * H : (ch + 1) * H]
    cells = cell16[...]
    l_col = (cells & (wide - 1)) - me_j * C
    tiles = (0, 1, -1)
    masks, codes = [], []
    for di in tiles:
        l_row = lax.shift_right_logical(cells, shift) - lax.rem(me_i + (di + la), la) * R
        mine = (l_row >= 0) & (l_row < R) & (l_col >= 0) & (l_col < C)
        masks.append(jnp.where(mine, 1.0, 0.0))
        codes.append(jnp.where(mine, l_row * C + l_col, 0).astype(jnp.float32))
    mask = jnp.concatenate(masks, axis=0)
    all_rows = len(tiles) * n_rows
    before = jnp.where(iota((H, H), 0) < iota((H, H), 1), 1.0, 0.0)
    ii, jj = iota((all_rows, all_rows), 0), iota((all_rows, all_rows), 1)
    related = (lax.rem(ii, BATCHES) == lax.rem(jj, BATCHES)) & (lax.div(ii, n_rows) == lax.div(jj, n_rows))
    rows_before = jnp.where(related & (jj < ii), 1.0, 0.0)
    totals = jnp.broadcast_to(jnp.sum(mask, axis=1, keepdims=True), (all_rows, H))
    rank = dot(mask, before) + dot(rows_before, totals)
    rank = jnp.where(mask > 0.5, rank, -1.0).astype(jnp.int32)
    slot = iota((SLOTS, H), 0)
    slot_lane = iota((SLOTS, H), 1)
    slot_wide = iota((SLOTS, C), 1)
    chosen, own_code, columns = [], [], []
    for n, di in enumerate(tiles):
        for b in range(BATCHES):
            rows_b = [BATCHES * ch + b for ch in range(chunks)]
            picked = [jnp.broadcast_to(rank[n * n_rows + k : n * n_rows + k + 1, :], (SLOTS, H)) == slot for k in rows_b]
            total = jnp.zeros((SLOTS, H), jnp.float32)
            for here, k in zip(picked, rows_b):
                total = jnp.where(here, jnp.broadcast_to(codes[n][k : k + 1, :], (SLOTS, H)), total)
            code_b = jnp.sum(total, axis=1, keepdims=True).astype(jnp.int32)
            columns.append(jnp.broadcast_to(code_b & (C - 1), (SLOTS, C)))
            if di == 0:
                chosen.append(jnp.concatenate([jnp.where(here, 1.0, 0.0) for here in picked], axis=1))
                own_code.append(jnp.concatenate([codes[n][k : k + 1, :] for k in rows_b], axis=1))

    def hot(n, b, by=0):
        return jnp.where(slot_wide == columns[BATCHES * n + b] + by, 1.0, 0.0)

    loaded(courant, 1)
    diff_copy.wait()
    cxv, cyv = courant[0], courant[1]
    for side, row in ((0, R - 1), (1, 0)):
        crow_s[side, 0:1, :] = cxv[row : row + 1, :]
        crow_s[side, 1:2, :] = cyv[row : row + 1, :]
    spot = (lax.shift_right_logical(lane, 1) == iota((R, H), 0)) & (lane < 2 * R)
    even = (lane & 1) == 0
    for side, col in ((0, C - 2), (1, 0)):
        for n, source in enumerate((cxv, cyv)):
            pair = [jnp.broadcast_to(source[:, col + c : col + c + 1], (R, H)) for c in range(2)]
            spread = jnp.where(spot, jnp.where(even, pair[0], pair[1]), 0.0)
            ccol_s[side, n : n + 1, :] = jnp.sum(spread, axis=0, keepdims=True)

    loaded(halves, 0)

    def corner_lanes(f):
        cells = [
            halves[0, f, pl.ds(0, M, stride=R), :],
            pltpu.roll(halves[1, f, pl.ds(0, M, stride=R), :], 2, 1),
            pltpu.roll(halves[0, f, pl.ds(R - 1, M, stride=R), :], 2, 1),
            pltpu.roll(halves[1, f, pl.ds(R - 1, M, stride=R), :], 4, 1),
        ]
        out = jnp.where(lane == 3, cells[3], 0.0)
        for n in range(3):
            out = jnp.where(lane == n, cells[n], out)
        return out

    fill = jnp.zeros((H - F * M, H), jnp.float32)
    corner_s[...] = jnp.concatenate([corner_lanes(0), corner_lanes(1), fill], axis=0).T[0:8]

    def pack(f):
        def body(r, carry):
            west, east = carry
            c0 = halves[0, f, pl.ds(r, M, stride=R), :]
            c1 = halves[1, f, pl.ds(r, M, stride=R), :]
            q[f, r + 2, :, 0:H] = c0
            q[f, r + 2, :, H:C] = c1
            here = lax.shift_right_logical(lane, 1) == r
            west = jnp.where(here, pltpu.roll(c0, 2 * r, 1), west)
            east = jnp.where(here, pltpu.roll(c1, lax.rem(2 * r + 2, H), 1), east)
            return west, east

        zero = jnp.zeros((M, H), jnp.float32)
        west, east = lax.fori_loop(0, R, body, (zero, zero), unroll=R)
        own_w[f] = west
        own_e[f] = east

    def send_field(f):
        send(COLS + f, own_e.at[f], far.at[f, 0], at(0, 1))
        send(COLS + f, own_w.at[f], far.at[f, 1], at(0, -1))

    def send_rows(f):
        send(ROWS + f, q.at[f, pl.ds(R, 2)], q.at[f, pl.ds(0, 2)], at(1, 0))
        send(ROWS + f, q.at[f, pl.ds(2, 2)], q.at[f, pl.ds(R + 2, 2)], at(-1, 0))

    pack(0)

    def edge_row(f, r):
        return jnp.concatenate([halves[h, f, pl.ds(r, M, stride=R), :] for h in range(2)], axis=1)

    none = jnp.zeros((2 * M, C), jnp.float32)
    for side, (outer, inner_row) in enumerate(((R - 1, R - 2), (0, 1))):
        out = jnp.zeros((M, H), jnp.float32)
        for b in range(BATCHES):
            spots = jnp.concatenate([hot(side + 1, b, by) for by in (-1, 0, 1, 0)], axis=0)
            spots = jnp.concatenate([spots, none] if b == 0 else [none, spots], axis=0)
            both = dot_t(jnp.concatenate([edge_row(b % F, outer), edge_row(b % F, inner_row)], axis=0), spots)
            out = out + jnp.where((lane & 63) < 48, both[0:M], both[M : 2 * M])
        near_s[side] = out
    pl.semaphore_wait(barrier, len(ADJACENT))
    for n, target in enumerate(((1, 1), (1, -1), (-1, 1), (-1, -1))):
        send(CORNER, corner_s, corner_r.at[n], at(*target))
    send(NEAR, near_s.at[0], near_r.at[0], at(1, 0))
    send(NEAR, near_s.at[1], near_r.at[1], at(-1, 0))
    send(CROWS, crow_s.at[0], crow_r.at[0], at(1, 0))
    send(CROWS, crow_s.at[1], crow_r.at[1], at(-1, 0))
    send(CCOLS, ccol_s.at[0], ccol_r.at[0], at(0, 1))
    send(CCOLS, ccol_s.at[1], ccol_r.at[1], at(0, -1))
    send_field(0)
    pack(1)
    send_field(1)

    loaded(value, 4)
    noise_copy.wait()
    picks[...] = jnp.zeros((BATCHES, M + 8, H), jnp.float32)
    sub_wide = iota((8, count), 0)
    for b in range(BATCHES):
        more = jnp.where(sub_wide == 0, jnp.broadcast_to(value[0, b : b + 1, :], (8, count)), 0.0)
        more = jnp.where(sub_wide == 1, jnp.broadcast_to(value[1, b : b + 1, :], (8, count)), more)
        more = jnp.where(sub_wide == 2, jnp.broadcast_to(own_code[b], (8, count)), more)
        picks[b, :, 0:SLOTS] = dot_t(jnp.concatenate([noise[b], more], axis=0), chosen[b])
        id_v[b] = (picks[b, M : M + 8, :] + 0.5).astype(jnp.int32)
    id_copy = load(id_v, id_s, 6)

    def parts_of(x, y):
        return jnp.maximum(x, 0.0), -jnp.minimum(x, 0.0), jnp.maximum(y, 0.0), -jnp.minimum(y, 0.0)

    rates = [diff[f] for f in range(F)]
    low_edge, high_edge = me_i == 0, me_i == la - 1

    def centre_of(p, k):
        return 1.0 - p[0] - p[1] - p[2] - p[3] - 4.0 * k

    own_parts = parts_of(cxv, cyv)
    row_id = iota((R, C), 0)

    def set_coef(f, first, values):
        for n in range(5):
            for h in range(2):
                v = values[n][:, h * H : (h + 1) * H]
                coef[f, n, h, first : first + max(8, v.shape[0]), :] = jnp.broadcast_to(v, (max(8, v.shape[0]), H))

    for f in range(F):
        south = jnp.where((row_id == 0) & low_edge, 0.0, own_parts[2] + rates[f])
        north = jnp.where((row_id == R - 1) & high_edge, 0.0, own_parts[3] + rates[f])
        set_coef(f, 8, [centre_of(own_parts, rates[f]), own_parts[0] + rates[f], own_parts[1] + rates[f], south, north])

    def row_step(src, dst, f, r, src_at, dst_at, far, south=True, north=True):
        first, last = lane == 0, lane == H - 1
        if far is None:
            hw = he = jnp.zeros((M, H), jnp.float32)
        else:
            turn = (H - 1 - 2 * r) & (H - 1)
            hw, he = pltpu.roll(far[0], turn, 1), pltpu.roll(far[1], turn, 1)
        c0, c1 = src[f, r + src_at, :, 0:H], src[f, r + src_at, :, H:C]
        w0, w1 = pltpu.roll(c0, 1, 1), pltpu.roll(c1, 1, 1)
        e0, e1 = pltpu.roll(c0, H - 1, 1), pltpu.roll(c1, H - 1, 1)
        w0, w1 = jnp.where(first, hw, w0), jnp.where(first, w0, w1)
        e0, e1 = jnp.where(last, e1, e0), jnp.where(last, he, e1)
        for h, (c, w, e) in enumerate(((c0, w0, e0), (c1, w1, e1))):
            cut = slice(h * H, (h + 1) * H)
            rate = [coef[f, n, h, pl.ds(r + 8, 1), :] for n in range(5)]
            out = rate[0] * c + rate[1] * w + rate[2] * e
            if south:
                out = out + rate[3] * src[f, r + src_at - 1, :, cut]
            if north:
                out = out + rate[4] * src[f, r + src_at + 1, :, cut]
            dst[f, r + dst_at, :, cut] = out

    def step_one(f, r):
        row_step(q, x1, f, r, 2, 1, (far[f, 0], far[f, 1]))

    def rows_of(step, begin, end):
        for r in range(begin, end):
            step(r)

    def inner(f, src, dst, src_at, dst_at):
        row_step(src, dst, f, 0, src_at, dst_at, None, south=False)
        rows_of(lambda r: row_step(src, dst, f, r, src_at, dst_at, None), 1, R - 1)
        row_step(src, dst, f, R - 1, src_at, dst_at, None, north=False)

    inner(0, q, x1, 2, 1)
    send_rows(0)
    inner(0, x1, x2, 1, 0)
    send_rows(1)
    id_copy.wait()
    ids = [[id_s[b, 2, s] for s in range(SLOTS)] for b in range(BATCHES)]

    came(crow_r, CROWS)
    halo_rows = [parts_of(crow_r[side, 0:1, :], crow_r[side, 1:2, :]) for side in range(2)]
    for f in range(F):
        for side, first in ((0, 0), (1, 8 + R)):
            p = halo_rows[side]
            set_coef(f, first, [centre_of(p, rates[f])] + [part + rates[f] for part in p])

    def near_weights(b):
        f = b % F

        def row_of(n, r):
            return jnp.concatenate([coef[f, n, h, r + 8 : r + 9, :] for h in range(2)], axis=1)

        at_first, at_last = iota((1, C), 1) == 0, iota((1, C), 1) == C - 1
        rows = []
        for n, back, row, halo, inner_row in ((3, 4, 0, -1, 1), (4, 3, R - 1, R, R - 2)):
            edge = row_of(n, row)
            from_w = jnp.where(at_first, 0.0, pltpu.roll(edge, 1, 1))
            from_e = jnp.where(at_last, 0.0, pltpu.roll(edge, C - 1, 1))
            rows += [
                edge * row_of(1, halo) + row_of(1, row) * from_w,
                edge * row_of(0, halo) + row_of(0, row) * edge,
                edge * row_of(2, halo) + row_of(2, row) * from_e,
                edge * row_of(n, halo),
                edge * row_of(back, halo),
                row_of(n, inner_row) * edge,
            ]
        pad = jnp.zeros((H - SLOTS, C), jnp.float32)
        spots = jnp.concatenate([hot(0, b), pad], axis=0)
        sub = iota((16, C), 0)
        stacked = jnp.zeros((16, C), jnp.float32)
        for k, row in enumerate(rows):
            stacked = jnp.where(sub == k, jnp.broadcast_to(row, (16, C)), stacked)
        weights = dot_t(stacked, spots)
        own = dot_t(jnp.concatenate([q[f, 2], q[f, R + 1]], axis=0), spots)
        code_row = id_v[b, 2:3, :]
        at_row = lax.shift_right_logical(code_row, 8) & (R - 1)
        out = []
        for side, (row, inner_row) in enumerate(((0, 1), (R - 1, R - 2))):
            w = [weights[6 * side + k : 6 * side + k + 1, :] for k in range(6)]
            w = [jnp.where(at_row == row, v, 0.0) for v in w[:5]] + [jnp.where(at_row == inner_row, w[5], 0.0)]
            out.append((w[0], w[1] + w[5], w[2], w[3], w[4] * own[side * M : (side + 1) * M]))
        return out

    lane_row = iota((1, H), 1)

    def packed_rates(f, ref, side):
        p = parts_of(ref[side, 0:1, :], ref[side, 1:2, :])
        south = jnp.where((lane_row < 2) & low_edge, 0.0, p[2] + rates[f])
        north = jnp.where((lane_row >= 2 * R - 2) & high_edge, 0.0, p[3] + rates[f])
        return centre_of(p, rates[f]), p[0] + rates[f], p[1] + rates[f], south, north

    def halo_columns(f):
        came(far.at[f], COLS + f)
        west, east = far[f, 0], far[f, 1]
        sides = (
            (next_w, west, pltpu.roll(west, 1, 1), pltpu.roll(own_w[f], 1, 1)),
            (next_e, east, pltpu.roll(own_e[f], H - 1, 1), pltpu.roll(east, H - 1, 1)),
        )
        for side, (to, c, w, e) in enumerate(sides):
            rate = packed_rates(f, ccol_r, side)
            out = rate[0] * c + rate[1] * w + rate[2] * e
            out = out + rate[3] * pltpu.roll(c, 2, 1) + rate[4] * pltpu.roll(c, H - 2, 1)
            to[f] = jnp.where(lane < 2 * R, out, 0.0)

    def near_rows(b):
        total = jnp.zeros((M, H), jnp.float32)
        for side in range(2):
            got_rows = near_r[side]
            g = [pltpu.roll(got_rows, (2 * H - 64 * b - SLOTS * k) % H, 1) for k in range(4)]
            w = near[b][side]
            total = total + w[0] * g[0] + w[1] * g[1] + w[2] * g[2] + w[3] * g[3] + w[4]
        return total

    def corner_rates(f):
        halo_w, halo_e = packed_rates(f, ccol_r, 0), packed_rates(f, ccol_r, 1)
        west, east = packed_rates(f, ccol_s, 1)[1], packed_rates(f, ccol_s, 0)[2]
        w = west * pltpu.roll(jnp.where(lane_row < R, halo_w[3], halo_w[4]), H - 1, 1)
        e = east * pltpu.roll(jnp.where(lane_row < R, halo_e[3], halo_e[4]), 1, 1)
        w = jnp.where((lane_row == 0) | (lane_row == 2 * R - 2), w, 0.0)
        e = jnp.where((lane_row == 1) | (lane_row == 2 * R - 1), e, 0.0)
        return w, e

    near = [near_weights(b) for b in range(BATCHES)]
    came(near_r, NEAR)
    rows0 = near_rows(0)
    came(ccol_r, CCOLS)
    beyond = [corner_rates(f) for f in range(F)]

    def corner_weights(b):
        code_row = id_v[b, 2:3, :]
        at_row, at_col = lax.shift_right_logical(code_row, 8) & (R - 1), code_row & (C - 1)
        west, east = beyond[b % F]
        out = []
        for side, (row, at) in enumerate(((0, 0), (R - 1, 2 * R - 2))):
            w = near[b][side]
            through_w, through_e = west[:, at : at + 1], east[:, at + 1 : at + 2]
            out.append(jnp.where(at_col == 0, w[0] + jnp.where(at_row == row, through_w, 0.0), 0.0))
            out.append(jnp.where(at_col == C - 1, w[2] + jnp.where(at_row == row, through_e, 0.0), 0.0))
        return out

    corner_part = [corner_weights(b) for b in range(BATCHES)]

    def corner_columns(f):
        turned = corner_t[...]
        return [jnp.broadcast_to(turned[f * M : (f + 1) * M, n : n + 1], (M, H)) for n in (3, 10, 17, 24)]

    def late_corners(f):
        south_w, south_e, north_w, north_e = corner_columns(f)
        far[f, 0] = jnp.where(lane == H - 1, south_w, jnp.where(lane == 2 * R + 1, north_w, far[f, 0]))
        far[f, 1] = jnp.where(lane == H - 2, south_e, jnp.where(lane == 2 * R, north_e, far[f, 1]))
        west, east = beyond[f]
        fix_w[f] = fix_w[f] + west * jnp.where(lane < R, south_w, north_w)
        fix_e[f] = fix_e[f] + east * jnp.where(lane < R, south_e, north_e)

    def fix_columns(f):
        inside = lane < 2 * R
        for side, to, outside, new, outer, turn in (
            (1, fix_w, far[f, 0], next_w, even, H - 1),
            (0, fix_e, far[f, 1], next_e, ~even, 1),
        ):
            rate = packed_rates(f, ccol_s, side)
            beside = rate[1] if side == 1 else rate[2]
            u = jnp.where(inside & outer, beside * pltpu.roll(outside, turn, 1), 0.0)
            near = beside * pltpu.roll(new[f], turn, 1) + rate[0] * u
            near = near + rate[3] * pltpu.roll(u, 2, 1) + rate[4] * pltpu.roll(u, H - 2, 1)
            to[f] = jnp.where(inside, jnp.where(outer, near, beside * pltpu.roll(u, H - turn, 1)), 0.0)

    def fix_rows(f):
        came(q.at[f, pl.ds(0, 4)], ROWS + f)
        first, last = lane == 0, lane == H - 1
        for halo, q_at, x_at, n, row, inner_row in ((-1, 1, 0, 3, 0, 1), (R, R + 2, R + 1, 4, R - 1, R - 2)):
            step_one(f, halo)
            rate = [[coef[f, k, h, row + 8 : row + 9, :] for k in range(5)] for h in range(2)]
            t = [rate[h][n] * q[f, q_at, :, h * H : (h + 1) * H] for h in range(2)]
            w = [pltpu.roll(v, 1, 1) for v in t]
            e = [pltpu.roll(v, H - 1, 1) for v in t]
            w = [jnp.where(first, 0.0, w[0]), jnp.where(first, w[0], w[1])]
            e = [jnp.where(last, e[1], e[0]), jnp.where(last, 0.0, e[1])]
            for h in range(2):
                cut = slice(h * H, (h + 1) * H)
                add = rate[h][n] * x1[f, x_at, :, cut] + rate[h][0] * t[h] + rate[h][1] * w[h] + rate[h][2] * e[h]
                x2[f, row, :, cut] = x2[f, row, :, cut] + add
                x2[f, inner_row, :, cut] = (
                    x2[f, inner_row, :, cut] + coef[f, n, h, inner_row + 8 : inner_row + 9, :] * t[h]
                )

    def unpack_columns(f):
        def body(r):
            west = pltpu.roll(fix_w[f], (H - 2 * r) & (H - 1), 1)
            east = pltpu.roll(fix_e[f], (H - 2 - 2 * r) & (H - 1), 1)
            x2[f, r, :, 0:H] = x2[f, r, :, 0:H] + jnp.where(lane < 2, west, 0.0)
            x2[f, r, :, H:C] = x2[f, r, :, H:C] + jnp.where(lane >= H - 2, east, 0.0)

        rows_of(body, 0, R)

    def see(b):
        f = b % F
        seen = jnp.zeros((M, H), jnp.float32)
        for s in range(SLOTS):
            code_s = ids[b][s]
            at_row = lax.shift_right_logical(code_s, 8) & (R - 1)
            col = code_s & (C - 1)
            row = x2[f, at_row]
            picked = jnp.where(lane == col, row[:, 0:H], 0.0) + jnp.where(lane + H == col, row[:, H:C], 0.0)
            spot_w = jnp.where(col < 2, 2 * at_row + col, -1)
            spot_e = jnp.where(col >= C - 2, 2 * at_row + col - (C - 2), -1)
            picked = picked + jnp.where(lane == spot_w, fix_w[f], 0.0) + jnp.where(lane == spot_e, fix_e[f], 0.0)
            seen = jnp.where(lane == s, jnp.broadcast_to(jnp.sum(picked, axis=1, keepdims=True), (M, H)), seen)
        return seen

    def observe(b, seen):
        for weight, column in zip(corner_part[b], corner_columns(b % F)):
            seen = seen + weight * column
        mean = jnp.sum(seen, axis=0, keepdims=True) * (1.0 / M)
        var_b = picks[b, M + 1 : M + 2, :]
        there = var_b > 0.0
        scale = jnp.where(there, jnp.sqrt(1.0 / jnp.where(there, var_b, 1.0)), 0.0)
        innovation = picks[b, M : M + 1, :] + picks[b, 0:M, :] - seen
        stacked = jnp.concatenate([scale * (seen - mean), scale * innovation, fill], axis=0)
        return stacked.T[0:SLOTS]

    def tell(b, r):
        packed = r[0:8] + pltpu.roll(r[8:16], 2 * M, 1)
        msg[b] = packed
        got[b, 14] = packed
        got[b, 15] = jnp.zeros((8, H), jnp.float32)
        for n, (di, dj) in enumerate(REACH):
            pltpu.make_async_remote_copy(
                src_ref=msg.at[b], dst_ref=got.at[b, n], send_sem=p2_send.at[b], recv_sem=p2_recv.at[b],
                device_id=at(-di, -dj), device_id_type=MESH,
            ).start()

    def transform(b):
        others = got.at[b, pl.ds(0, len(REACH))]
        pltpu.make_async_copy(others, others, p2_recv.at[b]).wait()
        stack = got[b].reshape(16 * 8, H)
        place = lax.shift_right_logical(iota((16 * 8, H), 0), 3)
        keep = jnp.ones((16 * 8, H), jnp.float32)
        for n, (di, dj) in enumerate(REACH):
            if di != 0:
                keep = jnp.where((low_edge if di < 0 else high_edge) & (place == n), 0.0, keep)
        stack = stack * keep
        turned = stack.T
        gram = dot(jnp.concatenate([turned[0:M], turned[2 * M : 3 * M]], axis=0), stack)
        both = gram[0:M] + pltpu.roll(gram[M : 2 * M], 2 * M, 1)
        system = jnp.where(lane < 2 * M, both, 0.0) + jnp.where(lane == iota((M, H), 0), M - 1.0, 0.0)
        return eliminate(system)

    def centered_rows(solved):
        w = jnp.where(lane < M, pltpu.roll(solved, H - M, 1), 0.0)
        return w - jnp.sum(w, axis=0, keepdims=True) * (1.0 / M)

    halo_columns(0)
    fix_columns(0)
    seen0 = see(0)
    seen0 = seen0 + rows0
    came(corner_r, CORNER)
    corner_t[...] = jnp.concatenate([corner_r[n] for n in range(4)] + [jnp.zeros((H - 32, H), jnp.float32)], axis=0).T
    tell(0, observe(0, seen0))
    inner(1, q, x1, 2, 1)
    inner(1, x1, x2, 1, 0)
    halo_columns(1)
    fix_columns(1)
    r1 = observe(1, see(1) + near_rows(1))
    solved0 = transform(0)
    w0 = jnp.where(lane < M, pltpu.roll(solved0, H - M, 1), 0.0)
    w0_mean = jnp.sum(w0, axis=1, keepdims=True) * (1.0 / M)
    both0 = jnp.where(lane < M, w0 - w0_mean, jnp.where(lane < 2 * M, -solved0, 0.0))
    tell(1, r1 + dot(r1[:, 0:M], both0))
    c0 = centered_rows(solved0)
    late_corners(0)
    late_corners(1)
    unpack_columns(0)
    unpack_columns(1)
    fix_rows(0)
    fix_rows(1)
    sent(near_s, NEAR)
    for f in range(F):
        sent(q.at[f, pl.ds(2, 4)], ROWS + f)
        sent(far.at[f], COLS + f)
    sent(corner_r, CORNER)
    sent(crow_s, CROWS)
    sent(ccol_s, CCOLS)
    solved1 = transform(1)
    c1 = centered_rows(solved1)
    e_out[...] = c0 + c1 + dot(c0[:, 0:M], c1)
    for b in range(BATCHES):
        others = got.at[b, pl.ds(0, len(REACH))]
        pltpu.make_async_copy(others, others, p2_send.at[b]).wait()


def analysis_kernel(e_ref, x, out, y, out_sem):
    groups = [(f, r) for f in range(F) for r in range(0, R, GROUP)]
    e = jnp.concatenate([e_ref[...], jnp.zeros((H - M, H), jnp.float32)], axis=0).T[0:M, 0:M]
    e_hi = e.astype(jnp.bfloat16)
    e_lo = (e - e_hi.astype(jnp.float32)).astype(jnp.bfloat16)
    left = jnp.concatenate([e_hi, e_hi, e_lo], axis=1)
    for f, r in groups:
        for row in range(r, r + GROUP):
            v = x[f, row]
            hi = v.astype(jnp.bfloat16)
            low = (v - hi.astype(jnp.float32)).astype(jnp.bfloat16)
            right = jnp.concatenate([hi, low, hi], axis=0)
            add = lax.dot_general(left, right, (((1,), (0,)), ((), ())), preferred_element_type=jnp.float32)
            y[f, row] = v + add
        for row in range(r, r + GROUP):
            pltpu.make_async_copy(y.at[f, row], out.at[f, :, row, :], out_sem).start()
    pltpu.make_async_copy(y, y, out_sem).wait()


def local(ensemble, courant_x, courant_y, diffusion, obs_cell, obs_value, obs_noise, obs_var, loc_mask):
    any_space = pl.BlockSpec(memory_space=pl.ANY)
    f32 = jnp.float32
    count = obs_cell.shape[1]
    vmem = pltpu.VMEM
    dma = pltpu.SemaphoreType.DMA
    noise_turned = obs_noise.swapaxes(1, 2)
    operands = (
        ensemble.reshape(F, M * R, C), courant_x, courant_y, diffusion, obs_cell, obs_value, noise_turned, obs_var
    )
    forecast, combined = pl.pallas_call(
        forecast_kernel,
        out_shape=(vmem((F, R, M, C), f32), vmem((M, H), f32)),
        in_specs=[pl.BlockSpec(memory_space=pltpu.HBM)] * 8,
        out_specs=(pl.BlockSpec(memory_space=pltpu.VMEM), pl.BlockSpec(memory_space=pltpu.VMEM)),
        scratch_shapes=[
            vmem((2, F, M * R, H), f32),
            vmem((F, R + 4, M, C), f32),
            vmem((F, R + 2, M, C), f32),
            vmem((F, M, H), f32),
            vmem((F, M, H), f32),
            vmem((F, 2, M, H), f32),
            vmem((F, M, H), f32),
            vmem((F, M, H), f32),
            vmem((8, H), f32),
            vmem((4, 8, H), f32),
            vmem((H, H), f32),
            vmem((2, M, H), f32),
            vmem((2, M, H), f32),
            vmem((2, 8, C), f32),
            vmem((2, 8, C), f32),
            vmem((2, 8, H), f32),
            vmem((2, 8, H), f32),
            vmem((F, M, H), f32),
            vmem((F, M, H), f32),
            vmem((F, 5, 2, R + 16, H), f32),
            vmem((2, R, C), f32),
            pltpu.SMEM((F,), f32),
            vmem((BATCHES, count), jnp.int32),
            vmem((BATCHES * count // H, H), jnp.int32),
            vmem((2, BATCHES, count), f32),
            vmem((BATCHES, M, count), f32),
            vmem((BATCHES, M + 8, H), f32),
            vmem((BATCHES, 8, H), jnp.int32),
            pltpu.SMEM((BATCHES, 8, H), jnp.int32),
            vmem((BATCHES, 8, H), f32),
            vmem((BATCHES, 16, 8, H), f32),
            dma((7,)),
            dma((CHANNELS,)),
            dma((CHANNELS,)),
            dma((BATCHES,)),
            dma((BATCHES,)),
        ],
        compiler_params=pltpu.CompilerParams(
            collective_id=0, has_side_effects=True, vmem_limit_bytes=48 * 1024 * 1024
        ),
        name="forecast_and_transform",
    )(*(pltpu.with_memory_space_constraint(a, pltpu.HBM) for a in operands))
    return pl.pallas_call(
        analysis_kernel,
        out_shape=jax.ShapeDtypeStruct((F, M, R, C), f32),
        in_specs=[pl.BlockSpec(memory_space=pltpu.VMEM)] * 2,
        out_specs=any_space,
        scratch_shapes=[
            vmem((F, R, M, C), f32),
            dma,
        ],
        compiler_params=pltpu.CompilerParams(vmem_limit_bytes=48 * 1024 * 1024),
        name="analysis",
    )(*(pltpu.with_memory_space_constraint(a, pltpu.VMEM) for a in (combined, forecast)))


def solution(mesh):
    in_specs = (
        P(None, None, "lat", "lon"),
        P("lat", "lon"),
        P("lat", "lon"),
        P(),
        P(),
        P(),
        P(),
        P(),
        P("lat", "lon", None, None),
    )
    out_specs = P(None, None, "lat", "lon")
    return jax.shard_map(local, mesh=mesh, in_specs=in_specs, out_specs=out_specs, check_vma=False)
```

```python
import jax
import jax.numpy as jnp
from jax import lax
from jax.experimental import pallas as pl
from jax.experimental.pallas import tpu as pltpu
from jax.sharding import PartitionSpec as P

MESH = pl.DeviceIdType.MESH
HI = lax.Precision.HIGHEST
F, M, R, C = 2, 32, 32, 256
H = 128
SLOTS = 16
BATCHES = 2
GROUP = 32
REACH = tuple(sorted(((di, dj) for di in (-1, 0, 1) for dj in range(-2, 3) if (di, dj) != (0, 0)), key=lambda d: -abs(d[0]) * 3 - abs(d[1])))
ADJACENT = tuple(d for d in REACH if abs(d[1]) < 2)
ROWS, COLS, CORNER, CROWS, CCOLS, NEAR = 0, 2, 4, 5, 6, 7
CHANNELS = 8


def iota(shape, axis):
    return lax.broadcasted_iota(jnp.int32, shape, axis)


def dot(a, b):
    return lax.dot_general(a, b, (((1,), (0,)), ((), ())), precision=HI, preferred_element_type=jnp.float32)


def dot_t(a, b):
    return lax.dot_general(a, b, (((1,), (1,)), ((), ())), precision=HI, preferred_element_type=jnp.float32)


def eliminate(system):
    parts = [system[8 * g : 8 * g + 8] for g in range(4)]
    sub = iota((8, H), 0)
    for own in range(4):
        lanes = range(8 * own, 8 * own + 8)
        columns = [[jnp.broadcast_to(part[:, k : k + 1], (8, H)) for part in parts] for k in lanes]
        pivots = [[jnp.broadcast_to(columns[j][own][i : i + 1], (8, H)) for j in range(8)] for i in range(8)]
        rows = [jnp.broadcast_to(parts[own][i : i + 1], (8, H)) for i in range(8)]
        for p in range(8):
            inverse = 1.0 / pivots[p][p]
            rows[p] = rows[p] * inverse
            for j in range(p + 1, 8):
                pivots[p][j] = pivots[p][j] * inverse
            for i in range(8):
                if i != p:
                    factor = pivots[i][p]
                    rows[i] = rows[i] - factor * rows[p]
                    for j in range(p + 1, 8):
                        pivots[i][j] = pivots[i][j] - factor * pivots[p][j]
        new = []
        for g in range(4):
            terms = [columns[j][g] * rows[j] for j in range(8)]
            while len(terms) > 1:
                terms = [terms[n] + terms[n + 1] for n in range(0, len(terms), 2)]
            new.append(parts[g] - terms[0])
        for i in range(8):
            new[own] = jnp.where(sub == i, rows[i], new[own])
        parts = new
    return jnp.concatenate(parts, axis=0)


def forecast_kernel(
    ens, cx_in, cy_in, diff_in, cell_in, value_in, noise_in, var_in,
    x2, e_out,
    halves, q, x1, own_w, own_e, far, next_w, next_e, corner_s, corner_r, corner_t, near_s, near_r, crow_s, crow_r, ccol_s, ccol_r,
    fix_w, fix_e, coef, courant, diff, cell, cell16, value, noise, picks, id_v, id_s, msg, got,
    in_sem, p1_send, p1_recv, p2_send, p2_recv,
):
    la, lo = lax.axis_size("lat"), lax.axis_size("lon")
    me_i, me_j = lax.axis_index("lat"), lax.axis_index("lon")

    def at(di, dj):
        return (lax.rem(me_i + (di + la), la), lax.rem(me_j + (dj + lo), lo))

    barrier = pltpu.get_barrier_semaphore()
    for di, dj in ADJACENT:
        pl.semaphore_signal(barrier, inc=1, device_id=at(di, dj), device_id_type=MESH)

    def load(src, dst, sem):
        copy = pltpu.make_async_copy(src, dst, in_sem.at[sem])
        copy.start()
        return copy

    def loaded(dst, sem):
        pltpu.make_async_copy(dst, dst, in_sem.at[sem]).wait()

    cell_copy = load(cell_in, cell, 3)
    load(cx_in, courant.at[0], 1)
    load(cy_in, courant.at[1], 1)
    for f in range(F):
        for h in range(2):
            load(ens.at[f, :, pl.ds(h * H, H)], halves.at[h, f], 0)
    diff_copy = load(diff_in, diff, 2)
    load(value_in, value.at[0], 4)
    load(var_in, value.at[1], 4)
    noise_copy = load(noise_in, noise, 5)

    lane = iota((M, H), 1)
    lane8 = iota((8, H), 1)
    def send(channel, src, dst, target):
        copy = pltpu.make_async_remote_copy(
            src_ref=src, dst_ref=dst, send_sem=p1_send.at[channel], recv_sem=p1_recv.at[channel],
            device_id=target, device_id_type=MESH,
        )
        copy.start()

    def sent(src, channel):
        pltpu.make_async_copy(src, src, p1_send.at[channel]).wait()

    def came(dst, channel):
        pltpu.make_async_copy(dst, dst, p1_recv.at[channel]).wait()

    count = cell.shape[1]
    chunks = count // H
    wide = lo * C
    shift = wide.bit_length() - 1
    n_rows = BATCHES * chunks
    cell_copy.wait()
    for ch in range(chunks):
        cell16[BATCHES * ch : BATCHES * (ch + 1), :] = cell[:, ch * H : (ch + 1) * H]
    cells = cell16[...]
    l_col = (cells & (wide - 1)) - me_j * C
    tiles = (0, 1, -1)
    masks, codes = [], []
    for di in tiles:
        l_row = lax.shift_right_logical(cells, shift) - lax.rem(me_i + (di + la), la) * R
        mine = (l_row >= 0) & (l_row < R) & (l_col >= 0) & (l_col < C)
        masks.append(jnp.where(mine, 1.0, 0.0))
        codes.append(jnp.where(mine, l_row * C + l_col, 0).astype(jnp.float32))
    mask = jnp.concatenate(masks, axis=0)
    all_rows = len(tiles) * n_rows
    before = jnp.where(iota((H, H), 0) < iota((H, H), 1), 1.0, 0.0)
    ii, jj = iota((all_rows, all_rows), 0), iota((all_rows, all_rows), 1)
    related = (lax.rem(ii, BATCHES) == lax.rem(jj, BATCHES)) & (lax.div(ii, n_rows) == lax.div(jj, n_rows))
    rows_before = jnp.where(related & (jj < ii), 1.0, 0.0)
    totals = jnp.broadcast_to(jnp.sum(mask, axis=1, keepdims=True), (all_rows, H))
    rank = dot(mask, before) + dot(rows_before, totals)
    rank = jnp.where(mask > 0.5, rank, -1.0).astype(jnp.int32)
    slot = iota((SLOTS, H), 0)
    slot_lane = iota((SLOTS, H), 1)
    slot_wide = iota((SLOTS, C), 1)
    chosen, own_code, columns = [], [], []
    for n, di in enumerate(tiles):
        for b in range(BATCHES):
            rows_b = [BATCHES * ch + b for ch in range(chunks)]
            picked = [jnp.broadcast_to(rank[n * n_rows + k : n * n_rows + k + 1, :], (SLOTS, H)) == slot for k in rows_b]
            total = jnp.zeros((SLOTS, H), jnp.float32)
            for here, k in zip(picked, rows_b):
                total = jnp.where(here, jnp.broadcast_to(codes[n][k : k + 1, :], (SLOTS, H)), total)
            code_b = jnp.sum(total, axis=1, keepdims=True).astype(jnp.int32)
            columns.append(jnp.broadcast_to(code_b & (C - 1), (SLOTS, C)))
            if di == 0:
                chosen.append(jnp.concatenate([jnp.where(here, 1.0, 0.0) for here in picked], axis=1))
                own_code.append(jnp.concatenate([codes[n][k : k + 1, :] for k in rows_b], axis=1))

    def hot(n, b, by=0):
        return jnp.where(slot_wide == columns[BATCHES * n + b] + by, 1.0, 0.0)

    loaded(courant, 1)
    diff_copy.wait()
    cxv, cyv = courant[0], courant[1]
    for side, row in ((0, R - 1), (1, 0)):
        crow_s[side, 0:1, :] = cxv[row : row + 1, :]
        crow_s[side, 1:2, :] = cyv[row : row + 1, :]
    spot = (lax.shift_right_logical(lane, 1) == iota((R, H), 0)) & (lane < 2 * R)
    even = (lane & 1) == 0
    for side, col in ((0, C - 2), (1, 0)):
        for n, source in enumerate((cxv, cyv)):
            pair = [jnp.broadcast_to(source[:, col + c : col + c + 1], (R, H)) for c in range(2)]
            spread = jnp.where(spot, jnp.where(even, pair[0], pair[1]), 0.0)
            ccol_s[side, n : n + 1, :] = jnp.sum(spread, axis=0, keepdims=True)

    loaded(halves, 0)

    def corner_lanes(f):
        cells = [
            halves[0, f, pl.ds(0, M, stride=R), :],
            pltpu.roll(halves[1, f, pl.ds(0, M, stride=R), :], 2, 1),
            pltpu.roll(halves[0, f, pl.ds(R - 1, M, stride=R), :], 2, 1),
            pltpu.roll(halves[1, f, pl.ds(R - 1, M, stride=R), :], 4, 1),
        ]
        out = jnp.where(lane == 3, cells[3], 0.0)
        for n in range(3):
            out = jnp.where(lane == n, cells[n], out)
        return out

    fill = jnp.zeros((H - F * M, H), jnp.float32)
    corner_s[...] = jnp.concatenate([corner_lanes(0), corner_lanes(1), fill], axis=0).T[0:8]

    def pack(f):
        def body(r, carry):
            west, east = carry
            c0 = halves[0, f, pl.ds(r, M, stride=R), :]
            c1 = halves[1, f, pl.ds(r, M, stride=R), :]
            q[f, r + 2, :, 0:H] = c0
            q[f, r + 2, :, H:C] = c1
            here = lax.shift_right_logical(lane, 1) == r
            west = jnp.where(here, pltpu.roll(c0, 2 * r, 1), west)
            east = jnp.where(here, pltpu.roll(c1, lax.rem(2 * r + 2, H), 1), east)
            return west, east

        zero = jnp.zeros((M, H), jnp.float32)
        west, east = lax.fori_loop(0, R, body, (zero, zero), unroll=R)
        own_w[f] = west
        own_e[f] = east

    def send_field(f):
        send(COLS + f, own_e.at[f], far.at[f, 0], at(0, 1))
        send(COLS + f, own_w.at[f], far.at[f, 1], at(0, -1))

    def send_rows(f):
        send(ROWS + f, q.at[f, pl.ds(R, 2)], q.at[f, pl.ds(0, 2)], at(1, 0))
        send(ROWS + f, q.at[f, pl.ds(2, 2)], q.at[f, pl.ds(R + 2, 2)], at(-1, 0))

    pack(0)

    def edge_row(f, r):
        return jnp.concatenate([halves[h, f, pl.ds(r, M, stride=R), :] for h in range(2)], axis=1)

    none = jnp.zeros((2 * M, C), jnp.float32)
    for side, (outer, inner_row) in enumerate(((R - 1, R - 2), (0, 1))):
        out = jnp.zeros((M, H), jnp.float32)
        for b in range(BATCHES):
            spots = jnp.concatenate([hot(side + 1, b, by) for by in (-1, 0, 1, 0)], axis=0)
            spots = jnp.concatenate([spots, none] if b == 0 else [none, spots], axis=0)
            both = dot_t(jnp.concatenate([edge_row(b % F, outer), edge_row(b % F, inner_row)], axis=0), spots)
            out = out + jnp.where((lane & 63) < 48, both[0:M], both[M : 2 * M])
        near_s[side] = out
    pl.semaphore_wait(barrier, len(ADJACENT))
    for n, target in enumerate(((1, 1), (1, -1), (-1, 1), (-1, -1))):
        send(CORNER, corner_s, corner_r.at[n], at(*target))
    send(NEAR, near_s.at[0], near_r.at[0], at(1, 0))
    send(NEAR, near_s.at[1], near_r.at[1], at(-1, 0))
    send(CROWS, crow_s.at[0], crow_r.at[0], at(1, 0))
    send(CROWS, crow_s.at[1], crow_r.at[1], at(-1, 0))
    send(CCOLS, ccol_s.at[0], ccol_r.at[0], at(0, 1))
    send(CCOLS, ccol_s.at[1], ccol_r.at[1], at(0, -1))
    send_field(0)
    pack(1)
    send_field(1)

    loaded(value, 4)
    noise_copy.wait()
    picks[...] = jnp.zeros((BATCHES, M + 8, H), jnp.float32)
    sub_wide = iota((8, count), 0)
    for b in range(BATCHES):
        more = jnp.where(sub_wide == 0, jnp.broadcast_to(value[0, b : b + 1, :], (8, count)), 0.0)
        more = jnp.where(sub_wide == 1, jnp.broadcast_to(value[1, b : b + 1, :], (8, count)), more)
        more = jnp.where(sub_wide == 2, jnp.broadcast_to(own_code[b], (8, count)), more)
        picks[b, :, 0:SLOTS] = dot_t(jnp.concatenate([noise[b], more], axis=0), chosen[b])
        id_v[b] = (picks[b, M : M + 8, :] + 0.5).astype(jnp.int32)
    id_copy = load(id_v, id_s, 6)

    def parts_of(x, y):
        return jnp.maximum(x, 0.0), -jnp.minimum(x, 0.0), jnp.maximum(y, 0.0), -jnp.minimum(y, 0.0)

    rates = [diff[f] for f in range(F)]
    low_edge, high_edge = me_i == 0, me_i == la - 1

    def centre_of(p, k):
        return 1.0 - p[0] - p[1] - p[2] - p[3] - 4.0 * k

    own_parts = parts_of(cxv, cyv)
    row_id = iota((R, C), 0)

    def set_coef(f, first, values):
        for n in range(5):
            for h in range(2):
                v = values[n][:, h * H : (h + 1) * H]
                coef[f, n, h, first : first + max(8, v.shape[0]), :] = jnp.broadcast_to(v, (max(8, v.shape[0]), H))

    for f in range(F):
        south = jnp.where((row_id == 0) & low_edge, 0.0, own_parts[2] + rates[f])
        north = jnp.where((row_id == R - 1) & high_edge, 0.0, own_parts[3] + rates[f])
        set_coef(f, 8, [centre_of(own_parts, rates[f]), own_parts[0] + rates[f], own_parts[1] + rates[f], south, north])

    def row_step(src, dst, f, r, src_at, dst_at, far, south=True, north=True):
        first, last = lane == 0, lane == H - 1
        if far is None:
            hw = he = jnp.zeros((M, H), jnp.float32)
        else:
            turn = (H - 1 - 2 * r) & (H - 1)
            hw, he = pltpu.roll(far[0], turn, 1), pltpu.roll(far[1], turn, 1)
        c0, c1 = src[f, r + src_at, :, 0:H], src[f, r + src_at, :, H:C]
        w0, w1 = pltpu.roll(c0, 1, 1), pltpu.roll(c1, 1, 1)
        e0, e1 = pltpu.roll(c0, H - 1, 1), pltpu.roll(c1, H - 1, 1)
        w0, w1 = jnp.where(first, hw, w0), jnp.where(first, w0, w1)
        e0, e1 = jnp.where(last, e1, e0), jnp.where(last, he, e1)
        for h, (c, w, e) in enumerate(((c0, w0, e0), (c1, w1, e1))):
            cut = slice(h * H, (h + 1) * H)
            rate = [coef[f, n, h, pl.ds(r + 8, 1), :] for n in range(5)]
            out = rate[0] * c + rate[1] * w + rate[2] * e
            if south:
                out = out + rate[3] * src[f, r + src_at - 1, :, cut]
            if north:
                out = out + rate[4] * src[f, r + src_at + 1, :, cut]
            dst[f, r + dst_at, :, cut] = out

    def step_one(f, r):
        row_step(q, x1, f, r, 2, 1, (far[f, 0], far[f, 1]))

    def rows_of(step, begin, end):
        for r in range(begin, end):
            step(r)

    def inner(f, src, dst, src_at, dst_at):
        row_step(src, dst, f, 0, src_at, dst_at, None, south=False)
        rows_of(lambda r: row_step(src, dst, f, r, src_at, dst_at, None), 1, R - 1)
        row_step(src, dst, f, R - 1, src_at, dst_at, None, north=False)

    inner(0, q, x1, 2, 1)
    send_rows(0)
    inner(0, x1, x2, 1, 0)
    send_rows(1)
    id_copy.wait()
    ids = [[id_s[b, 2, s] for s in range(SLOTS)] for b in range(BATCHES)]


    def near_weights(b):
        f = b % F

        def row_of(n, r):
            return jnp.concatenate([coef[f, n, h, r + 8 : r + 9, :] for h in range(2)], axis=1)

        at_first, at_last = iota((1, C), 1) == 0, iota((1, C), 1) == C - 1
        rows = []
        for n, back, row, halo, inner_row in ((3, 4, 0, -1, 1), (4, 3, R - 1, R, R - 2)):
            edge = row_of(n, row)
            from_w = jnp.where(at_first, 0.0, pltpu.roll(edge, 1, 1))
            from_e = jnp.where(at_last, 0.0, pltpu.roll(edge, C - 1, 1))
            rows += [
                edge * row_of(1, halo) + row_of(1, row) * from_w,
                edge * row_of(0, halo) + row_of(0, row) * edge,
                edge * row_of(2, halo) + row_of(2, row) * from_e,
                edge * row_of(n, halo),
                edge * row_of(back, halo),
                row_of(n, inner_row) * edge,
            ]
        sub = iota((16, C), 0)
        stacked = jnp.zeros((16, C), jnp.float32)
        for k, row in enumerate(rows):
            stacked = jnp.where(sub == k, jnp.broadcast_to(row, (16, C)), stacked)
        weights = dot_t(stacked, spots[b])
        own = own_edges[b]
        code_row = id_v[b, 2:3, :]
        at_row = lax.shift_right_logical(code_row, 8) & (R - 1)
        out = []
        for side, (row, inner_row) in enumerate(((0, 1), (R - 1, R - 2))):
            w = [weights[6 * side + k : 6 * side + k + 1, :] for k in range(6)]
            w = [jnp.where(at_row == row, v, 0.0) for v in w[:5]] + [jnp.where(at_row == inner_row, w[5], 0.0)]
            out.append((w[0], w[1] + w[5], w[2], w[3], w[4] * own[side * M : (side + 1) * M]))
        return out

    lane_row = iota((1, H), 1)

    def packed_rates(f, ref, side):
        p = parts_of(ref[side, 0:1, :], ref[side, 1:2, :])
        south = jnp.where((lane_row < 2) & low_edge, 0.0, p[2] + rates[f])
        north = jnp.where((lane_row >= 2 * R - 2) & high_edge, 0.0, p[3] + rates[f])
        return centre_of(p, rates[f]), p[0] + rates[f], p[1] + rates[f], south, north

    def halo_columns(f):
        came(far.at[f], COLS + f)
        west, east = far[f, 0], far[f, 1]
        sides = (
            (next_w, west, pltpu.roll(west, 1, 1), pltpu.roll(own_w[f], 1, 1)),
            (next_e, east, pltpu.roll(own_e[f], H - 1, 1), pltpu.roll(east, H - 1, 1)),
        )
        for side, (to, c, w, e) in enumerate(sides):
            rate = packed_rates(f, ccol_r, side)
            out = rate[0] * c + rate[1] * w + rate[2] * e
            out = out + rate[3] * pltpu.roll(c, 2, 1) + rate[4] * pltpu.roll(c, H - 2, 1)
            to[f] = jnp.where(lane < 2 * R, out, 0.0)

    def near_rows(b):
        total = jnp.zeros((M, H), jnp.float32)
        for side in range(2):
            got_rows = near_r[side]
            g = [pltpu.roll(got_rows, (2 * H - 64 * b - SLOTS * k) % H, 1) for k in range(4)]
            w = near[b][side]
            total = total + w[0] * g[0] + w[1] * g[1] + w[2] * g[2] + w[3] * g[3] + w[4]
        return total

    def corner_rates(f):
        halo_w, halo_e = packed_rates(f, ccol_r, 0), packed_rates(f, ccol_r, 1)
        west, east = packed_rates(f, ccol_s, 1)[1], packed_rates(f, ccol_s, 0)[2]
        w = west * pltpu.roll(jnp.where(lane_row < R, halo_w[3], halo_w[4]), H - 1, 1)
        e = east * pltpu.roll(jnp.where(lane_row < R, halo_e[3], halo_e[4]), 1, 1)
        w = jnp.where((lane_row == 0) | (lane_row == 2 * R - 2), w, 0.0)
        e = jnp.where((lane_row == 1) | (lane_row == 2 * R - 1), e, 0.0)
        return w, e

    near = [None] * BATCHES
    pad = jnp.zeros((H - SLOTS, C), jnp.float32)
    spots = [jnp.concatenate([hot(0, b), pad], axis=0) for b in range(BATCHES)]
    own_edges = [dot_t(jnp.concatenate([q[b % F, 2], q[b % F, R + 1]], axis=0), spots[b]) for b in range(BATCHES)]
    came(ccol_r, CCOLS)
    beyond = [corner_rates(f) for f in range(F)]

    def corner_weights(b):
        code_row = id_v[b, 2:3, :]
        at_row, at_col = lax.shift_right_logical(code_row, 8) & (R - 1), code_row & (C - 1)
        west, east = beyond[b % F]
        out = []
        for side, (row, at) in enumerate(((0, 0), (R - 1, 2 * R - 2))):
            w = near[b][side]
            through_w, through_e = west[:, at : at + 1], east[:, at + 1 : at + 2]
            out.append(jnp.where(at_col == 0, w[0] + jnp.where(at_row == row, through_w, 0.0), 0.0))
            out.append(jnp.where(at_col == C - 1, w[2] + jnp.where(at_row == row, through_e, 0.0), 0.0))
        return out

    corner_part = [None] * BATCHES

    def corner_columns(f):
        turned = corner_t[...]
        return [jnp.broadcast_to(turned[f * M : (f + 1) * M, n : n + 1], (M, H)) for n in (3, 10, 17, 24)]

    def late_corners(f):
        south_w, south_e, north_w, north_e = corner_columns(f)
        far[f, 0] = jnp.where(lane == H - 1, south_w, jnp.where(lane == 2 * R + 1, north_w, far[f, 0]))
        far[f, 1] = jnp.where(lane == H - 2, south_e, jnp.where(lane == 2 * R, north_e, far[f, 1]))
        west, east = beyond[f]
        fix_w[f] = fix_w[f] + west * jnp.where(lane < R, south_w, north_w)
        fix_e[f] = fix_e[f] + east * jnp.where(lane < R, south_e, north_e)

    def fix_columns(f):
        inside = lane < 2 * R
        for side, to, outside, new, outer, turn in (
            (1, fix_w, far[f, 0], next_w, even, H - 1),
            (0, fix_e, far[f, 1], next_e, ~even, 1),
        ):
            rate = packed_rates(f, ccol_s, side)
            beside = rate[1] if side == 1 else rate[2]
            u = jnp.where(inside & outer, beside * pltpu.roll(outside, turn, 1), 0.0)
            near = beside * pltpu.roll(new[f], turn, 1) + rate[0] * u
            near = near + rate[3] * pltpu.roll(u, 2, 1) + rate[4] * pltpu.roll(u, H - 2, 1)
            to[f] = jnp.where(inside, jnp.where(outer, near, beside * pltpu.roll(u, H - turn, 1)), 0.0)

    def fix_rows(f):
        came(q.at[f, pl.ds(0, 4)], ROWS + f)
        first, last = lane == 0, lane == H - 1
        for halo, q_at, x_at, n, row, inner_row in ((-1, 1, 0, 3, 0, 1), (R, R + 2, R + 1, 4, R - 1, R - 2)):
            step_one(f, halo)
            rate = [[coef[f, k, h, row + 8 : row + 9, :] for k in range(5)] for h in range(2)]
            t = [rate[h][n] * q[f, q_at, :, h * H : (h + 1) * H] for h in range(2)]
            w = [pltpu.roll(v, 1, 1) for v in t]
            e = [pltpu.roll(v, H - 1, 1) for v in t]
            w = [jnp.where(first, 0.0, w[0]), jnp.where(first, w[0], w[1])]
            e = [jnp.where(last, e[1], e[0]), jnp.where(last, 0.0, e[1])]
            for h in range(2):
                cut = slice(h * H, (h + 1) * H)
                add = rate[h][n] * x1[f, x_at, :, cut] + rate[h][0] * t[h] + rate[h][1] * w[h] + rate[h][2] * e[h]
                x2[f, row, :, cut] = x2[f, row, :, cut] + add
                x2[f, inner_row, :, cut] = (
                    x2[f, inner_row, :, cut] + coef[f, n, h, inner_row + 8 : inner_row + 9, :] * t[h]
                )

    def unpack_columns(f):
        def body(r):
            west = pltpu.roll(fix_w[f], (H - 2 * r) & (H - 1), 1)
            east = pltpu.roll(fix_e[f], (H - 2 - 2 * r) & (H - 1), 1)
            x2[f, r, :, 0:H] = x2[f, r, :, 0:H] + jnp.where(lane < 2, west, 0.0)
            x2[f, r, :, H:C] = x2[f, r, :, H:C] + jnp.where(lane >= H - 2, east, 0.0)

        rows_of(body, 0, R)

    def see(b):
        f = b % F
        seen = jnp.zeros((M, H), jnp.float32)
        for s in range(SLOTS):
            code_s = ids[b][s]
            at_row = lax.shift_right_logical(code_s, 8) & (R - 1)
            col = code_s & (C - 1)
            row = x2[f, at_row]
            picked = jnp.where(lane == col, row[:, 0:H], 0.0) + jnp.where(lane + H == col, row[:, H:C], 0.0)
            spot_w = jnp.where(col < 2, 2 * at_row + col, -1)
            spot_e = jnp.where(col >= C - 2, 2 * at_row + col - (C - 2), -1)
            picked = picked + jnp.where(lane == spot_w, fix_w[f], 0.0) + jnp.where(lane == spot_e, fix_e[f], 0.0)
            seen = jnp.where(lane == s, jnp.broadcast_to(jnp.sum(picked, axis=1, keepdims=True), (M, H)), seen)
        return seen

    def observe(b, seen):
        for weight, column in zip(corner_part[b], corner_columns(b % F)):
            seen = seen + weight * column
        mean = jnp.sum(seen, axis=0, keepdims=True) * (1.0 / M)
        var_b = picks[b, M + 1 : M + 2, :]
        there = var_b > 0.0
        scale = jnp.where(there, jnp.sqrt(1.0 / jnp.where(there, var_b, 1.0)), 0.0)
        innovation = picks[b, M : M + 1, :] + picks[b, 0:M, :] - seen
        stacked = jnp.concatenate([scale * (seen - mean), scale * innovation, fill], axis=0)
        return stacked.T[0:SLOTS]

    def tell(b, r):
        packed = r[0:8] + pltpu.roll(r[8:16], 2 * M, 1)
        msg[b] = packed
        got[b, 14] = packed
        got[b, 15] = jnp.zeros((8, H), jnp.float32)
        for n, (di, dj) in enumerate(REACH):
            pltpu.make_async_remote_copy(
                src_ref=msg.at[b], dst_ref=got.at[b, n], send_sem=p2_send.at[b], recv_sem=p2_recv.at[b],
                device_id=at(-di, -dj), device_id_type=MESH,
            ).start()

    def transform(b):
        others = got.at[b, pl.ds(0, len(REACH))]
        pltpu.make_async_copy(others, others, p2_recv.at[b]).wait()
        stack = got[b].reshape(16 * 8, H)
        place = lax.shift_right_logical(iota((16 * 8, H), 0), 3)
        keep = jnp.ones((16 * 8, H), jnp.float32)
        for n, (di, dj) in enumerate(REACH):
            if di != 0:
                keep = jnp.where((low_edge if di < 0 else high_edge) & (place == n), 0.0, keep)
        stack = stack * keep
        turned = stack.T
        gram = dot(jnp.concatenate([turned[0:M], turned[2 * M : 3 * M]], axis=0), stack)
        both = gram[0:M] + pltpu.roll(gram[M : 2 * M], 2 * M, 1)
        system = jnp.where(lane < 2 * M, both, 0.0) + jnp.where(lane == iota((M, H), 0), M - 1.0, 0.0)
        return eliminate(system)

    def centered_rows(solved):
        w = jnp.where(lane < M, pltpu.roll(solved, H - M, 1), 0.0)
        return w - jnp.sum(w, axis=0, keepdims=True) * (1.0 / M)

    halo_columns(0)
    fix_columns(0)
    seen0 = see(0)
    came(crow_r, CROWS)
    halo_rows = [parts_of(crow_r[side, 0:1, :], crow_r[side, 1:2, :]) for side in range(2)]
    for f in range(F):
        for side, first in ((0, 0), (1, 8 + R)):
            p = halo_rows[side]
            set_coef(f, first, [centre_of(p, rates[f])] + [part + rates[f] for part in p])
    near[0] = near_weights(0)
    corner_part[0] = corner_weights(0)
    came(near_r, NEAR)
    seen0 = seen0 + near_rows(0)
    came(corner_r, CORNER)
    corner_t[...] = jnp.concatenate([corner_r[n] for n in range(4)] + [jnp.zeros((H - 32, H), jnp.float32)], axis=0).T
    tell(0, observe(0, seen0))
    near[1] = near_weights(1)
    corner_part[1] = corner_weights(1)
    inner(1, q, x1, 2, 1)
    inner(1, x1, x2, 1, 0)
    halo_columns(1)
    fix_columns(1)
    r1 = observe(1, see(1) + near_rows(1))
    solved0 = transform(0)
    w0 = jnp.where(lane < M, pltpu.roll(solved0, H - M, 1), 0.0)
    w0_mean = jnp.sum(w0, axis=1, keepdims=True) * (1.0 / M)
    both0 = jnp.where(lane < M, w0 - w0_mean, jnp.where(lane < 2 * M, -solved0, 0.0))
    tell(1, r1 + dot(r1[:, 0:M], both0))
    c0 = centered_rows(solved0)
    late_corners(0)
    late_corners(1)
    unpack_columns(0)
    unpack_columns(1)
    fix_rows(0)
    fix_rows(1)
    sent(near_s, NEAR)
    for f in range(F):
        sent(q.at[f, pl.ds(2, 4)], ROWS + f)
        sent(far.at[f], COLS + f)
    sent(corner_r, CORNER)
    sent(crow_s, CROWS)
    sent(ccol_s, CCOLS)
    solved1 = transform(1)
    c1 = centered_rows(solved1)
    e_out[...] = c0 + c1 + dot(c0[:, 0:M], c1)
    for b in range(BATCHES):
        others = got.at[b, pl.ds(0, len(REACH))]
        pltpu.make_async_copy(others, others, p2_send.at[b]).wait()


def analysis_kernel(e_ref, x, out, y, out_sem):
    groups = [(f, r) for f in range(F) for r in range(0, R, GROUP)]
    e = jnp.concatenate([e_ref[...], jnp.zeros((H - M, H), jnp.float32)], axis=0).T[0:M, 0:M]
    e_hi = e.astype(jnp.bfloat16)
    e_lo = (e - e_hi.astype(jnp.float32)).astype(jnp.bfloat16)
    left = jnp.concatenate([e_hi, e_hi, e_lo], axis=1)
    for f, r in groups:
        for row in range(r, r + GROUP):
            v = x[f, row]
            hi = v.astype(jnp.bfloat16)
            low = (v - hi.astype(jnp.float32)).astype(jnp.bfloat16)
            right = jnp.concatenate([hi, low, hi], axis=0)
            add = lax.dot_general(left, right, (((1,), (0,)), ((), ())), preferred_element_type=jnp.float32)
            y[f, row] = v + add
        for row in range(r, r + GROUP):
            pltpu.make_async_copy(y.at[f, row], out.at[f, :, row, :], out_sem).start()
    pltpu.make_async_copy(y, y, out_sem).wait()


def local(ensemble, courant_x, courant_y, diffusion, obs_cell, obs_value, obs_noise, obs_var, loc_mask):
    any_space = pl.BlockSpec(memory_space=pl.ANY)
    f32 = jnp.float32
    count = obs_cell.shape[1]
    vmem = pltpu.VMEM
    dma = pltpu.SemaphoreType.DMA
    noise_turned = obs_noise.swapaxes(1, 2)
    operands = (
        ensemble.reshape(F, M * R, C), courant_x, courant_y, diffusion, obs_cell, obs_value, noise_turned, obs_var
    )
    forecast, combined = pl.pallas_call(
        forecast_kernel,
        out_shape=(vmem((F, R, M, C), f32), vmem((M, H), f32)),
        in_specs=[pl.BlockSpec(memory_space=pltpu.HBM)] * 8,
        out_specs=(pl.BlockSpec(memory_space=pltpu.VMEM), pl.BlockSpec(memory_space=pltpu.VMEM)),
        scratch_shapes=[
            vmem((2, F, M * R, H), f32),
            vmem((F, R + 4, M, C), f32),
            vmem((F, R + 2, M, C), f32),
            vmem((F, M, H), f32),
            vmem((F, M, H), f32),
            vmem((F, 2, M, H), f32),
            vmem((F, M, H), f32),
            vmem((F, M, H), f32),
            vmem((8, H), f32),
            vmem((4, 8, H), f32),
            vmem((H, H), f32),
            vmem((2, M, H), f32),
            vmem((2, M, H), f32),
            vmem((2, 8, C), f32),
            vmem((2, 8, C), f32),
            vmem((2, 8, H), f32),
            vmem((2, 8, H), f32),
            vmem((F, M, H), f32),
            vmem((F, M, H), f32),
            vmem((F, 5, 2, R + 16, H), f32),
            vmem((2, R, C), f32),
            pltpu.SMEM((F,), f32),
            vmem((BATCHES, count), jnp.int32),
            vmem((BATCHES * count // H, H), jnp.int32),
            vmem((2, BATCHES, count), f32),
            vmem((BATCHES, M, count), f32),
            vmem((BATCHES, M + 8, H), f32),
            vmem((BATCHES, 8, H), jnp.int32),
            pltpu.SMEM((BATCHES, 8, H), jnp.int32),
            vmem((BATCHES, 8, H), f32),
            vmem((BATCHES, 16, 8, H), f32),
            dma((7,)),
            dma((CHANNELS,)),
            dma((CHANNELS,)),
            dma((BATCHES,)),
            dma((BATCHES,)),
        ],
        compiler_params=pltpu.CompilerParams(
            collective_id=0, has_side_effects=True, vmem_limit_bytes=48 * 1024 * 1024
        ),
        name="forecast_and_transform",
    )(*(pltpu.with_memory_space_constraint(a, pltpu.HBM) for a in operands))
    return pl.pallas_call(
        analysis_kernel,
        out_shape=jax.ShapeDtypeStruct((F, M, R, C), f32),
        in_specs=[pl.BlockSpec(memory_space=pltpu.VMEM)] * 2,
        out_specs=any_space,
        scratch_shapes=[
            vmem((F, R, M, C), f32),
            dma,
        ],
        compiler_params=pltpu.CompilerParams(vmem_limit_bytes=48 * 1024 * 1024),
        name="analysis",
    )(*(pltpu.with_memory_space_constraint(a, pltpu.VMEM) for a in (combined, forecast)))


def solution(mesh):
    in_specs = (
        P(None, None, "lat", "lon"),
        P("lat", "lon"),
        P("lat", "lon"),
        P(),
        P(),
        P(),
        P(),
        P(),
        P("lat", "lon", None, None),
    )
    out_specs = P(None, None, "lat", "lon")
    return jax.shard_map(local, mesh=mesh, in_specs=in_specs, out_specs=out_specs, check_vma=False)
```
